128 devices in a mesh: blk: 64 (over x_hi, y, z, core), rep: 2 (over x_lo).
Axes of the slice: x: 4 (x_hi: 2, x_lo: 2; x = x_hi * 2 + x_lo), y: 4, z: 4, core: 2. Of those that a mesh axis runs over, the one named last changes fastest.
Arguments:
- image_feats: bfloat16 [2, 8192, 1536], P('rep', 'blk'), may hold values from -0.29882812 to 0.29882812
- text_feats: bfloat16 [2, 8192, 1152], P('rep', 'blk'), may hold values from -0.29882812 to 0.29882812
- match: int32 [2, 64, 128], P('rep', 'blk'), may hold values from 0 to 127, each once within a row
- w_image: bfloat16 [1536, 1536], replicated, may hold values from -0.15625 to 0.15625
- w_text: bfloat16 [1152, 1536], replicated, may hold values from -0.1875 to 0.1875
- log_temp: float32 [1], replicated, may hold values from 1.8 to 2.6
- bias: float32 [1], replicated, may hold values from -5 to -3
Outputs:
- row_loss: float32 [2, 8192], P('rep', 'blk')
- grad_image: bfloat16 [2, 8192, 1536], P('rep', 'blk')
- grad_text: bfloat16 [2, 8192, 1152], P('rep', 'blk')
- grad_w_image: float32 [1536, 1536], P(('blk', 'rep'))
- grad_w_text: float32 [1152, 1536], P(('blk', 'rep'))
The draws below stay inside these ranges and needn't reach their ends.
Inputs may be any that keep to these rules, and one draw needn't show every extreme that they name: `match`: each row of 128 entries is a permutation of the positions in the device's block.
All inputs are finite; a program needn't handle non-finite values.
Results may differ from the reference program's by a relative error of at most 0.0075.
Values may be sent and summed in bfloat16 or wider, within the bound.
No kernel may reach another device: no remote copies, remote signals or barrier semaphores. Data moves between devices by JAX's collectives and lax.ppermute only.
A program may use at most 192 MiB of HBM per device.

```python
import jax
import jax.numpy as jnp
from jax import lax

DI = 1536
DT = 1152
E = 1536
ROWS_DEV = 128
REPS = 2
BLOCKS = 64
GROUP_ROWS = 8192


def block_scale(key, shape, split, smallest, top_value):
    level, own = 1.0, jax.random.fold_in(key, 6)
    for axis_at, parts in split:
        draws = jnp.exp(jax.random.uniform(jax.random.fold_in(own, axis_at), (parts,), jnp.float32, smallest / len(split), top_value / len(split)))
        level = level * jnp.repeat(draws, shape[axis_at] // parts).reshape([-1 if axis == axis_at else 1 for axis in range(len(shape))])
    return level


def noise(key, extent, scale, limit, pieces=(), dtype=jnp.bfloat16):
    values = scale * jax.random.normal(key, extent, jnp.float32)
    if pieces:
        values = values * block_scale(key, extent, pieces, -0.22, 0.18)
    return jnp.clip(values, -limit, limit).astype(dtype)


def setup_inputs(seed: int = 0) -> dict:
    key_list = jax.random.split(jax.random.key(seed), 8)
    return {
        "image_feats": noise(key_list[0], (REPS, GROUP_ROWS, DI), 0.05, 0.29882812, ((0, 2), (1, 64))),
        "text_feats": noise(key_list[1], (REPS, GROUP_ROWS, DT), 0.05, 0.29882812, ((0, 2), (1, 64))),
        "match": jax.vmap(lambda own: jax.random.permutation(own, ROWS_DEV))(jax.random.split(key_list[2], REPS * BLOCKS)).reshape((REPS, BLOCKS, ROWS_DEV)).astype(jnp.int32),
        "w_image": noise(key_list[3], (DI, E), DI ** -0.5, 0.15625),
        "w_text": noise(key_list[4], (DT, E), DT ** -0.5, 0.1875),
        "log_temp": jnp.clip(jax.random.uniform(key_list[5], (1,), jnp.float32, 1.8, 2.6), 1.8, 2.6),
        "bias": jnp.clip(jax.random.uniform(key_list[6], (1,), jnp.float32, -5.0, -3.0), -5.0, -3.0),
    }


def project(feats, weight):
    proj = jnp.dot(feats, weight, preferred_element_type=jnp.float32)
    length = jnp.sqrt(lax.optimization_barrier(jnp.sum(proj * proj, axis=1, keepdims=True)) + 1e-06)
    return (proj / length, length)

def pair_terms(img_unit, txt_unit, positive, scale, offset):
    logits = scale * jnp.dot(img_unit, txt_unit.T, preferred_element_type=jnp.float32) + offset
    signs = jnp.where(positive, jnp.float32(1.0), jnp.float32(-1.0))
    margin = signs * logits
    loss_part = lax.optimization_barrier(jnp.sum(jax.nn.softplus(-margin), axis=1))
    coeffs = (-signs * jax.nn.sigmoid(-margin)).astype(jnp.bfloat16)
    return (loss_part, coeffs)

def unit_back(unit, length, grad_unit):
    inner = lax.optimization_barrier(jnp.sum(unit * grad_unit, axis=1, keepdims=True))
    return ((grad_unit - unit * inner) / length).astype(jnp.bfloat16)

def reference(image_feats, text_feats, match, w_image, w_text, log_temp, bias):
    scale = jnp.exp(log_temp[0])
    offset = bias[0]
    losses = []
    grads_img = []
    grads_txt = []
    grad_wi = jnp.zeros((DI, E), jnp.float32)
    grad_wt = jnp.zeros((DT, E), jnp.float32)
    columns = jnp.arange(GROUP_ROWS).astype(jnp.int32)
    owner = columns // ROWS_DEV * ROWS_DEV
    for group in range(REPS):
        img_x = image_feats[group]
        txt_x = text_feats[group]
        unit_img, len_img = project(img_x, w_image)
        unit_txt, len_txt = project(txt_x, w_text)
        img_b = unit_img.astype(jnp.bfloat16)
        txt_b = unit_txt.astype(jnp.bfloat16)
        paired = match[group].reshape(-1).astype(jnp.int32)
        positive = columns[None, :] == (owner + paired)[:, None]
        loss_rows, coeffs = pair_terms(img_b, txt_b, positive, scale, offset)
        losses.append(loss_rows / ROWS_DEV)
        grad_unit_img = scale * jnp.dot(coeffs, txt_b, preferred_element_type=jnp.float32)
        grad_unit_txt = scale * jnp.dot(coeffs.T, img_b, preferred_element_type=jnp.float32)
        delta_img = unit_back(unit_img, len_img, grad_unit_img)
        delta_txt = unit_back(unit_txt, len_txt, grad_unit_txt)
        grads_img.append(jnp.dot(delta_img, w_image.T, preferred_element_type=jnp.float32).astype(jnp.bfloat16))
        grads_txt.append(jnp.dot(delta_txt, w_text.T, preferred_element_type=jnp.float32).astype(jnp.bfloat16))
        grad_wi = grad_wi + jnp.dot(img_x.T, delta_img, preferred_element_type=jnp.float32)
        grad_wt = grad_wt + jnp.dot(txt_x.T, delta_txt, preferred_element_type=jnp.float32)
    return (jnp.stack(losses), jnp.stack(grads_img), jnp.stack(grads_txt), grad_wi, grad_wt)
```

```python
import jax
import jax.numpy as jnp
from jax import lax
from jax.sharding import Mesh
from jax.sharding import PartitionSpec as P

AXES = ("xh", "y", "z", "c", "xl")
SIZES = {"xh": 2, "y": 4, "z": 4, "c": 2, "xl": 2}
BF = jnp.bfloat16
F32 = jnp.float32


def rot(value, axis, steps):
    n = SIZES[axis]
    return lax.ppermute(value, axis, [(i, (i + steps) % n) for i in range(n)])


def mm(a, b):
    return jnp.dot(a, b, preferred_element_type=F32)


def mm_t(a, b):
    return lax.dot_general(a, b, (((1,), (1,)), ((), ())), preferred_element_type=F32)


def t_mm(a, b):
    return lax.dot_general(a, b, (((0,), (0,)), ((), ())), preferred_element_type=F32)


def project(feats, weight):
    proj = mm(feats, weight)
    length = jnp.sqrt(jnp.sum(proj * proj, axis=1, keepdims=True) + 1e-06)
    return proj / length, length


def unit_back(unit, length, grad_unit):
    inner = jnp.sum(unit * grad_unit, axis=1, keepdims=True)
    return ((grad_unit - unit * inner) / length).astype(BF)


def ring_gather(value, axis):
    return jnp.concatenate([value] + [rot(value, axis, k) for k in (1, 2, 3)], axis=0)


def ring_reduce(parts, axis):
    total = parts[0]
    for k in (1, 2, 3):
        total = total + rot(parts[k].astype(BF), axis, -k).astype(F32)
    return total


def pair_gather(value, axis):
    full = ring_gather(value, axis)
    return jnp.concatenate([full, rot(full, "c", 1)], axis=0)


def feature_columns(feats, ring, order):
    rows, width = feats.shape
    cut = width // 128
    split = feats.reshape(rows, 2, 4, 4, 2, 2 * cut)
    split = split.transpose(order + (0, 1, 3 if ring == "y" else 2, 5))
    me_r, me_c = lax.axis_index(ring), lax.axis_index("c")
    share = width // 8
    split = split.reshape(4, 2, rows, share)

    def take(pos, core, value):
        return lax.dynamic_slice(value, (pos % 4, core, 0, 0), (1, 1, rows, share))[0, 0]

    blocks = []
    for j in (0, 1):
        for k in range(4):
            piece = take(me_r + k, (me_c + j) % 2, split)
            if k:
                piece = rot(piece, ring, k)
            if j:
                piece = rot(piece, "c", 1)
            blocks.append(piece)
    return jnp.concatenate(blocks, axis=0)


def weight_reduce(partial, ring):
    _, _, rows, width = partial.shape
    me = lax.axis_index(ring)
    total = lax.dynamic_index_in_dim(partial, me, 1, keepdims=False)
    for k in (1, 2, 3):
        piece = lax.dynamic_index_in_dim(partial, (me + k) % 4, 1, keepdims=False)
        total = total + rot(piece.astype(BF), ring, k).astype(F32)
    total = total.reshape(2, 2, rows // 2, width)
    hi, lo = lax.axis_index("xh"), lax.axis_index("xl")
    out = None
    for dh in (0, 1):
        for dl in (0, 1):
            piece = lax.dynamic_slice(
                total, ((hi + dh) % 2, (lo + dl) % 2, 0, 0), (1, 1, rows // 2, width)
            )[0, 0]
            if dh or dl:
                pairs = [
                    (h * 2 + l, ((h + dh) % 2) * 2 + (l + dl) % 2) for h in (0, 1) for l in (0, 1)
                ]
                piece = lax.ppermute(piece.astype(BF), ("xh", "xl"), pairs).astype(F32)
            out = piece if out is None else out + piece
    return out


def per_device(image_feats, text_feats, match, w_image, w_text, log_temp, bias):
    img_x, txt_x = image_feats[0], text_feats[0]
    rows = img_x.shape[0]
    scale, offset = jnp.exp(log_temp[0]), bias[0]
    unit_txt, len_txt = project(txt_x, w_text)
    txt_b = unit_txt.astype(BF)
    unit_img, len_img = project(img_x, w_image)
    img_b = unit_img.astype(BF)

    pair = jnp.concatenate([txt_b, rot(txt_b, "xh", 1)], axis=0)
    images = pair_gather(img_b, "y")
    texts = [pair] + [rot(pair, "z", k) for k in (1, 2, 3)]

    columns = jnp.arange(2 * rows)
    place = jnp.arange(8 * rows)
    own = jnp.where(place < rows, jnp.tile(match[0, 0], 8), -1)
    grad_img = jnp.zeros((8 * rows, img_b.shape[1]), F32)
    losses = jnp.zeros((8 * rows,), F32)
    grad_txt = []
    for k in range(4):
        logits = scale * mm_t(images, texts[k]) + offset
        if k == 0:
            signs = jnp.where(columns[None, :] == own[:, None], F32(1.0), F32(-1.0))
        else:
            signs = F32(-1.0)
        margin = signs * logits
        losses = losses + jnp.sum(jax.nn.softplus(-margin), axis=1)
        coeffs = (-signs * jax.nn.sigmoid(-margin)).astype(BF)
        grad_txt.append(scale * t_mm(coeffs, images))
        grad_img = grad_img + scale * mm(coeffs, texts[k])

    both = ring_reduce(grad_txt, "z")
    grad_unit_txt = both[:rows] + rot(both[rows:].astype(BF), "xh", 1).astype(F32)
    half = 4 * rows
    mine = grad_img[:half] + rot(grad_img[half:].astype(BF), "c", 1).astype(F32)
    grad_unit_img = ring_reduce([mine[k * rows : (k + 1) * rows] for k in range(4)], "y")

    loss_half = losses[:half] + rot(losses[half:], "c", 1)
    row_loss = loss_half[:rows]
    for k in (1, 2, 3):
        row_loss = row_loss + rot(loss_half[k * rows : (k + 1) * rows], "y", -k)
    row_loss = (row_loss / rows)[None]

    delta_img = unit_back(unit_img, len_img, grad_unit_img)
    delta_txt = unit_back(unit_txt, len_txt, grad_unit_txt)
    grad_image = mm_t(delta_img, w_image).astype(BF)[None]
    grad_text = mm_t(delta_txt, w_text).astype(BF)[None]

    img_cols = feature_columns(img_x, "y", (2, 4))
    txt_cols = feature_columns(txt_x, "z", (3, 4))
    deltas_img = pair_gather(delta_img, "y")
    deltas_txt = pair_gather(delta_txt, "z")
    part_img = t_mm(img_cols, deltas_img)
    part_txt = t_mm(txt_cols, deltas_txt)
    width = part_img.shape[1]
    grad_w_image = weight_reduce(part_img.reshape(2, 4, -1, width), "z")
    grad_w_text = weight_reduce(part_txt.reshape(2, 4, -1, width), "y")
    return (row_loss, grad_image, grad_text, grad_w_image, grad_w_text)


def solution(mesh):
    fine = Mesh(mesh.devices.reshape([SIZES[a] for a in AXES]), AXES)
    blk = ("xh", "y", "z", "c")
    in_specs = (
        P("xl", blk, None),
        P("xl", blk, None),
        P("xl", blk, None),
        P(),
        P(),
        P(),
        P(),
    )
    out_specs = (
        P("xl", blk),
        P("xl", blk, None),
        P("xl", blk, None),
        P(AXES, None),
        P(AXES, None),
    )
    return jax.shard_map(
        per_device, mesh=fine, in_specs=in_specs, out_specs=out_specs, check_vma=False
    )
```

```python
import functools

import jax
import jax.numpy as jnp
from jax import lax
from jax.experimental import pallas as pl
from jax.experimental.pallas import tpu as pltpu
from jax.sharding import Mesh
from jax.sharding import PartitionSpec as P

AXES = ("xh", "y", "z", "c", "xl")
SIZES = {"xh": 2, "y": 4, "z": 4, "c": 2, "xl": 2}
BF = jnp.bfloat16
F32 = jnp.float32
VMEM = pl.BlockSpec(memory_space=pltpu.VMEM)
SMEM = pl.BlockSpec(memory_space=pltpu.SMEM)
MIB = 1 << 20


def rot(value, axis, steps):
    n = SIZES[axis]
    return lax.ppermute(value, axis, [(i, (i + steps) % n) for i in range(n)])


def mm(a, b):
    return jnp.dot(a, b, preferred_element_type=F32)


def mm_t(a, b):
    return lax.dot_general(a, b, (((1,), (1,)), ((), ())), preferred_element_type=F32)


def t_mm(a, b):
    return lax.dot_general(a, b, (((0,), (0,)), ((), ())), preferred_element_type=F32)


def unit_back(unit, length, grad_unit):
    inner = jnp.sum(unit * grad_unit, axis=1, keepdims=True)
    return ((grad_unit - unit * inner) / length).astype(BF)


def cost(macs, nbytes):
    return pl.CostEstimate(flops=2 * macs, bytes_accessed=nbytes, transcendentals=0)


def project_kernel(n, kept, *refs):
    blocks, w_ref, unit_ref = refs[:n], refs[n], refs[n + 1]
    rows = blocks[0].shape[0]
    for at in range(0, n, 2):
        pair = blocks[at : at + 2]
        feats = jnp.concatenate([b[...] for b in pair], axis=0) if len(pair) > 1 else pair[0][...]
        proj = mm(feats, w_ref[...])
        length = jnp.sqrt(jnp.sum(proj * proj, axis=1, keepdims=True) + 1e-06)
        unit = proj / length
        unit_ref[at * rows : at * rows + feats.shape[0], :] = unit.astype(BF)
        if at == 0 and kept:
            refs[n + 2][...] = unit[: kept * rows]
            refs[n + 3][...] = length[: kept * rows]


def project(blocks, weight, kept=0):
    n, rows = len(blocks), blocks[0].shape[0]
    depth, width = weight.shape
    out = [jax.ShapeDtypeStruct((n * rows, width), BF)]
    if kept:
        out += [
            jax.ShapeDtypeStruct((kept * rows, width), F32),
            jax.ShapeDtypeStruct((kept * rows, 1), F32),
        ]
    return pl.pallas_call(
        functools.partial(project_kernel, n, kept),
        out_shape=out,
        in_specs=[VMEM] * (n + 1),
        out_specs=[VMEM] * len(out),
        cost_estimate=cost(n * rows * depth * width, 2 * depth * width + 4 * n * rows * width),
        compiler_params=pltpu.CompilerParams(vmem_limit_bytes=32 * MIB),
    )(*blocks, weight)


def pair_kernel(n, first, *refs):
    params, images = refs[0], refs[1]
    units, at = refs[2 : 2 + n], 2 + n
    if first:
        paired = refs[at]
        at += 1
    coefs, grads, loss_ref = refs[at : at + n], refs[at + n : at + 2 * n], refs[at + 2 * n]
    scale, offset = params[0], params[1]
    total = images.shape[0]
    step = total // 4
    for k in range(n):
        for j in range(4):
            cols = slice(j * step, (j + 1) * step)
            margin = scale * mm_t(units[k][...], images[cols, :]) + offset
            if first and k == 0:
                place = lax.broadcasted_iota(jnp.int32, margin.shape, 0)
                positive = place == paired[:, cols]
                margin = jnp.where(positive, -margin, margin)
            small = jnp.exp(-jnp.abs(margin))
            whole = 1.0 + small
            terms = jnp.maximum(margin, 0.0) + jnp.log1p(small)
            coeff = jnp.where(margin >= 0.0, 1.0, small) / whole
            if first and k == 0:
                coeff = jnp.where(positive, -coeff, coeff)
            part = jnp.sum(terms, axis=0, keepdims=True)
            loss_ref[:, cols] = part if k == 0 else loss_ref[:, cols] + part
            coefs[k][:, cols] = coeff.astype(BF)
        grads[k][...] = (scale * mm(coefs[k][...], images[...])).astype(grads[k].dtype)


def pair_terms(params, images, units, paired=None):
    n, (rows, width), total = len(units), units[0].shape, images.shape[0]
    first = paired is not None
    out = [jax.ShapeDtypeStruct((rows, total), BF)] * n
    out += [
        jax.ShapeDtypeStruct((rows, width), F32 if first and k == 0 else BF) for k in range(n)
    ]
    out += [jax.ShapeDtypeStruct((1, total), F32)]
    args = [params, images] + list(units) + ([paired] if first else [])
    res = pl.pallas_call(
        functools.partial(pair_kernel, n, first),
        out_shape=out,
        in_specs=[SMEM] + [VMEM] * (len(args) - 1),
        out_specs=[VMEM] * len(out),
        cost_estimate=cost(2 * n * rows * total * width, 2 * width * (total + 2 * n * rows)),
        compiler_params=pltpu.CompilerParams(vmem_limit_bytes=40 * MIB),
    )(*args)
    return res[:n], res[n : 2 * n], res[2 * n]


def image_kernel(n, *refs):
    params, coefs, units = refs[0], refs[1 : 1 + n], refs[1 + n : 1 + 2 * n]
    other_ref, own_ref = refs[1 + 2 * n :]
    total = t_mm(coefs[0][...], units[0][...])
    for k in range(1, n):
        total = total + t_mm(coefs[k][...], units[k][...])
    total = params[0] * total
    j = pl.program_id(0)

    @pl.when(j < 2)
    def _():
        other_ref[...] = total.astype(BF)

    @pl.when(j >= 2)
    def _():
        own_ref[...] = total


def image_grad(params, coefs, units):
    n, (rows, total), width = len(coefs), coefs[0].shape, units[0].shape[1]
    tile = total // 4
    return pl.pallas_call(
        functools.partial(image_kernel, n),
        grid=(4,),
        out_shape=[
            jax.ShapeDtypeStruct((total // 2, width), BF),
            jax.ShapeDtypeStruct((total // 2, width), F32),
        ],
        in_specs=[SMEM]
        + [pl.BlockSpec((rows, tile), lambda j: (0, (j + 2) % 4))] * n
        + [pl.BlockSpec((rows, width), lambda j: (0, 0))] * n,
        out_specs=[
            pl.BlockSpec((tile, width), lambda j: (jnp.minimum(j, 1), 0)),
            pl.BlockSpec((tile, width), lambda j: (jnp.maximum(j - 2, 0), 0)),
        ],
        cost_estimate=cost(n * rows * total * width, 2 * n * rows * (total + width) + 3 * total * width),
        compiler_params=pltpu.CompilerParams(vmem_limit_bytes=40 * MIB),
    )(params, *coefs, *units)


def direct(value, axis):
    return [value] + [rot(value, axis, k) for k in (1, 2, 3)]


def collect(own, parts, axis):
    total = own
    for k in (1, 3, 2):
        total = total + rot(parts[k - 1].astype(BF), axis, -k).astype(F32)
    return total


def scatter(value, axis):
    cut = value.shape[0] // 4
    total = value[:cut]
    for k in (1, 3, 2):
        total = total + rot(value[k * cut : (k + 1) * cut].astype(BF), axis, k).astype(F32)
    return total


def core_scatter(value):
    half = value.shape[0] // 2
    return value[:half] + rot(value[half:].astype(BF), "c", 1).astype(F32)


def selection(depth, cut, steps):
    dims = [SIZES[a] if a in steps else 1 for a in ("c", "z", "y", "xh", "xl")] + [cut]
    parts = {
        a: (lax.broadcasted_iota(jnp.int32, dims, i) + lax.axis_index(a)) % SIZES[a]
        for i, a in enumerate(("c", "z", "y", "xh", "xl"))
    }
    place = parts["xh"]
    for a in ("y", "z", "c", "xl"):
        place = place * SIZES[a] + parts[a]
    place = (place * cut + lax.broadcasted_iota(jnp.int32, dims, 5)).reshape(1, -1)
    return (jnp.arange(depth)[:, None] == place).astype(BF)


def per_device(image_feats, text_feats, match, w_image, w_text, log_temp, bias):
    img_x, txt_x = image_feats[0], text_feats[0]
    rows, width = img_x.shape[0], w_image.shape[1]
    scale = jnp.exp(log_temp[0])
    params = jnp.stack([scale, bias[0]])

    img_blocks = direct(img_x, "y")
    partner = rot(txt_x, "xh", 1)
    txt_blocks = direct(txt_x, "z")
    partners = direct(partner, "z")

    mine, unit_img, len_img = project(img_blocks, w_image, kept=1)
    images = jnp.concatenate([mine, rot(mine, "c", 1)], axis=0)
    unit_0, unit_txt, len_txt = project([txt_x, partner], w_text, kept=2)
    units = [unit_0] + [project([txt_blocks[k], partners[k]], w_text)[0] for k in (1, 2, 3)]

    place = jnp.arange(8 * rows)
    paired = jnp.where(place < rows, jnp.tile(match[0, 0], 8), -1)[None]
    coefs, grads, loss_a = pair_terms(params, images, [units[0], units[1], units[3]], paired)
    coefs_b, grads_b, loss_b = pair_terms(params, images, [units[2]])
    other, own = image_grad(params, [*coefs, *coefs_b], [units[0], units[1], units[3], units[2]])
    grad_txt = [grads[1], grads_b[0], grads[2]]

    img_half = own + rot(other, "c", 1).astype(F32)
    img_parts = [img_half[k * rows : (k + 1) * rows] for k in range(4)]
    pair_grad = collect(grads[0], grad_txt, "z")
    grad_unit_img = collect(img_parts[0], img_parts[1:], "y")
    grad_unit_txt = pair_grad[:rows] + rot(pair_grad[rows:].astype(BF), "xh", 1).astype(F32)

    losses = (loss_a + loss_b).reshape(8, rows)
    loss_half = losses[:4] + rot(losses[4:], "c", 1)
    row_loss = loss_half[0]
    for k in (1, 3, 2):
        row_loss = row_loss + rot(loss_half[k], "y", -k)
    row_loss = (row_loss / rows)[None]

    delta_img = unit_back(unit_img, len_img, grad_unit_img)
    grad_image = mm_t(delta_img, w_image).astype(BF)[None]
    delta_txt = unit_back(unit_txt[:rows], len_txt[:rows], grad_unit_txt)
    grad_text = mm_t(delta_txt, w_text).astype(BF)[None]

    cut = txt_x.shape[1] // 128
    pick = selection(txt_x.shape[1], cut, ("c", "z", "y", "xh", "xl"))
    feats = mm(jnp.concatenate([txt_x, partner], axis=0), pick).astype(BF)
    pair_delta = unit_back(unit_txt, len_txt, pair_grad)
    sum_txt = core_scatter(t_mm(feats, pair_delta))
    sum_txt = scatter(scatter(sum_txt, "z"), "y")

    cut_img = img_x.shape[1] // 128
    pick = selection(img_x.shape[1], cut_img, ("c", "z", "xh", "xl"))
    feats = mm(jnp.concatenate(img_blocks, axis=0), pick).astype(BF)
    sum_img = core_scatter(t_mm(feats, jnp.concatenate(direct(delta_img, "y"), axis=0)))
    sum_img = scatter(sum_img, "z")

    both = jnp.concatenate(
        [sum_img.reshape(2, 2, cut_img, width), sum_txt.reshape(2, 2, cut, width)], axis=2
    )
    total = both[0, 0]
    for dh, dl in ((0, 1), (1, 0), (1, 1)):
        pairs = [(h * 2 + l, ((h + dh) % 2) * 2 + (l + dl) % 2) for h in (0, 1) for l in (0, 1)]
        moved = lax.ppermute(both[dh, dl].astype(BF), ("xh", "xl"), pairs)
        total = total + moved.astype(F32)
    return (row_loss, grad_image, grad_text, total[:cut_img], total[cut_img:])


def solution(mesh):
    fine = Mesh(mesh.devices.reshape([SIZES[a] for a in AXES]), AXES)
    blk = ("xh", "y", "z", "c")
    in_specs = (
        P("xl", blk, None),
        P("xl", blk, None),
        P("xl", blk, None),
        P(),
        P(),
        P(),
        P(),
    )
    out_specs = (
        P("xl", blk),
        P("xl", blk, None),
        P("xl", blk, None),
        P(AXES, None),
        P(AXES, None),
    )
    return jax.shard_map(
        per_device, mesh=fine, in_specs=in_specs, out_specs=out_specs, check_vma=False
    )
```

```python
import functools

import jax
import jax.numpy as jnp
import numpy as np
from jax import lax
from jax.experimental import pallas as pl
from jax.experimental.pallas import tpu as pltpu
from jax.sharding import Mesh
from jax.sharding import PartitionSpec as P

AXES = ("xh", "y", "z", "c", "xl")
SIZES = {"xh": 2, "y": 4, "z": 4, "c": 2, "xl": 2}
BF = jnp.bfloat16
F32 = jnp.float32
VMEM = pl.BlockSpec(memory_space=pltpu.VMEM)
SMEM = pl.BlockSpec(memory_space=pltpu.SMEM)
MIB = 1 << 20


def rot(value, axis, steps):
    n = SIZES[axis]
    return lax.ppermute(value, axis, [(i, (i + steps) % n) for i in range(n)])


def mm(a, b):
    return jnp.dot(a, b, preferred_element_type=F32)


def mm_t(a, b):
    return lax.dot_general(a, b, (((1,), (1,)), ((), ())), preferred_element_type=F32)


def t_mm(a, b):
    return lax.dot_general(a, b, (((0,), (0,)), ((), ())), preferred_element_type=F32)


def call(kernel, out, args, smem=0, flops=1024):
    return pl.pallas_call(
        kernel,
        out_shape=[jax.ShapeDtypeStruct(shape, dtype) for shape, dtype in out],
        in_specs=[SMEM] * smem + [VMEM] * (len(args) - smem),
        out_specs=[VMEM] * len(out),
        cost_estimate=pl.CostEstimate(flops=flops, bytes_accessed=1024, transcendentals=0),
        compiler_params=pltpu.CompilerParams(vmem_limit_bytes=40 * MIB),
    )(*args)


def project_kernel(n, step, kept, *refs):
    blocks, w_ref, unit_ref = refs[:n], refs[n], refs[n + 1]
    feats = jnp.concatenate([b[...] for b in blocks], axis=0)
    for at in range(0, feats.shape[0], step):
        proj = mm(feats[at : at + step], w_ref[...])
        length = jnp.sqrt(jnp.sum(proj * proj, axis=1, keepdims=True) + 1e-06)
        unit = proj / length
        unit_ref[at : at + step, :] = unit.astype(BF)
        if at == 0 and kept:
            refs[n + 2][...] = unit[:kept]
            refs[n + 3][...] = length[:kept]


def project(blocks, weight, step, kept=0):
    n, rows, width = len(blocks), sum(b.shape[0] for b in blocks), weight.shape[1]
    out = [((rows, width), BF)]
    if kept:
        out += [((kept, width), F32), ((kept, 1), F32)]
    return call(functools.partial(project_kernel, n, step, kept), out, [*blocks, weight])


def stack_kernel(*refs):
    rows = refs[0].shape[0]
    for k, ref in enumerate(refs[:-1]):
        refs[-1][k * rows : (k + 1) * rows, :] = ref[...]


def pair_kernel(n, first, split, *refs):
    params, images = refs[0], refs[1]
    units, at = refs[2 : 2 + n], 2 + n
    if first:
        paired = refs[at]
        at += 1
    coefs, loss_ref, grads = refs[at : at + n], refs[at + n], refs[at + n + 1 :]
    scale, offset = params[0], params[1]
    step = images.shape[0] // 4
    for k in range(n):
        own = first and k == n - 1
        for j in range(4):
            cols = slice(j * step, (j + 1) * step)
            margin = scale * mm_t(units[k][...], images[cols, :]) + offset
            if own:
                place = lax.broadcasted_iota(jnp.int32, margin.shape, 0)
                positive = place == paired[:, cols]
                margin = jnp.where(positive, -margin, margin)
            power = jnp.exp(margin)
            whole = 1.0 + power
            near = power * (1.0 - power * (0.5 - power * (1.0 / 3.0)))
            terms = jnp.where(power < 0.01, near, jnp.log(whole))
            turn = pl.reciprocal(whole, approx=True)
            coeff = power * (turn * (2.0 - whole * turn))
            if own:
                coeff = jnp.where(positive, -coeff, coeff)
            part = jnp.sum(terms, axis=0, keepdims=True)
            loss_ref[:, cols] = part if k == 0 else loss_ref[:, cols] + part
            coefs[k][:, cols] = coeff.astype(BF)
    if split:
        grad = scale * mm(coefs[0][...], images[...])
        cut = grad.shape[0] // 2
        grads[0][...] = grad[:cut].astype(BF)
        grads[1][...] = grad[cut:].astype(BF)


def pair_terms(params, images, units, paired=None, split=False):
    n, (rows, width), total = len(units), units[0].shape, images.shape[0]
    first = paired is not None
    grads = [((rows // 2, width), BF)] * 2 if split else []
    out = [((rows, total), BF)] * n + [((1, total), F32)] + grads
    args = [params, images, *units] + ([paired] if first else [])
    res = call(functools.partial(pair_kernel, n, first, split), out, args, smem=1)
    return res[:n], res[n], res[n + 1 :]


def text_grad_kernel(n, *refs):
    params, images, coefs, grads = refs[0], refs[1], refs[2 : 2 + n], refs[2 + n :]
    for coef, grad in zip(coefs, grads):
        grad[...] = params[0] * mm(coef[...], images[...])


def text_grads(params, images, coefs):
    n, out = len(coefs), ((coefs[0].shape[0], images.shape[1]), F32)
    return call(functools.partial(text_grad_kernel, n), [out] * n, [params, images, *coefs], smem=1)


def join_kernel(before, after, up, down, before_out, after_out):
    cut = up.shape[0]
    before_out[:cut] = before[:cut].astype(BF)
    before_out[cut:] = (before[cut:] + down[...].astype(F32)).astype(BF)
    after_out[:cut] = (after[:cut] + up[...].astype(F32)).astype(BF)
    after_out[cut:] = after[cut:].astype(BF)


def loss_rows(losses, at, rows):
    return jnp.concatenate([losses[:, at + k * rows : at + (k + 1) * rows] for k in range(4)], axis=0)


def two_parts(value, width):
    high = value.astype(BF)
    low = (value - high.astype(F32)).astype(BF)
    parts = jnp.concatenate([high, low], axis=0).astype(F32)
    down = jnp.zeros((16 - parts.shape[0], parts.shape[1]), F32)
    parts = jnp.concatenate([parts, down], axis=0)
    right = jnp.zeros((16, width - parts.shape[1]), F32)
    return jnp.concatenate([parts, right], axis=1).astype(BF)


def image_kernel(n, half, *refs):
    params, coefs, units = refs[0], refs[1 : 1 + n], refs[1 + n : 1 + 2 * n]
    *losses, out_ref = refs[1 + 2 * n :]
    total, width = coefs[0].shape[1], units[0].shape[1]
    tile = total // 4
    for j in range(2):
        cols = slice((2 * half + j) * tile, (2 * half + j + 1) * tile)
        grad = t_mm(coefs[0][:, cols], units[0][...])
        for k in range(1, n):
            grad = grad + t_mm(coefs[k][:, cols], units[k][...])
        out_ref[j * tile : (j + 1) * tile, :] = (params[0] * grad).astype(out_ref.dtype)
    if losses:
        rows = total // 8
        tail = loss_rows(losses[0][...] + losses[1][...], total // 2, rows)
        out_ref[2 * tile :, :] = two_parts(tail, width)


def image_grad(params, coefs, units, half, dtype, losses=()):
    n, total, width = len(coefs), coefs[0].shape[1], units[0].shape[1]
    out = [((total // 2 + (16 if losses else 0), width), dtype)]
    args = [params, *coefs, *units, *losses]
    flops = 1024 if losses else 400 * 10**9
    return call(functools.partial(image_kernel, n, half), out, args, smem=1, flops=flops)[0]


def quarter_kernel(own, moved, keep, *go):
    cut = keep.shape[0]
    keep[...] = own[:cut] + moved[:cut].astype(F32)
    for k, ref in enumerate(go):
        at = slice((k + 1) * cut, (k + 2) * cut)
        ref[...] = (own[at] + moved[at].astype(F32)).astype(BF)


def quarters(own, moved):
    cut, width = own.shape[0] // 4, own.shape[1]
    return call(quarter_kernel, [((cut, width), F32)] + [((cut, width), BF)] * 3, [own, moved])


def image_quarter_kernel(own, moved, loss_a, loss_b, keep, loss_out, *go):
    rows, width = keep.shape
    total = own.shape[0]
    keep[...] = own[:rows] + moved[:rows].astype(F32)
    losses = loss_rows(loss_a[...] + loss_b[...], 0, rows)
    tail = moved[total:, :rows].astype(F32)
    losses = losses + tail[0:4] + tail[4:8]
    loss_out[...] = losses[0:1]
    for k, ref in enumerate(go):
        at = slice((k + 1) * rows, (k + 2) * rows)
        ref[:rows] = (own[at] + moved[at].astype(F32)).astype(BF)
        ref[rows:] = two_parts(losses[k + 1 : k + 2], width)


def back(unit, length, grad):
    inner = jnp.sum(unit * grad, axis=1, keepdims=True)
    return ((grad - unit * inner) / length).astype(BF)


def image_delta_kernel(own, loss, a, b, c, unit, length, out, loss_out):
    rows = own.shape[0]
    grad, total = own[...], loss[...]
    for ref in (a, b, c):
        grad = grad + ref[:rows].astype(F32)
        tail = ref[rows:, :rows].astype(F32)
        total = total + tail[0:1] + tail[1:2]
    out[...] = back(unit[...], length[...], grad)
    loss_out[...] = total / rows


def text_kernel(own, a, b, unit, length, feats, keep, go, part_keep, part_go):
    grad = own[...] + a[...].astype(F32) + b[...].astype(F32)
    rows, half = keep.shape[0], part_keep.shape[0]
    keep[...] = grad[:rows]
    go[...] = grad[rows:].astype(BF)
    delta = back(unit[...], length[...], grad)
    part_go[...] = t_mm(feats[:, half:], delta).astype(BF)
    part_keep[...] = t_mm(feats[:, :half], delta)


def weight_kernel(feats, a, b, c, d, part_keep, part_go):
    half = part_keep.shape[0]
    delta = jnp.concatenate([a[...], b[...], c[...], d[...]], axis=0)
    part_go[...] = t_mm(feats[:, half:], delta).astype(BF)
    part_keep[...] = t_mm(feats[:, :half], delta)


def select_kernel(n, *refs):
    feats = jnp.concatenate([r[...] for r in refs[:n]], axis=0)
    refs[n + 1][...] = mm(feats, refs[n][...]).astype(BF)


def select(blocks, pick):
    n, rows = len(blocks), blocks[0].shape[0]
    out = [((n * rows, pick.shape[1]), BF)]
    return call(functools.partial(select_kernel, n), out, [*blocks, pick])[0]


def tail_kernel(img, i1, i2, i3, txt, t1, t2, t3, keep, *go):
    total_i, total_t = img[...], txt[...]
    for ref in (i1, i2, i3):
        total_i = total_i + ref[...].astype(F32)
    for ref in (t1, t2, t3):
        total_t = total_t + ref[...].astype(F32)
    cut_i, cut_t, width = total_i.shape[0] // 4, total_t.shape[0] // 4, total_i.shape[1]
    for k, ref in enumerate((keep, *go)):
        parts = [
            total_i[k * cut_i : (k + 1) * cut_i],
            jnp.zeros((16 - cut_i, width), F32),
            total_t[k * cut_t : (k + 1) * cut_t],
            jnp.zeros((16 - cut_t, width), F32),
        ]
        ref[...] = jnp.concatenate(parts, axis=0).astype(ref.dtype)


def last_kernel(keep, a, b, c, out_i, out_t):
    total = keep[...] + a[...].astype(F32) + b[...].astype(F32) + c[...].astype(F32)
    out_i[...] = total[: out_i.shape[0]]
    out_t[...] = total[16 : 16 + out_t.shape[0]]


def direct(value, axis):
    return [rot(value, axis, k) for k in (1, 2, 3)]


def scatter(keep, go, axis):
    for k in (1, 3, 2):
        keep = keep + rot(go[k - 1], axis, k).astype(F32)
    return keep


def selection(depth, cut, steps):
    names = ("c", "z", "y", "xh", "xl")
    dims = [SIZES[a] if a in steps else 1 for a in names] + [cut]
    away = dict(zip(names + ("row",), (i.reshape(1, -1).astype(np.int32) for i in np.indices(dims))))
    place = 0
    for a in ("xh", "y", "z", "c", "xl"):
        place = place * SIZES[a] + ((lax.axis_index(a) + away[a]) & (SIZES[a] - 1))
    return (jnp.arange(depth)[:, None] == place * cut + away["row"]).astype(BF)


def per_device(image_feats, text_feats, match, w_image, w_text, log_temp, bias):
    img_x, txt_x = image_feats[0], text_feats[0]
    rows, width = img_x.shape[0], w_image.shape[1]
    scale = jnp.exp(log_temp[0])
    params = jnp.stack([scale, bias[0]])

    place = jnp.arange(8 * rows)
    paired = jnp.where(place < rows, jnp.tile(match[0, 0], 8), -1)[None]
    cut, cut_img = txt_x.shape[1] // 128, img_x.shape[1] // 128
    txt_pick = selection(txt_x.shape[1], cut, ("c", "z", "y", "xh", "xl"))
    img_pick = selection(img_x.shape[1], cut_img, ("c", "z", "xh", "xl"))

    pair_rows = 2 * rows
    img_near = direct(img_x, "y")
    (pair,) = call(stack_kernel, [((pair_rows, txt_x.shape[1]), BF)], [txt_x, rot(txt_x, "xh", 1)])
    before, after = rot(pair, "z", 1), rot(pair, "z", -1)
    far = [rot(before[:rows], "z", 1), rot(after[rows:], "z", -1)]
    *img_near, before, after, paired, txt_pick, img_pick = lax.optimization_barrier(
        (*img_near, before, after, paired, txt_pick, img_pick)
    )
    (img_mine,) = call(stack_kernel, [((4 * rows, img_x.shape[1]), BF)], [img_x, *img_near])
    img_moved = rot(img_mine, "c", 1)

    unit_0, unit_txt, len_txt = project([pair], w_text, pair_rows, kept=pair_rows)
    txt_feats, img_feats = select([pair], txt_pick), select([img_mine], img_pick)
    units = [project([before], w_text, pair_rows)[0], None, project([after], w_text, pair_rows)[0]]
    images, unit_img, len_img = project([img_mine, img_moved], w_image, pair_rows, kept=rows)
    *far, images, unit_0, units[0], units[2], txt_feats, img_feats = lax.optimization_barrier(
        (*far, images, unit_0, units[0], units[2], txt_feats, img_feats)
    )
    units[1] = project(far, w_text, pair_rows)[0]

    coefs_b, loss_b, far = pair_terms(params, images, [units[1]], split=True)
    far = [rot(far[0], "z", 1), rot(far[1], "z", -1)]
    coefs_a, loss_a, _ = pair_terms(params, images, [units[0], units[2], unit_0], paired)
    losses = [loss_a, loss_b]
    coefs, sets = [*coefs_a, *coefs_b], [units[0], units[2], unit_0, units[1]]
    other = image_grad(params, coefs, sets, 1, BF, losses)
    *grads, own_txt = text_grads(params, images, coefs_a)

    before, after = call(join_kernel, [((pair_rows, width), BF)] * 2, [*grads, *far])
    txt_parts = [rot(before, "z", -1), rot(after, "z", 1)]
    *coefs, _ = lax.optimization_barrier((*coefs, before))
    own = image_grad(params, coefs, sets, 0, F32)
    keep, loss, *go = call(
        image_quarter_kernel,
        [((rows, width), F32), ((1, rows), F32)] + [((rows + 16, width), BF)] * 3,
        [own, rot(other, "c", 1), *losses],
    )
    img_parts = [rot(go[k - 1], "y", -k) for k in (1, 3, 2)]
    delta_img, row_loss = call(
        image_delta_kernel,
        [((rows, width), BF), ((1, rows), F32)],
        [keep, loss, *img_parts, unit_img, len_img],
    )
    *txt_parts, _ = lax.optimization_barrier((*txt_parts, delta_img))

    half = txt_x.shape[1] // 2
    own_grad, go_x, part_keep, part_go = call(
        text_kernel,
        [((rows, width), F32), ((rows, width), BF), ((half, width), F32), ((half, width), BF)],
        [own_txt, *txt_parts, unit_txt, len_txt, txt_feats],
    )
    near = direct(delta_img, "y")
    keep, *txt_go = quarters(part_keep, rot(part_go, "c", 1))
    *near, keep = lax.optimization_barrier((*near, keep))
    sum_txt = scatter(keep, txt_go, "z")
    grad_unit_txt = own_grad + rot(go_x, "xh", 1).astype(F32)
    cut_y = sum_txt.shape[0] // 4
    go = [sum_txt[k * cut_y : (k + 1) * cut_y].astype(BF) for k in (1, 2, 3)]
    txt_go = [rot(go[k - 1], "y", k) for k in (1, 3, 2)]

    half = img_feats.shape[1] // 2
    part_keep, part_go = call(
        weight_kernel,
        [((half, width), F32), ((half, width), BF)],
        [img_feats, delta_img, *near],
    )
    keep, *go = quarters(part_keep, rot(part_go, "c", 1))
    img_go = [rot(go[k - 1], "z", k) for k in (1, 3, 2)]
    keep, *go = call(
        tail_kernel,
        [((32, width), F32)] + [((32, width), BF)] * 3,
        [keep, *img_go, sum_txt[:cut_y], *txt_go],
    )
    moved = []
    for dh, dl in ((0, 1), (1, 0), (1, 1)):
        pairs = [(h * 2 + l, ((h + dh) % 2) * 2 + (l + dl) % 2) for h in (0, 1) for l in (0, 1)]
        moved.append(lax.ppermute(go[2 * dh + dl - 1], ("xh", "xl"), pairs))
    grad_w_image, grad_w_text = call(
        last_kernel, [((cut_img, width), F32), ((cut, width), F32)], [keep, *moved]
    )

    grad_image = mm_t(delta_img, w_image).astype(BF)[None]
    delta_txt = back(unit_txt[:rows], len_txt[:rows], grad_unit_txt)
    grad_text = mm_t(delta_txt, w_text).astype(BF)[None]
    return (row_loss, grad_image, grad_text, grad_w_image, grad_w_text)


def solution(mesh):
    fine = Mesh(mesh.devices.reshape([SIZES[a] for a in AXES]), AXES)
    blk = ("xh", "y", "z", "c")
    in_specs = (
        P("xl", blk, None),
        P("xl", blk, None),
        P("xl", blk, None),
        P(),
        P(),
        P(),
        P(),
    )
    out_specs = (
        P("xl", blk),
        P("xl", blk, None),
        P("xl", blk, None),
        P(AXES, None),
        P(AXES, None),
    )
    return jax.shard_map(
        per_device, mesh=fine, in_specs=in_specs, out_specs=out_specs, check_vma=False
    )
```

```python
import functools

import jax
import jax.numpy as jnp
import numpy as np
from jax import lax
from jax.experimental import pallas as pl
from jax.experimental.pallas import tpu as pltpu
from jax.sharding import Mesh
from jax.sharding import PartitionSpec as P

AXES = ("xh", "y", "z", "c", "xl")
SIZES = {"xh": 2, "y": 4, "z": 4, "c": 2, "xl": 2}
BF = jnp.bfloat16
F32 = jnp.float32
VMEM = pl.BlockSpec(memory_space=pltpu.VMEM)
SMEM = pl.BlockSpec(memory_space=pltpu.SMEM)
MIB = 1 << 20


def rot(value, axis, steps):
    n = SIZES[axis]
    return lax.ppermute(value, axis, [(i, (i + steps) % n) for i in range(n)])


def mm(a, b):
    return jnp.dot(a, b, preferred_element_type=F32)


def mm_t(a, b):
    return lax.dot_general(a, b, (((1,), (1,)), ((), ())), preferred_element_type=F32)


def t_mm(a, b):
    return lax.dot_general(a, b, (((0,), (0,)), ((), ())), preferred_element_type=F32)


def call(kernel, out, args, smem=0, flops=1024):
    return pl.pallas_call(
        kernel,
        out_shape=[jax.ShapeDtypeStruct(shape, dtype) for shape, dtype in out],
        in_specs=[SMEM] * smem + [VMEM] * (len(args) - smem),
        out_specs=[VMEM] * len(out),
        cost_estimate=pl.CostEstimate(flops=flops, bytes_accessed=1024, transcendentals=0),
        compiler_params=pltpu.CompilerParams(vmem_limit_bytes=24 * MIB),
    )(*args)


def project_kernel(n, step, kept, *refs):
    blocks, w_ref, unit_ref = refs[:n], refs[n], refs[n + 1]
    feats = jnp.concatenate([b[...] for b in blocks], axis=0)
    for at in range(0, feats.shape[0], step):
        proj = mm(feats[at : at + step], w_ref[...])
        length = jnp.sqrt(jnp.sum(proj * proj, axis=1, keepdims=True) + 1e-06)
        unit = proj / length
        unit_ref[at : at + step, :] = unit.astype(BF)
        if at == 0 and kept:
            refs[n + 2][...] = unit[:kept]
            refs[n + 3][...] = length[:kept]


def project(blocks, weight, step, kept=0):
    n, rows, width = len(blocks), sum(b.shape[0] for b in blocks), weight.shape[1]
    out = [((rows, width), BF)]
    if kept:
        out += [((kept, width), F32), ((kept, 1), F32)]
    return call(functools.partial(project_kernel, n, step, kept), out, [*blocks, weight])


def stack_kernel(*refs):
    rows = refs[0].shape[0]
    for k, ref in enumerate(refs[:-1]):
        refs[-1][k * rows : (k + 1) * rows, :] = ref[...]


def pair_kernel(n, first, split, *refs):
    params, images = refs[0], refs[1]
    units, at = refs[2 : 2 + n], 2 + n
    if first:
        paired = refs[at]
        at += 1
    coefs, loss_ref, grads = refs[at : at + n], refs[at + n], refs[at + n + 1 :]
    scale, offset = params[0], params[1]
    step = images.shape[0] // 4
    for k in range(n):
        own = first and k == n - 1
        for j in range(4):
            cols = slice(j * step, (j + 1) * step)
            margin = scale * mm_t(units[k][...], images[cols, :]) + offset
            if own:
                place = lax.broadcasted_iota(jnp.int32, margin.shape, 0)
                positive = place == paired[:, cols]
                margin = jnp.where(positive, -margin, margin)
            power = jnp.exp(margin)
            whole = 1.0 + power
            near = power * (1.0 - power * (0.5 - power * (1.0 / 3.0)))
            terms = jnp.where(power < 0.01, near, jnp.log(whole))
            turn = pl.reciprocal(whole, approx=True)
            coeff = power * (turn * (2.0 - whole * turn))
            if own:
                coeff = jnp.where(positive, -coeff, coeff)
            part = jnp.sum(terms, axis=0, keepdims=True)
            loss_ref[:, cols] = part if k == 0 else loss_ref[:, cols] + part
            coefs[k][:, cols] = coeff.astype(BF)
    if split:
        grad = scale * mm(coefs[0][...], images[...])
        cut = grad.shape[0] // 2
        grads[0][...] = grad[:cut].astype(BF)
        grads[1][...] = grad[cut:].astype(BF)


def pair_terms(params, images, units, paired=None, split=False):
    n, (rows, width), total = len(units), units[0].shape, images.shape[0]
    first = paired is not None
    grads = [((rows // 2, width), BF)] * 2 if split else []
    out = [((rows, total), BF)] * n + [((1, total), F32)] + grads
    args = [params, images, *units] + ([paired] if first else [])
    res = call(functools.partial(pair_kernel, n, first, split), out, args, smem=1)
    return res[:n], res[n], res[n + 1 :]


def text_grad_kernel(n, *refs):
    params, images, coefs, grads = refs[0], refs[1], refs[2 : 2 + n], refs[2 + n :]
    for coef, grad in zip(coefs, grads):
        grad[...] = params[0] * mm(coef[...], images[...])


def text_grads(params, images, coefs):
    n, out = len(coefs), ((coefs[0].shape[0], images.shape[1]), F32)
    return call(functools.partial(text_grad_kernel, n), [out] * n, [params, images, *coefs], smem=1)


def join_kernel(before, after, up, down, before_out, after_out):
    cut = up.shape[0]
    before_out[:cut] = before[:cut].astype(BF)
    before_out[cut:] = (before[cut:] + down[...].astype(F32)).astype(BF)
    after_out[:cut] = (after[:cut] + up[...].astype(F32)).astype(BF)
    after_out[cut:] = after[cut:].astype(BF)


def loss_rows(losses, at, rows):
    return jnp.concatenate([losses[:, at + k * rows : at + (k + 1) * rows] for k in range(4)], axis=0)


def two_parts(value, width):
    high = value.astype(BF)
    low = (value - high.astype(F32)).astype(BF)
    parts = jnp.concatenate([high, low], axis=0).astype(F32)
    down = jnp.zeros((16 - parts.shape[0], parts.shape[1]), F32)
    parts = jnp.concatenate([parts, down], axis=0)
    right = jnp.zeros((16, width - parts.shape[1]), F32)
    return jnp.concatenate([parts, right], axis=1).astype(BF)


def image_kernel(n, half, *refs):
    params, coefs, units = refs[0], refs[1 : 1 + n], refs[1 + n : 1 + 2 * n]
    *losses, out_ref = refs[1 + 2 * n :]
    total, width = coefs[0].shape[1], units[0].shape[1]
    tile = total // 4
    for j in range(2):
        cols = slice((2 * half + j) * tile, (2 * half + j + 1) * tile)
        grad = t_mm(coefs[0][:, cols], units[0][...])
        for k in range(1, n):
            grad = grad + t_mm(coefs[k][:, cols], units[k][...])
        out_ref[j * tile : (j + 1) * tile, :] = (params[0] * grad).astype(out_ref.dtype)
    if losses:
        rows = total // 8
        tail = loss_rows(losses[0][...] + losses[1][...], total // 2, rows)
        out_ref[2 * tile :, :] = two_parts(tail, width)


def image_grad(params, coefs, units, half, dtype, losses=()):
    n, total, width = len(coefs), coefs[0].shape[1], units[0].shape[1]
    out = [((total // 2 + (16 if losses else 0), width), dtype)]
    args = [params, *coefs, *units, *losses]
    flops = 1024 if losses else 400 * 10**9
    return call(functools.partial(image_kernel, n, half), out, args, smem=1, flops=flops)[0]


def quarter_kernel(own, moved, keep, *go):
    cut = keep.shape[0]
    keep[...] = own[:cut] + moved[:cut].astype(F32)
    for k, ref in enumerate(go):
        at = slice((k + 1) * cut, (k + 2) * cut)
        ref[...] = (own[at] + moved[at].astype(F32)).astype(BF)


def quarters(own, moved):
    cut, width = own.shape[0] // 4, own.shape[1]
    return call(quarter_kernel, [((cut, width), F32)] + [((cut, width), BF)] * 3, [own, moved])


def image_quarter_kernel(own, moved, loss_a, loss_b, keep, loss_out, *go):
    rows = keep.shape[0]
    keep[...] = own[:rows] + moved[:rows].astype(F32)
    tail = moved[own.shape[0] :, :rows].astype(F32)
    loss_out[...] = loss_rows(loss_a[...] + loss_b[...], 0, rows) + tail[0:4] + tail[4:8]
    for k, ref in enumerate(go):
        at = slice((k + 1) * rows, (k + 2) * rows)
        ref[...] = (own[at] + moved[at].astype(F32)).astype(BF)


def back(unit, length, grad):
    inner = jnp.sum(unit * grad, axis=1, keepdims=True)
    return ((grad - unit * inner) / length).astype(BF)


def image_delta_kernel(own, a, b, c, unit, length, out):
    grad = own[...] + a[...].astype(F32) + b[...].astype(F32) + c[...].astype(F32)
    out[...] = back(unit[...], length[...], grad)


def text_kernel(own, a, b, unit, length, feats, keep, go, part_keep, part_go):
    grad = own[...] + a[...].astype(F32) + b[...].astype(F32)
    rows, half = keep.shape[0], part_keep.shape[0]
    keep[...] = grad[:rows]
    go[...] = grad[rows:].astype(BF)
    delta = back(unit[...], length[...], grad)
    part_go[...] = t_mm(feats[:, half:], delta).astype(BF)
    part_keep[...] = t_mm(feats[:, :half], delta)


def weight_kernel(feats, a, b, c, d, e, part_keep, part_go):
    half = part_keep.shape[0]
    delta = jnp.concatenate([a[...], b[...], c[...], d[...], e[...]], axis=0)
    part_go[...] = t_mm(feats[:, half:], delta).astype(BF)
    part_keep[...] = t_mm(feats[:, :half], delta)


def select_kernel(n, *refs):
    feats = jnp.concatenate([r[...] for r in refs[:n]], axis=0)
    refs[n + 1][...] = mm(feats, refs[n][...]).astype(BF)


def select(blocks, pick):
    n, rows = len(blocks), blocks[0].shape[0]
    out = [((n * rows, pick.shape[1]), BF)]
    return call(functools.partial(select_kernel, n), out, [*blocks, pick])[0]


def text_quarter_kernel(own, a, b, c, loss, keep, *go):
    total = own[...] + a[...].astype(F32) + b[...].astype(F32) + c[...].astype(F32)
    cut, width = keep.shape
    keep[...] = total[:cut]
    for k, ref in enumerate(go):
        part = total[(k + 1) * cut : (k + 2) * cut]
        fill = jnp.zeros((ref.shape[0] - 16 - cut, width), F32)
        tail = two_parts(loss[3 - k : 4 - k], width).astype(F32)
        ref[...] = jnp.concatenate([part, fill, tail], axis=0).astype(BF)


def tail_kernel(img, i1, i2, i3, txt, t1, t2, t3, loss, keep, loss_out, *go):
    total_i, total_t, losses = img[...], txt[...], loss[0:1]
    rows, cut = losses.shape[1], total_t.shape[0]
    for ref in (i1, i2, i3):
        total_i = total_i + ref[...].astype(F32)
    for ref in (t1, t2, t3):
        moved = ref[...].astype(F32)
        total_t = total_t + moved[:cut]
        tail = moved[moved.shape[0] - 16 :, :rows]
        losses = losses + tail[0:1] + tail[1:2]
    loss_out[...] = losses / rows
    cut_i, cut_t, width = total_i.shape[0] // 4, cut // 4, total_i.shape[1]
    for k, ref in enumerate((keep, *go)):
        parts = [
            total_i[k * cut_i : (k + 1) * cut_i],
            jnp.zeros((16 - cut_i, width), F32),
            total_t[k * cut_t : (k + 1) * cut_t],
            jnp.zeros((16 - cut_t, width), F32),
        ]
        ref[...] = jnp.concatenate(parts, axis=0).astype(ref.dtype)


def last_kernel(keep, a, b, c, out_i, out_t):
    total = keep[...] + a[...].astype(F32) + b[...].astype(F32) + c[...].astype(F32)
    out_i[...] = total[: out_i.shape[0]]
    out_t[...] = total[16 : 16 + out_t.shape[0]]


def direct(value, axis):
    return [rot(value, axis, k) for k in (1, 2, 3)]


def scatter(keep, go, axis):
    for k in (1, 3, 2):
        keep = keep + rot(go[k - 1], axis, k).astype(F32)
    return keep


def selection(depth, cut, steps):
    names = ("c", "z", "y", "xh", "xl")
    dims = [SIZES[a] if a in steps else 1 for a in names] + [cut]
    away = dict(zip(names + ("row",), (i.reshape(1, -1).astype(np.int32) for i in np.indices(dims))))
    place = 0
    for a in ("xh", "y", "z", "c", "xl"):
        place = place * SIZES[a] + ((lax.axis_index(a) + away[a]) & (SIZES[a] - 1))
    return (jnp.arange(depth)[:, None] == place * cut + away["row"]).astype(BF)


def per_device(image_feats, text_feats, match, w_image, w_text, log_temp, bias):
    img_x, txt_x = image_feats[0], text_feats[0]
    rows, width = img_x.shape[0], w_image.shape[1]
    scale = jnp.exp(log_temp[0])
    params = jnp.stack([scale, bias[0]])

    place = jnp.arange(8 * rows)
    paired = jnp.where(place < rows, jnp.tile(match[0, 0], 8), -1)[None]
    cut, cut_img = txt_x.shape[1] // 128, img_x.shape[1] // 128
    txt_pick = selection(txt_x.shape[1], cut, ("c", "z", "y", "xh", "xl"))
    img_pick = selection(img_x.shape[1], cut_img, ("c", "z", "xh", "xl"))

    pair_rows = 2 * rows
    partner = rot(txt_x, "xh", 1)
    img_x, partner = lax.optimization_barrier((img_x, partner))
    img_near = direct(img_x, "y")
    (pair,) = call(stack_kernel, [((pair_rows, txt_x.shape[1]), BF)], [txt_x, partner])
    before, after = rot(pair, "z", 1), rot(pair, "z", -1)
    far = [rot(before[:rows], "z", 1), rot(after[rows:], "z", -1)]
    unit_0, unit_txt, len_txt = project([pair], w_text, pair_rows, kept=pair_rows)
    txt_feats = select([pair], txt_pick)
    *img_near, before, after, paired, unit_0, unit_txt, txt_feats, img_pick = lax.optimization_barrier(
        (*img_near, before, after, paired, unit_0, unit_txt, txt_feats, img_pick)
    )
    (img_mine,) = call(stack_kernel, [((4 * rows, img_x.shape[1]), BF)], [img_x, *img_near])
    img_moved = rot(img_mine, "c", 1)

    units = [project([before], w_text, pair_rows)[0], None, project([after], w_text, pair_rows)[0]]
    img_moved, units[0], units[2] = lax.optimization_barrier((img_moved, units[0], units[2]))
    images, unit_img, len_img = project([img_mine, img_moved], w_image, pair_rows, kept=rows)
    *far, images = lax.optimization_barrier((*far, images))
    units[1] = project(far, w_text, pair_rows)[0]

    coefs_b, loss_b, far = pair_terms(params, images, [units[1]], split=True)
    far = [rot(far[0], "z", 1), rot(far[1], "z", -1)]
    coefs_a, loss_a, _ = pair_terms(params, images, [units[0], units[2], unit_0], paired)
    losses = [loss_a, loss_b]
    coefs, sets = [*coefs_a, *coefs_b], [units[0], units[2], unit_0, units[1]]
    other = image_grad(params, coefs, sets, 1, BF, losses)
    *grads, own_txt = text_grads(params, images, coefs_a)

    before, after = call(join_kernel, [((pair_rows, width), BF)] * 2, [*grads, *far])
    txt_parts = [rot(before, "z", -1), rot(after, "z", 1)]
    *coefs, _ = lax.optimization_barrier((*coefs, before))
    own = image_grad(params, coefs, sets, 0, F32)
    keep, loss, *go = call(
        image_quarter_kernel,
        [((rows, width), F32), ((4, rows), F32)] + [((rows, width), BF)] * 3,
        [own, rot(other, "c", 1), *losses],
    )
    img_parts = [rot(go[k - 1], "y", -k) for k in (1, 3, 2)]
    (delta_img,) = call(
        image_delta_kernel, [((rows, width), BF)], [keep, *img_parts, unit_img, len_img]
    )
    *txt_parts, _ = lax.optimization_barrier((*txt_parts, delta_img))

    half = txt_x.shape[1] // 2
    own_grad, go_x, part_keep, part_go = call(
        text_kernel,
        [((rows, width), F32), ((rows, width), BF), ((half, width), F32), ((half, width), BF)],
        [own_txt, *txt_parts, unit_txt, len_txt, txt_feats],
    )
    near = rot(delta_img, "y", 1), rot(delta_img, "y", -1)
    keep, *txt_go = quarters(part_keep, rot(part_go, "c", 1))
    *near, keep = lax.optimization_barrier((*near, keep))
    far = [rot(near[0][: rows // 2], "y", 1), rot(near[1][rows // 2 :], "y", -1)]
    img_feats = select([img_mine], img_pick)
    grad_image = mm_t(delta_img, w_image).astype(BF)[None]
    *far, keep, img_feats, grad_image = lax.optimization_barrier((*far, keep, img_feats, grad_image))
    grad_unit_txt = own_grad + rot(go_x, "xh", 1).astype(F32)
    txt_go = [rot(txt_go[k - 1], "z", k) for k in (1, 3, 2)]
    cut_y = keep.shape[0] // 4
    sum_txt, *go = call(
        text_quarter_kernel,
        [((cut_y, width), F32)] + [(((cut_y + 15) // 16 * 16 + 16, width), BF)] * 3,
        [keep, *txt_go, loss],
    )
    txt_go = [rot(go[k - 1], "y", k) for k in (1, 3, 2)]

    half = img_feats.shape[1] // 2
    part_keep, part_go = call(
        weight_kernel,
        [((half, width), F32), ((half, width), BF)],
        [img_feats, delta_img, near[0], *far, near[1]],
    )
    keep, *go = quarters(part_keep, rot(part_go, "c", 1))
    img_go = [rot(go[k - 1], "z", k) for k in (1, 3, 2)]
    keep, row_loss, *go = call(
        tail_kernel,
        [((32, width), F32), ((1, rows), F32)] + [((32, width), BF)] * 3,
        [keep, *img_go, sum_txt, *txt_go, loss],
    )
    moved = []
    for dh, dl in ((0, 1), (1, 0), (1, 1)):
        pairs = [(h * 2 + l, ((h + dh) % 2) * 2 + (l + dl) % 2) for h in (0, 1) for l in (0, 1)]
        moved.append(lax.ppermute(go[2 * dh + dl - 1], ("xh", "xl"), pairs))
    grad_w_image, grad_w_text = call(
        last_kernel, [((cut_img, width), F32), ((cut, width), F32)], [keep, *moved]
    )

    delta_txt = back(unit_txt[:rows], len_txt[:rows], grad_unit_txt)
    grad_text = mm_t(delta_txt, w_text).astype(BF)[None]
    return (row_loss, grad_image, grad_text, grad_w_image, grad_w_text)


def solution(mesh):
    fine = Mesh(mesh.devices.reshape([SIZES[a] for a in AXES]), AXES)
    blk = ("xh", "y", "z", "c")
    in_specs = (
        P("xl", blk, None),
        P("xl", blk, None),
        P("xl", blk, None),
        P(),
        P(),
        P(),
        P(),
    )
    out_specs = (
        P("xl", blk),
        P("xl", blk, None),
        P("xl", blk, None),
        P(AXES, None),
        P(AXES, None),
    )
    return jax.shard_map(
        per_device, mesh=fine, in_specs=in_specs, out_specs=out_specs, check_vma=False
    )
```

```python
import functools

import jax
import jax.numpy as jnp
import numpy as np
from jax import lax
from jax.experimental import pallas as pl
from jax.experimental.pallas import tpu as pltpu
from jax.sharding import Mesh
from jax.sharding import PartitionSpec as P

AXES = ("xh", "y", "z", "c", "xl")
SIZES = {"xh": 2, "y": 4, "z": 4, "c": 2, "xl": 2}
BF = jnp.bfloat16
F32 = jnp.float32
VMEM = pl.BlockSpec(memory_space=pltpu.VMEM)
SMEM = pl.BlockSpec(memory_space=pltpu.SMEM)
MIB = 1 << 20
LONG = 400 * 10**9


def rot(value, axis, steps):
    n = SIZES[axis]
    return lax.ppermute(value, axis, [(i, (i + steps) % n) for i in range(n)])


def mm(a, b):
    return jnp.dot(a, b, preferred_element_type=F32)


def mm_t(a, b):
    return lax.dot_general(a, b, (((1,), (1,)), ((), ())), preferred_element_type=F32)


def t_mm(a, b):
    return lax.dot_general(a, b, (((0,), (0,)), ((), ())), preferred_element_type=F32)


def call(kernel, out, args, smem=0, flops=1024):
    return pl.pallas_call(
        kernel,
        out_shape=[jax.ShapeDtypeStruct(shape, dtype) for shape, dtype in out],
        in_specs=[SMEM] * smem + [VMEM] * (len(args) - smem),
        out_specs=[VMEM] * len(out),
        cost_estimate=pl.CostEstimate(flops=flops, bytes_accessed=1024, transcendentals=0),
        compiler_params=pltpu.CompilerParams(vmem_limit_bytes=24 * MIB),
    )(*args)


def project_kernel(cuts, step, kept, *refs):
    n = len(cuts)
    blocks, w_ref, unit_ref = refs[:n], refs[n], refs[n + 1]
    feats = jnp.concatenate([b[lo:hi, :] for b, (lo, hi) in zip(blocks, cuts)], axis=0)
    for at in range(0, feats.shape[0], step):
        proj = mm(feats[at : at + step], w_ref[...])
        length = jnp.sqrt(jnp.sum(proj * proj, axis=1, keepdims=True) + 1e-06)
        unit = proj / length
        unit_ref[at : at + step, :] = unit.astype(BF)
        if at == 0 and kept:
            refs[n + 2][...] = unit[:kept]
            refs[n + 3][...] = length[:kept]


def project(blocks, weight, step, kept=0):
    blocks = [b if isinstance(b, tuple) else (b, 0, b.shape[0]) for b in blocks]
    cuts = tuple((lo, hi) for _, lo, hi in blocks)
    rows, width = sum(hi - lo for lo, hi in cuts), weight.shape[1]
    out = [((rows, width), BF)]
    if kept:
        out += [((kept, width), F32), ((kept, 1), F32)]
    args = [b for b, _, _ in blocks] + [weight]
    return call(functools.partial(project_kernel, cuts, step, kept), out, args)


def second_kernel(partner, t_before, t_after, own, i_before, i_after, up, down, i_up, i_down, swap):
    rows, half = partner.shape[0], partner.shape[0] // 2
    up[:rows] = partner[...]
    up[rows:] = t_before[:half]
    down[:rows] = partner[...]
    down[rows:] = t_after[half:]
    i_up[...] = i_before[:half]
    i_down[...] = i_after[half:]
    swap[:rows] = own[...]
    swap[rows : 2 * rows] = i_before[...]
    swap[2 * rows :] = i_after[...]


def third_kernel(up, down, i_up, i_down, t_up, t_down, far):
    half = t_up.shape[0]
    t_up[...] = up[:half]
    t_down[...] = down[half : 2 * half]
    far[:half] = i_up[...]
    far[half:] = i_down[...]


def image_tiles(near, far):
    step = far.shape[0]
    return [near.at[k * step : (k + 1) * step, :] for k in range(3)] + [far]


def tile_mm(coef, near, far):
    cut = near.shape[0]
    return mm(coef[:, :cut], near[...]) + mm(coef[:, cut:], far[...])


def pair_kernel(n, first, split, *refs):
    params, tiles, units, at = refs[0], image_tiles(*refs[1:3]), refs[3 : 3 + n], 3 + n
    if first:
        paired = refs[at]
        at += 1
    coefs, loss_ref, grads = refs[at : at + n], refs[at + n], refs[at + n + 1 :]
    scale, offset = params[0], params[1]
    step = refs[2].shape[0]
    for k in range(n):
        own = first and k == n - 1
        for j in range(4):
            cols = slice(j * step, (j + 1) * step)
            margin = scale * mm_t(units[k][...], tiles[j][...]) + offset
            if own:
                place = lax.broadcasted_iota(jnp.int32, margin.shape, 0)
                positive = place == paired[:, cols]
                margin = jnp.where(positive, -margin, margin)
            power = jnp.exp(margin)
            whole = 1.0 + power
            near = power * (1.0 - power * (0.5 - power * (1.0 / 3.0)))
            terms = jnp.where(power < 0.01, near, jnp.log(whole))
            turn = pl.reciprocal(whole, approx=True)
            coeff = power * (turn * (2.0 - whole * turn))
            if own:
                coeff = jnp.where(positive, -coeff, coeff)
            part = jnp.sum(terms, axis=0, keepdims=True)
            loss_ref[:, cols] = part if k == 0 else loss_ref[:, cols] + part
            coefs[k][:, cols] = coeff.astype(BF)
    if split:
        grad = scale * tile_mm(coefs[0], *refs[1:3])
        cut = grad.shape[0] // 2
        grads[0][...] = grad[:cut].astype(BF)
        grads[1][...] = grad[cut:].astype(BF)


def pair_terms(params, images, units, paired=None, split=False):
    n, (rows, width), total = len(units), units[0].shape, 4 * images[1].shape[0]
    first = paired is not None
    grads = [((rows // 2, width), BF)] * 2 if split else []
    out = [((rows, total), BF)] * n + [((1, total), F32)] + grads
    args = [params, *images, *units] + ([paired] if first else [])
    res = call(functools.partial(pair_kernel, n, first, split), out, args, smem=1)
    return res[:n], res[n], res[n + 1 :]


def text_grad_kernel(n, *refs):
    params, images, coefs, grads = refs[0], refs[1:3], refs[3 : 3 + n], refs[3 + n :]
    for coef, grad in zip(coefs, grads):
        grad[...] = params[0] * tile_mm(coef, *images)


def text_grads(params, images, coefs):
    n, out = len(coefs), ((coefs[0].shape[0], images[0].shape[1]), F32)
    args = [params, *images, *coefs]
    return call(functools.partial(text_grad_kernel, n), [out] * n, args, smem=1, flops=LONG)


def join_kernel(before, after, up, down, before_out, after_out):
    cut = up.shape[0]
    before_out[:cut] = before[:cut].astype(BF)
    before_out[cut:] = (before[cut:] + down[...].astype(F32)).astype(BF)
    after_out[:cut] = (after[:cut] + up[...].astype(F32)).astype(BF)
    after_out[cut:] = after[cut:].astype(BF)


def loss_rows(losses, core, rows):
    return jnp.concatenate(
        [losses[:, at : at + rows] for at in range(core * rows, losses.shape[1], 2 * rows)], axis=0
    )


def two_parts(value, width):
    high = value.astype(BF)
    low = (value - high.astype(F32)).astype(BF)
    parts = jnp.concatenate([high, low], axis=0).astype(F32)
    down = jnp.zeros((16 - parts.shape[0], parts.shape[1]), F32)
    parts = jnp.concatenate([parts, down], axis=0)
    right = jnp.zeros((16, width - parts.shape[1]), F32)
    return jnp.concatenate([parts, right], axis=1).astype(BF)


def image_kernel(n, cores, tiles, *refs):
    params, coefs, units = refs[0], refs[1 : 1 + n], refs[1 + n : 1 + 2 * n]
    rest = refs[1 + 2 * n :]
    losses, outs = rest[: len(rest) - len(cores)], rest[len(rest) - len(cores) :]
    rows, width = coefs[0].shape[1] // 8, units[0].shape[1]
    places = [(core, k) for core in cores for k in tiles]

    def columns(coef):
        parts = [coef[:, (2 * k + core) * rows : (2 * k + core + 1) * rows] for core, k in places]
        return jnp.concatenate(parts, axis=1)

    grad = t_mm(columns(coefs[0]), units[0][...])
    for k in range(1, n):
        grad = grad + t_mm(columns(coefs[k]), units[k][...])
    grad = params[0] * grad
    count = len(tiles) * rows
    for at, (core, out) in enumerate(zip(cores, outs)):
        out[:count] = grad[at * count : (at + 1) * count].astype(out.dtype)
        if core and losses:
            out[count:] = two_parts(loss_rows(losses[0][...] + losses[1][...], 1, rows), width)


def image_grad(params, coefs, units, cores, tiles, losses=(), flops=1024):
    n, rows, width = len(coefs), coefs[0].shape[1] // 8, units[0].shape[1]
    count = len(tiles) * rows
    out = [((count + (16 if core and losses else 0), width), BF if core else F32) for core in cores]
    args = [params, *coefs, *units, *losses]
    return call(functools.partial(image_kernel, n, cores, tiles), out, args, smem=1, flops=flops)


def image_far_kernel(own, moved, up, down):
    half = up.shape[0]
    total = own[...] + moved[...].astype(F32)
    up[...] = total[:half].astype(BF)
    down[...] = total[half:].astype(BF)


def image_near_kernel(own, moved, up, down, loss_a, loss_b, keep, loss_out, before, after):
    rows, half = keep.shape[0], up.shape[0]
    keep[...] = own[:rows] + moved[:rows].astype(F32)
    part = own[rows : 2 * rows] + moved[rows : 2 * rows].astype(F32)
    before[:half] = part[:half].astype(BF)
    before[half:] = (part[half:] + down[...].astype(F32)).astype(BF)
    part = own[2 * rows :] + moved[2 * rows : 3 * rows].astype(F32)
    after[:half] = (part[:half] + up[...].astype(F32)).astype(BF)
    after[half:] = part[half:].astype(BF)
    tail = moved[3 * rows :, :rows].astype(F32)
    loss_out[...] = loss_rows(loss_a[...] + loss_b[...], 0, rows) + tail[0:4] + tail[4:8]


def quarter_kernel(own, moved, keep, *go):
    cut = keep.shape[0]
    keep[...] = own[:cut] + moved[:cut].astype(F32)
    for k, ref in enumerate(go):
        at = slice((k + 1) * cut, (k + 2) * cut)
        ref[...] = (own[at] + moved[at].astype(F32)).astype(BF)


def quarters(own, moved):
    cut, width = own.shape[0] // 4, own.shape[1]
    return call(quarter_kernel, [((cut, width), F32)] + [((cut, width), BF)] * 3, [own, moved])


def back(unit, length, grad):
    inner = jnp.sum(unit * grad, axis=1, keepdims=True)
    return ((grad - unit * inner) / length).astype(BF)


def image_delta_kernel(own, a, b, unit, length, out):
    grad = own[...] + a[...].astype(F32) + b[...].astype(F32)
    out[...] = back(unit[...], length[...], grad)


def text_kernel(own, a, b, unit, length, feats, keep, go, part_keep, part_go):
    grad = own[...] + a[...].astype(F32) + b[...].astype(F32)
    rows, half = keep.shape[0], part_keep.shape[0]
    keep[...] = grad[:rows]
    go[...] = grad[rows:].astype(BF)
    delta = back(unit[...], length[...], grad)
    part_go[...] = t_mm(feats[:, half:], delta).astype(BF)
    part_keep[...] = t_mm(feats[:, :half], delta)


def weight_kernel(feats, a, b, c, d, e, part_keep, part_go):
    half = part_keep.shape[0]
    delta = jnp.concatenate([a[...], b[...], c[...], d[...], e[...]], axis=0)
    part_go[...] = t_mm(feats[:, half:], delta).astype(BF)
    part_keep[...] = t_mm(feats[:, :half], delta)


def select_kernel(n, *refs):
    feats = jnp.concatenate([r[...] for r in refs[:n]], axis=0)
    refs[n + 1][...] = mm(feats, refs[n][...]).astype(BF)


def select(blocks, pick):
    n, rows = len(blocks), blocks[0].shape[0]
    out = [((n * rows, pick.shape[1]), BF)]
    return call(functools.partial(select_kernel, n), out, [*blocks, pick])[0]


def text_quarter_kernel(own, a, b, c, loss, keep, *go):
    total = own[...] + a[...].astype(F32) + b[...].astype(F32) + c[...].astype(F32)
    cut, width = keep.shape
    keep[...] = total[:cut]
    for k, ref in enumerate(go):
        part = total[(k + 1) * cut : (k + 2) * cut]
        fill = jnp.zeros((ref.shape[0] - 16 - cut, width), F32)
        row = (2, 3, 1)[k]
        tail = two_parts(loss[row : row + 1], width).astype(F32)
        ref[...] = jnp.concatenate([part, fill, tail], axis=0).astype(BF)


def feature_grad_kernel(delta, weight, out):
    out[...] = mm_t(delta[...], weight[...]).astype(BF)


def tail_kernel(img, i1, i2, i3, txt, t1, t2, t3, loss, keep, loss_out, *go):
    total_i, total_t, losses = img[...], txt[...], loss[0:1]
    rows, cut = losses.shape[1], total_t.shape[0]
    for ref in (i1, i2, i3):
        total_i = total_i + ref[...].astype(F32)
    for ref in (t1, t2, t3):
        moved = ref[...].astype(F32)
        total_t = total_t + moved[:cut]
        tail = moved[moved.shape[0] - 16 :, :rows]
        losses = losses + tail[0:1] + tail[1:2]
    loss_out[...] = losses / rows
    cut_i, cut_t, width = total_i.shape[0] // 4, cut // 4, total_i.shape[1]
    for k, ref in enumerate((keep, *go)):
        parts = [
            total_i[k * cut_i : (k + 1) * cut_i],
            jnp.zeros((16 - cut_i, width), F32),
            total_t[k * cut_t : (k + 1) * cut_t],
            jnp.zeros((16 - cut_t, width), F32),
        ]
        ref[...] = jnp.concatenate(parts, axis=0).astype(ref.dtype)


def last_kernel(keep, a, b, c, out_i, out_t):
    total = keep[...] + a[...].astype(F32) + b[...].astype(F32) + c[...].astype(F32)
    out_i[...] = total[: out_i.shape[0]]
    out_t[...] = total[16 : 16 + out_t.shape[0]]


def selection(depth, cut, steps):
    names = ("c", "z", "y", "xh", "xl")
    dims = [SIZES[a] if a in steps else 1 for a in names] + [cut]
    away = dict(zip(names + ("row",), (i.reshape(1, -1).astype(np.int32) for i in np.indices(dims))))
    place = 0
    for a in ("xh", "y", "z", "c", "xl"):
        place = place * SIZES[a] + ((lax.axis_index(a) + away[a]) & (SIZES[a] - 1))
    return (jnp.arange(depth)[:, None] == place * cut + away["row"]).astype(BF)


def per_device(image_feats, text_feats, match, w_image, w_text, log_temp, bias):
    img_x, txt_x = image_feats[0], text_feats[0]
    rows, width = img_x.shape[0], w_image.shape[1]
    scale = jnp.exp(log_temp[0])
    params = jnp.stack([scale, bias[0]])

    paired = jnp.concatenate([match[0], jnp.full((1, 7 * rows), -1, jnp.int32)], axis=1)
    cut, cut_img = txt_x.shape[1] // 128, img_x.shape[1] // 128
    txt_pick = selection(txt_x.shape[1], cut, ("c", "z", "y", "xh", "xl"))
    img_pick = selection(img_x.shape[1], cut_img, ("c", "z", "xh", "xl"))

    pair_rows = 2 * rows
    half = rows // 2
    partner = rot(txt_x, "xh", 1)
    t_before, t_after = rot(txt_x, "z", 1), rot(txt_x, "z", -1)
    i_before, i_after = rot(img_x, "y", 1), rot(img_x, "y", -1)
    partner, t_before, t_after, i_before, i_after, txt_pick, paired = lax.optimization_barrier(
        (partner, t_before, t_after, i_before, i_after, txt_pick, paired)
    )
    depth_t, depth_i = txt_x.shape[1], img_x.shape[1]
    up, down, i_up, i_down, swap = call(
        second_kernel,
        [((rows + half, depth_t), BF)] * 2 + [((half, depth_i), BF)] * 2 + [((3 * rows, depth_i), BF)],
        [partner, t_before, t_after, img_x, i_before, i_after],
    )
    up, down = rot(up, "z", 1), rot(down, "z", -1)
    i_up, i_down = rot(i_up, "y", 1), rot(i_down, "y", -1)
    swap = rot(swap, "c", 1)

    unit_0, unit_txt, len_txt = project([txt_x, partner], w_text, pair_rows, kept=pair_rows)
    txt_feats = select([txt_x, partner], txt_pick)
    blocks = [img_x, (swap, 0, rows), i_before, (swap, rows, 2 * rows), i_after, (swap, 2 * rows, 3 * rows)]
    near, unit_img, len_img = project(blocks, w_image, pair_rows, kept=rows)
    up, down, i_up, i_down, near, unit_0, txt_feats, img_pick = lax.optimization_barrier(
        (up, down, i_up, i_down, near, unit_0, txt_feats, img_pick)
    )
    t_up, t_down, i_far = call(
        third_kernel,
        [((half, depth_t), BF)] * 2 + [((rows, depth_i), BF)],
        [up, down, i_up, i_down],
    )
    t_up, t_down = rot(t_up, "z", 1), rot(t_down, "z", -1)
    swap = rot(i_far, "c", 1)
    units = [
        project([t_before, (up, 0, rows)], w_text, pair_rows)[0],
        None,
        project([t_after, (down, 0, rows)], w_text, pair_rows)[0],
    ]
    swap, t_up, t_down, units[0], units[2] = lax.optimization_barrier(
        (swap, t_up, t_down, units[0], units[2])
    )
    images = [near, project([i_far, swap], w_image, pair_rows)[0]]
    far = [(up, rows, rows + half), (down, rows, rows + half), t_up, t_down]
    units[1] = project(far, w_text, pair_rows)[0]

    coefs_b, loss_b, far = pair_terms(params, images, [units[1]], split=True)
    far = [rot(far[0], "z", 1), rot(far[1], "z", -1)]
    coefs_a, loss_a, _ = pair_terms(params, images, [units[0], units[2], unit_0], paired)
    losses = [loss_a, loss_b]
    coefs, sets = [*coefs_a, *coefs_b], [units[0], units[2], unit_0, units[1]]
    own_far, other_far = image_grad(params, coefs, sets, (0, 1), (3,))
    other_far = rot(other_far, "c", 1)
    (other,) = image_grad(params, coefs, sets, (1,), (0, 1, 2), losses)
    *grads, own_txt = text_grads(params, images, coefs_a)

    before, after = call(join_kernel, [((pair_rows, width), BF)] * 2, [*grads, *far])
    txt_parts = [rot(before, "z", -1), rot(after, "z", 1)]
    i_up, i_down = call(image_far_kernel, [((half, width), BF)] * 2, [own_far, other_far])
    *coefs, _, _ = lax.optimization_barrier((*coefs, before, i_up))
    (own,) = image_grad(params, coefs, sets, (0,), (0, 1, 2), flops=LONG)
    keep, loss, i_before_go, i_after_go = call(
        image_near_kernel,
        [((rows, width), F32), ((4, rows), F32)] + [((rows, width), BF)] * 2,
        [own, rot(other, "c", 1), rot(i_up, "y", 1), rot(i_down, "y", -1), *losses],
    )
    img_parts = [rot(i_before_go, "y", -1), rot(i_after_go, "y", 1)]
    (delta_img,) = call(
        image_delta_kernel, [((rows, width), BF)], [keep, *img_parts, unit_img, len_img]
    )
    *txt_parts, _ = lax.optimization_barrier((*txt_parts, delta_img))

    half_t = txt_x.shape[1] // 2
    own_grad, go_x, part_keep, part_go = call(
        text_kernel,
        [((rows, width), F32), ((rows, width), BF), ((half_t, width), F32), ((half_t, width), BF)],
        [own_txt, *txt_parts, unit_txt, len_txt, txt_feats],
    )
    gathered = rot(delta_img, "y", 1), rot(delta_img, "y", -1)
    keep, *txt_go = quarters(part_keep, rot(part_go, "c", 1))
    txt_go = [rot(txt_go[k - 1], "z", k) for k in (1, 3, 2)]
    *gathered, txt_go[0] = lax.optimization_barrier((*gathered, txt_go[0]))
    far = [rot(gathered[0][:half], "y", 1), rot(gathered[1][half:], "y", -1)]
    img_feats = select([img_x, i_before, i_after, i_far], img_pick)
    (grad_image,) = call(
        feature_grad_kernel, [((rows, img_x.shape[1]), BF)], [delta_img, w_image]
    )
    txt_go[0], txt_go[1], txt_go[2], keep, moved, *far, img_feats, grad_image = lax.optimization_barrier(
        (*txt_go, keep, rot(go_x, "xh", 1), *far, img_feats, grad_image)
    )
    grad_unit_txt = own_grad + moved.astype(F32)
    half_i = img_feats.shape[1] // 2
    part_keep, part_go = call(
        weight_kernel,
        [((half_i, width), F32), ((half_i, width), BF)],
        [img_feats, delta_img, *gathered, *far],
    )
    keep_i, *go = quarters(part_keep, rot(part_go, "c", 1))
    img_go = [rot(go[k - 1], "z", k) for k in (1, 3, 2)]
    cut_y = keep.shape[0] // 4
    sum_txt, *go = call(
        text_quarter_kernel,
        [((cut_y, width), F32)] + [(((cut_y + 15) // 16 * 16 + 16, width), BF)] * 3,
        [keep, *txt_go, loss],
    )
    txt_go = [rot(go[k - 1], "y", k) for k in (1, 3, 2)]
    keep, row_loss, *go = call(
        tail_kernel,
        [((32, width), F32), ((1, rows), F32)] + [((32, width), BF)] * 3,
        [keep_i, *img_go, sum_txt, *txt_go, loss],
    )
    moved = []
    for dh, dl in ((0, 1), (1, 0), (1, 1)):
        pairs = [(h * 2 + l, ((h + dh) % 2) * 2 + (l + dl) % 2) for h in (0, 1) for l in (0, 1)]
        moved.append(lax.ppermute(go[2 * dh + dl - 1], ("xh", "xl"), pairs))
    grad_w_image, grad_w_text = call(
        last_kernel, [((cut_img, width), F32), ((cut, width), F32)], [keep, *moved]
    )

    delta_txt = back(unit_txt[:rows], len_txt[:rows], grad_unit_txt)
    grad_text = mm_t(delta_txt, w_text).astype(BF)[None]
    return (row_loss, grad_image[None], grad_text, grad_w_image, grad_w_text)


def solution(mesh):
    fine = Mesh(mesh.devices.reshape([SIZES[a] for a in AXES]), AXES)
    blk = ("xh", "y", "z", "c")
    in_specs = (
        P("xl", blk, None),
        P("xl", blk, None),
        P("xl", blk, None),
        P(),
        P(),
        P(),
        P(),
    )
    out_specs = (
        P("xl", blk),
        P("xl", blk, None),
        P("xl", blk, None),
        P(AXES, None),
        P(AXES, None),
    )
    return jax.shard_map(
        per_device, mesh=fine, in_specs=in_specs, out_specs=out_specs, check_vma=False
    )
```

```python
import functools

import jax
import jax.numpy as jnp
import numpy as np
from jax import lax
from jax.experimental import pallas as pl
from jax.experimental.pallas import tpu as pltpu
from jax.sharding import Mesh
from jax.sharding import PartitionSpec as P

AXES = ("xh", "y", "z", "c", "xl")
SIZES = {"xh": 2, "y": 4, "z": 4, "c": 2, "xl": 2}
BF = jnp.bfloat16
F32 = jnp.float32
VMEM = pl.BlockSpec(memory_space=pltpu.VMEM)
SMEM = pl.BlockSpec(memory_space=pltpu.SMEM)
MIB = 1 << 20
LONG = 400 * 10**9


def rot(value, axis, steps):
    n = SIZES[axis]
    return lax.ppermute(value, axis, [(i, (i + steps) % n) for i in range(n)])


def mm(a, b):
    return jnp.dot(a, b, preferred_element_type=F32)


def mm_t(a, b):
    return lax.dot_general(a, b, (((1,), (1,)), ((), ())), preferred_element_type=F32)


def t_mm(a, b):
    return lax.dot_general(a, b, (((0,), (0,)), ((), ())), preferred_element_type=F32)


def call(kernel, out, args, smem=0, flops=1024):
    return pl.pallas_call(
        kernel,
        out_shape=[jax.ShapeDtypeStruct(shape, dtype) for shape, dtype in out],
        in_specs=[SMEM] * smem + [VMEM] * (len(args) - smem),
        out_specs=[VMEM] * len(out),
        cost_estimate=pl.CostEstimate(flops=flops, bytes_accessed=1024, transcendentals=0),
        compiler_params=pltpu.CompilerParams(vmem_limit_bytes=24 * MIB),
    )(*args)


def project_kernel(n, step, kept, *refs):
    blocks, w_ref, unit_ref = refs[:n], refs[n], refs[n + 1]
    feats = jnp.concatenate([b[...] for b in blocks], axis=0)
    for at in range(0, feats.shape[0], step):
        proj = mm(feats[at : at + step], w_ref[...])
        length = jnp.sqrt(jnp.sum(proj * proj, axis=1, keepdims=True) + 1e-06)
        unit = proj / length
        unit_ref[at : at + step, :] = unit.astype(BF)
        if at == 0 and kept:
            refs[n + 2][...] = unit[:kept]
            refs[n + 3][...] = length[:kept]


def project(blocks, weight, step, kept=0):
    n, rows, width = len(blocks), sum(b.shape[0] for b in blocks), weight.shape[1]
    out = [((rows, width), BF)]
    if kept:
        out += [((kept, width), F32), ((kept, 1), F32)]
    return list(call(functools.partial(project_kernel, n, step, kept), out, [*blocks, weight]))


def stack_kernel(*refs):
    rows = refs[0].shape[0]
    for k, ref in enumerate(refs[:-1]):
        refs[-1][k * rows : (k + 1) * rows, :] = ref[...]


def pair_kernel(n, first, split, *refs):
    params, images = refs[0], refs[1]
    units, at = refs[2 : 2 + n], 2 + n
    if first:
        paired = refs[at]
        at += 1
    coefs, loss_ref, grads = refs[at : at + n], refs[at + n], refs[at + n + 1 :]
    scale, offset = params[0], params[1]
    step = images.shape[0] // 4
    for k in range(n):
        own = first and k == n - 1
        for j in range(4):
            cols = slice(j * step, (j + 1) * step)
            margin = scale * mm_t(units[k][...], images[cols, :]) + offset
            if own:
                place = lax.broadcasted_iota(jnp.int32, margin.shape, 0)
                positive = place == paired[:, cols]
                margin = jnp.where(positive, -margin, margin)
            power = jnp.exp(margin)
            whole = 1.0 + power
            near = power * (1.0 - power * (0.5 - power * (1.0 / 3.0)))
            terms = jnp.where(power < 0.01, near, jnp.log(whole))
            turn = pl.reciprocal(whole, approx=True)
            coeff = power * (turn * (2.0 - whole * turn))
            if own:
                coeff = jnp.where(positive, -coeff, coeff)
            part = jnp.sum(terms, axis=0, keepdims=True)
            loss_ref[:, cols] = part if k == 0 else loss_ref[:, cols] + part
            coefs[k][:, cols] = coeff.astype(BF)
    if split:
        grad = scale * mm(coefs[0][...], images[...])
        cut = grad.shape[0] // 2
        grads[0][...] = grad[:cut].astype(BF)
        grads[1][...] = grad[cut:].astype(BF)


def pair_terms(params, images, units, paired=None, split=False):
    n, (rows, width), total = len(units), units[0].shape, images.shape[0]
    first = paired is not None
    grads = [((rows // 2, width), BF)] * 2 if split else []
    out = [((rows, total), BF)] * n + [((1, total), F32)] + grads
    args = [params, images, *units] + ([paired] if first else [])
    res = call(functools.partial(pair_kernel, n, first, split), out, args, smem=1)
    return res[:n], res[n], list(res[n + 1 :])


def text_grad_kernel(n, *refs):
    params, images, coefs, grads = refs[0], refs[1], refs[2 : 2 + n], refs[2 + n :]
    for coef, grad in zip(coefs, grads):
        grad[...] = params[0] * mm(coef[...], images[...])


def text_grads(params, images, coefs):
    n, out = len(coefs), ((coefs[0].shape[0], images.shape[1]), F32)
    return call(functools.partial(text_grad_kernel, n), [out] * n, [params, images, *coefs], smem=1)


def join_kernel(before, after, up, down, before_out, after_out):
    cut = up.shape[0]
    before_out[:cut] = before[:cut].astype(BF)
    before_out[cut:] = (before[cut:] + down[...].astype(F32)).astype(BF)
    after_out[:cut] = (after[:cut] + up[...].astype(F32)).astype(BF)
    after_out[cut:] = after[cut:].astype(BF)


def loss_rows(losses, at, rows):
    return jnp.concatenate([losses[:, at + k * rows : at + (k + 1) * rows] for k in range(4)], axis=0)


def two_parts(value, width):
    high = value.astype(BF)
    low = (value - high.astype(F32)).astype(BF)
    parts = jnp.concatenate([high, low], axis=0).astype(F32)
    down = jnp.zeros((16 - parts.shape[0], parts.shape[1]), F32)
    parts = jnp.concatenate([parts, down], axis=0)
    right = jnp.zeros((16, width - parts.shape[1]), F32)
    return jnp.concatenate([parts, right], axis=1).astype(BF)


def image_kernel(n, half, *refs):
    params, coefs, units = refs[0], refs[1 : 1 + n], refs[1 + n : 1 + 2 * n]
    *losses, out_ref = refs[1 + 2 * n :]
    total, width = coefs[0].shape[1], units[0].shape[1]
    tile = total // 4
    for j in range(2):
        cols = slice((2 * half + j) * tile, (2 * half + j + 1) * tile)
        grad = t_mm(coefs[0][:, cols], units[0][...])
        for k in range(1, n):
            grad = grad + t_mm(coefs[k][:, cols], units[k][...])
        out_ref[j * tile : (j + 1) * tile, :] = (params[0] * grad).astype(out_ref.dtype)
    if losses:
        rows = total // 8
        tail = loss_rows(losses[0][...] + losses[1][...], total // 2, rows)
        out_ref[2 * tile :, :] = two_parts(tail, width)


def image_grad(params, coefs, units, half, dtype, losses=()):
    n, total, width = len(coefs), coefs[0].shape[1], units[0].shape[1]
    out = [((total // 2 + (16 if losses else 0), width), dtype)]
    args = [params, *coefs, *units, *losses]
    flops = 1024 if losses else LONG
    return call(functools.partial(image_kernel, n, half), out, args, smem=1, flops=flops)[0]


def quarter_kernel(own, moved, keep, *go):
    cut = keep.shape[0]
    keep[...] = own[:cut] + moved[:cut].astype(F32)
    for k, ref in enumerate(go):
        at = slice((k + 1) * cut, (k + 2) * cut)
        ref[...] = (own[at] + moved[at].astype(F32)).astype(BF)


def quarters(own, moved):
    cut, width = own.shape[0] // 4, own.shape[1]
    return call(quarter_kernel, [((cut, width), F32)] + [((cut, width), BF)] * 3, [own, moved])


def image_quarter_kernel(own, moved, loss_a, loss_b, keep, loss_out, *go):
    rows = keep.shape[0]
    keep[...] = own[:rows] + moved[:rows].astype(F32)
    tail = moved[own.shape[0] :, :rows].astype(F32)
    loss_out[...] = loss_rows(loss_a[...] + loss_b[...], 0, rows) + tail[0:4] + tail[4:8]
    for k, ref in enumerate(go):
        at = slice((k + 1) * rows, (k + 2) * rows)
        ref[...] = (own[at] + moved[at].astype(F32)).astype(BF)


def back(unit, length, grad):
    inner = jnp.sum(unit * grad, axis=1, keepdims=True)
    return ((grad - unit * inner) / length).astype(BF)


def image_delta_kernel(own, a, b, c, unit, length, out):
    grad = own[...] + a[...].astype(F32) + b[...].astype(F32) + c[...].astype(F32)
    out[...] = back(unit[...], length[...], grad)


def text_kernel(own, a, b, keep, go):
    grad = own[...] + a[...].astype(F32) + b[...].astype(F32)
    rows = keep.shape[0]
    keep[...] = grad[:rows]
    go[...] = grad[rows:].astype(BF)


def text_weight_kernel(n, *refs):
    pick, part_keep, part_go = refs[-3:]
    half = part_keep.shape[0]
    feats, units, lengths, grads = refs[:n], refs[n : 2 * n], refs[2 * n : 3 * n], refs[3 * n : -3]
    deltas = []
    for k in range(n):
        grad = grads[k][...] if k < n - 1 else jnp.concatenate([g[...] for g in grads[k:]], axis=0)
        deltas.append(back(units[k][...], lengths[k][...], grad.astype(F32)))
    delta = jnp.concatenate(deltas, axis=0)
    feats = jnp.concatenate([f[...] for f in feats], axis=0)
    feats = mm(feats, pick[...]).astype(BF)
    part_go[...] = t_mm(feats[:, half:], delta).astype(BF)
    part_keep[...] = t_mm(feats[:, :half], delta)


def weight_kernel(feats, a, b, c, d, part_keep, part_go):
    half = part_keep.shape[0]
    delta = jnp.concatenate([a[...], b[...], c[...], d[...]], axis=0)
    part_go[...] = t_mm(feats[:, half:], delta).astype(BF)
    part_keep[...] = t_mm(feats[:, :half], delta)


def select_kernel(n, *refs):
    feats = jnp.concatenate([r[...] for r in refs[:n]], axis=0)
    refs[n + 1][...] = mm(feats, refs[n][...]).astype(BF)


def select(blocks, pick):
    n, rows = len(blocks), blocks[0].shape[0]
    out = [((n * rows, pick.shape[1]), BF)]
    return call(functools.partial(select_kernel, n), out, [*blocks, pick])[0]


def feature_grad_kernel(delta, weight, out):
    out[...] = mm_t(delta[...], weight[...]).astype(BF)


def text_quarter_kernel(own, a, b, c, loss, keep, *go):
    total = own[...] + a[...].astype(F32) + b[...].astype(F32) + c[...].astype(F32)
    cut, width = keep.shape
    keep[...] = total[:cut]
    for k, ref in enumerate(go):
        part = total[(k + 1) * cut : (k + 2) * cut]
        fill = jnp.zeros((ref.shape[0] - 16 - cut, width), F32)
        tail = two_parts(loss[3 - k : 4 - k], width).astype(F32)
        ref[...] = jnp.concatenate([part, fill, tail], axis=0).astype(BF)


def tail_kernel(img, i1, i2, i3, txt, t1, t2, t3, loss, keep, loss_out, *go):
    total_i, total_t, losses = img[...], txt[...], loss[0:1]
    rows, cut = losses.shape[1], total_t.shape[0]
    for ref in (i1, i2, i3):
        total_i = total_i + ref[...].astype(F32)
    for ref in (t1, t2, t3):
        moved = ref[...].astype(F32)
        total_t = total_t + moved[:cut]
        tail = moved[moved.shape[0] - 16 :, :rows]
        losses = losses + tail[0:1] + tail[1:2]
    loss_out[...] = losses / rows
    cut_i, cut_t, width = total_i.shape[0] // 4, cut // 4, total_i.shape[1]
    for k, ref in enumerate((keep, *go)):
        parts = [
            total_i[k * cut_i : (k + 1) * cut_i],
            jnp.zeros((16 - cut_i, width), F32),
            total_t[k * cut_t : (k + 1) * cut_t],
            jnp.zeros((16 - cut_t, width), F32),
        ]
        ref[...] = jnp.concatenate(parts, axis=0).astype(ref.dtype)


def last_kernel(keep, a, b, c, out_i, out_t):
    total = keep[...] + a[...].astype(F32) + b[...].astype(F32) + c[...].astype(F32)
    out_i[...] = total[: out_i.shape[0]]
    out_t[...] = total[16 : 16 + out_t.shape[0]]


def selection(depth, cut, steps):
    names = ("c", "z", "y", "xh", "xl")
    dims = [SIZES[a] if a in steps else 1 for a in names] + [cut]
    away = dict(zip(names + ("row",), (i.reshape(1, -1).astype(np.int32) for i in np.indices(dims))))
    place = 0
    for a in ("xh", "y", "z", "c", "xl"):
        place = place * SIZES[a] + ((lax.axis_index(a) + away[a]) & (SIZES[a] - 1))
    return (jnp.arange(depth)[:, None] == place * cut + away["row"]).astype(BF)


def per_device(image_feats, text_feats, match, w_image, w_text, log_temp, bias):
    img_x, txt_x = image_feats[0], text_feats[0]
    rows, width = img_x.shape[0], w_image.shape[1]
    scale = jnp.exp(log_temp[0])
    params = jnp.stack([scale, bias[0]])

    paired = jnp.concatenate([match[0], jnp.full((1, 7 * rows), -1, jnp.int32)], axis=1)
    cut, cut_img = txt_x.shape[1] // 128, img_x.shape[1] // 128
    txt_pick = selection(txt_x.shape[1], cut, ("c", "z", "y", "xh", "xl"))
    img_pick = selection(img_x.shape[1], cut_img, ("c", "z", "xh", "xl"))

    pair_rows = 2 * rows
    partner = rot(txt_x, "xh", 1)
    img_last, partner = lax.optimization_barrier((img_x, partner))
    img_near = [rot(img_x, "y", 1), rot(img_last, "y", 2), rot(img_x, "y", 3)]
    (pair,) = call(stack_kernel, [((pair_rows, txt_x.shape[1]), BF)], [txt_x, partner])
    before, after = rot(pair, "z", 1), rot(pair, "z", -1)
    far = [rot(before[:rows], "z", 1), rot(after[rows:], "z", -1)]
    unit_0, unit_txt, len_txt = project([pair], w_text, pair_rows, kept=pair_rows)
    *img_near, before, after, paired, unit_0, unit_txt, txt_pick, img_pick = lax.optimization_barrier(
        (*img_near, before, after, paired, unit_0, unit_txt, txt_pick, img_pick)
    )
    (img_mine,) = call(stack_kernel, [((4 * rows, img_x.shape[1]), BF)], [img_x, *img_near])
    img_moved = rot(img_mine, "c", 1)

    sets = [project([before], w_text, pair_rows, kept=pair_rows), None]
    sets.append(project([after], w_text, pair_rows, kept=pair_rows))
    img_moved, sets[0][0], sets[2][0] = lax.optimization_barrier((img_moved, sets[0][0], sets[2][0]))
    images, unit_img, len_img = project([img_mine, img_moved], w_image, pair_rows, kept=rows)
    *far, images = lax.optimization_barrier((*far, images))
    (txt_far,) = call(stack_kernel, [((pair_rows, txt_x.shape[1]), BF)], far)
    sets[1] = project([txt_far], w_text, pair_rows, kept=pair_rows)
    units = [part[0] for part in sets]

    coefs_b, loss_b, far_grad = pair_terms(params, images, [units[1]], split=True)
    far = [rot(far_grad[0], "z", 1), rot(far_grad[1], "z", -1)]
    coefs_a, loss_a, _ = pair_terms(params, images, [units[0], units[2], unit_0], paired)
    losses = [loss_a, loss_b]
    coefs, rows_of = [*coefs_a, *coefs_b], [units[0], units[2], unit_0, units[1]]
    other = image_grad(params, coefs, rows_of, 1, BF, losses)
    own = image_grad(params, coefs, rows_of, 0, F32)
    *coefs_a, own = lax.optimization_barrier((*coefs_a, own))
    *grads, own_txt = text_grads(params, images, coefs_a)

    keep, loss, *go = call(
        image_quarter_kernel,
        [((rows, width), F32), ((4, rows), F32)] + [((rows, width), BF)] * 3,
        [own, rot(other, "c", 1), *losses],
    )
    img_parts = [rot(go[k - 1], "y", -k) for k in (1, 3, 2)]
    up, down, keep = lax.optimization_barrier((*far, keep))
    before_go, after_go = call(join_kernel, [((pair_rows, width), BF)] * 2, [*grads, up, down])
    txt_parts = [rot(before_go, "z", -1), rot(after_go, "z", 1)]

    half_t = txt_x.shape[1] // 2
    feats = [pair, before, after, txt_far]
    row_units = [unit_txt, sets[0][1], sets[2][1], sets[1][1]]
    lengths = [len_txt, sets[0][2], sets[2][2], sets[1][2]]
    far_grad[0], _ = lax.optimization_barrier((far_grad[0], before_go))
    part_keep, part_go = call(
        functools.partial(text_weight_kernel, 4),
        [((half_t, width), F32), ((half_t, width), BF)],
        [*feats, *row_units, *lengths, own_txt, *grads, *far_grad, txt_pick],
        flops=LONG,
    )
    img_parts[0], img_parts[1], img_parts[2], part_keep = lax.optimization_barrier((*img_parts, part_keep))
    (delta_img,) = call(
        image_delta_kernel,
        [((rows, width), BF)],
        [keep, *img_parts, unit_img, len_img],
        flops=LONG,
    )
    gathered = [rot(delta_img, "y", k) for k in (1, 2, 3)]
    keep, *txt_go = quarters(part_keep, rot(part_go, "c", 1))
    txt_go = [rot(txt_go[k - 1], "z", k) for k in (1, 3, 2)]
    own_grad, go_x = call(
        text_kernel, [((rows, width), F32), ((rows, width), BF)], [own_txt, *txt_parts]
    )
    img_feats = select([img_mine], img_pick)
    (grad_image,) = call(
        feature_grad_kernel, [((rows, img_x.shape[1]), BF)], [delta_img, w_image]
    )
    *gathered, txt_go[0], txt_go[1], moved, img_feats, grad_image = lax.optimization_barrier(
        (*gathered, txt_go[0], txt_go[1], rot(go_x, "xh", 1), img_feats, grad_image)
    )
    grad_unit_txt = own_grad + moved.astype(F32)
    half_i = img_feats.shape[1] // 2
    part_keep, part_go = call(
        weight_kernel,
        [((half_i, width), F32), ((half_i, width), BF)],
        [img_feats, delta_img, *gathered],
    )
    keep_i, *go = quarters(part_keep, rot(part_go, "c", 1))
    img_go = [rot(go[k - 1], "z", k) for k in (1, 3, 2)]
    cut_y = keep.shape[0] // 4
    sum_txt, *go = call(
        text_quarter_kernel,
        [((cut_y, width), F32)] + [(((cut_y + 15) // 16 * 16 + 16, width), BF)] * 3,
        [keep, *txt_go, loss],
    )
    txt_go = [rot(go[k - 1], "y", k) for k in (1, 3, 2)]
    keep, row_loss, *go = call(
        tail_kernel,
        [((32, width), F32), ((1, rows), F32)] + [((32, width), BF)] * 3,
        [keep_i, *img_go, sum_txt, *txt_go, loss],
    )
    moved = []
    for dh, dl in ((0, 1), (1, 0), (1, 1)):
        pairs = [(h * 2 + l, ((h + dh) % 2) * 2 + (l + dl) % 2) for h in (0, 1) for l in (0, 1)]
        moved.append(lax.ppermute(go[2 * dh + dl - 1], ("xh", "xl"), pairs))
    grad_w_image, grad_w_text = call(
        last_kernel, [((cut_img, width), F32), ((cut, width), F32)], [keep, *moved]
    )

    delta_txt = back(unit_txt[:rows], len_txt[:rows], grad_unit_txt)
    grad_text = mm_t(delta_txt, w_text).astype(BF)[None]
    return (row_loss, grad_image[None], grad_text, grad_w_image, grad_w_text)


def solution(mesh):
    fine = Mesh(mesh.devices.reshape([SIZES[a] for a in AXES]), AXES)
    blk = ("xh", "y", "z", "c")
    in_specs = (
        P("xl", blk, None),
        P("xl", blk, None),
        P("xl", blk, None),
        P(),
        P(),
        P(),
        P(),
    )
    out_specs = (
        P("xl", blk),
        P("xl", blk, None),
        P("xl", blk, None),
        P(AXES, None),
        P(AXES, None),
    )
    return jax.shard_map(
        per_device, mesh=fine, in_specs=in_specs, out_specs=out_specs, check_vma=False
    )
```

```python
import functools

import jax
import jax.numpy as jnp
import numpy as np
from jax import lax
from jax.experimental import pallas as pl
from jax.experimental.pallas import tpu as pltpu
from jax.sharding import Mesh
from jax.sharding import PartitionSpec as P

AXES = ("xh", "y", "z", "c", "xl")
SIZES = {"xh": 2, "y": 4, "z": 4, "c": 2, "xl": 2}
BF = jnp.bfloat16
F32 = jnp.float32
VMEM = pl.BlockSpec(memory_space=pltpu.VMEM)
SMEM = pl.BlockSpec(memory_space=pltpu.SMEM)
MIB = 1 << 20
LONG = 400 * 10**9


def rot(value, axis, steps):
    n = SIZES[axis]
    return lax.ppermute(value, axis, [(i, (i + steps) % n) for i in range(n)])


def mm(a, b):
    return jnp.dot(a, b, preferred_element_type=F32)


def mm_t(a, b):
    return lax.dot_general(a, b, (((1,), (1,)), ((), ())), preferred_element_type=F32)


def t_mm(a, b):
    return lax.dot_general(a, b, (((0,), (0,)), ((), ())), preferred_element_type=F32)


def call(kernel, out, args, smem=0, flops=1024, mib=24):
    return pl.pallas_call(
        kernel,
        out_shape=[jax.ShapeDtypeStruct(shape, dtype) for shape, dtype in out],
        in_specs=[SMEM] * smem + [VMEM] * (len(args) - smem),
        out_specs=[VMEM] * len(out),
        cost_estimate=pl.CostEstimate(flops=flops, bytes_accessed=1024, transcendentals=0),
        compiler_params=pltpu.CompilerParams(vmem_limit_bytes=mib * MIB),
    )(*args)


def project_kernel(n, step, kept, *refs):
    blocks, w_ref, unit_ref = refs[:n], refs[n], refs[n + 1]
    feats = jnp.concatenate([b[...] for b in blocks], axis=0)
    for at in range(0, feats.shape[0], step):
        proj = mm(feats[at : at + step], w_ref[...])
        length = jnp.sqrt(jnp.sum(proj * proj, axis=1, keepdims=True) + 1e-06)
        unit = proj / length
        unit_ref[at : at + step, :] = unit.astype(BF)
        if at == 0 and kept:
            refs[n + 2][...] = unit[:kept]
            refs[n + 3][...] = length[:kept]


def project(blocks, weight, step, kept=0):
    n, rows, width = len(blocks), sum(b.shape[0] for b in blocks), weight.shape[1]
    out = [((rows, width), BF)]
    if kept:
        out += [((kept, width), F32), ((kept, 1), F32)]
    return list(call(functools.partial(project_kernel, n, step, kept), out, [*blocks, weight]))


def stack_kernel(*refs):
    rows = refs[0].shape[0]
    for k, ref in enumerate(refs[:-1]):
        refs[-1][k * rows : (k + 1) * rows, :] = ref[...]


def pair_kernel(n, *refs):
    params, images = refs[0], refs[1]
    units, paired, coefs, loss_ref = refs[2 : 2 + n], refs[2 + n], refs[3 + n : -1], refs[-1]
    scale, offset = params[0], params[1]
    step = images.shape[0] // 4
    for k in range(n):
        own = k == n - 1
        for j in range(4):
            cols = slice(j * step, (j + 1) * step)
            margin = scale * mm_t(units[k][...], images[cols, :]) + offset
            if own:
                place = lax.broadcasted_iota(jnp.int32, margin.shape, 0)
                positive = place == paired[:, cols]
                margin = jnp.where(positive, -margin, margin)
            power = jnp.exp(margin)
            whole = 1.0 + power
            near = power * (1.0 - power * (0.5 - power * (1.0 / 3.0)))
            terms = jnp.where(power < 0.01, near, jnp.log(whole))
            turn = pl.reciprocal(whole, approx=True)
            coeff = power * (turn * (2.0 - whole * turn))
            if own:
                coeff = jnp.where(positive, -coeff, coeff)
            part = jnp.sum(terms, axis=0, keepdims=True)
            loss_ref[:, cols] = part if k == 0 else loss_ref[:, cols] + part
            coefs[k][:, cols] = coeff.astype(BF)


def pair_terms(params, images, units, paired):
    n, rows, total = len(units), units[0].shape[0], images.shape[0]
    out = [((rows, total), BF)] * n + [((1, total), F32)]
    *coefs, losses = call(
        functools.partial(pair_kernel, n), out, [params, images, *units, paired], smem=1
    )
    return coefs, losses


def far_kernel(params, images, coef, up, down):
    grad = params[0] * mm(coef[...], images[...])
    cut = grad.shape[0] // 2
    up[...] = grad[:cut].astype(BF)
    down[...] = grad[cut:].astype(BF)


def join_kernel(before, after, up, down, before_out, after_out):
    cut = up.shape[0]
    before_out[:cut] = before[:cut].astype(BF)
    before_out[cut:] = (before[cut:] + down[...].astype(F32)).astype(BF)
    after_out[:cut] = (after[:cut] + up[...].astype(F32)).astype(BF)
    after_out[cut:] = after[cut:].astype(BF)


def loss_rows(losses, at, rows):
    return jnp.concatenate([losses[:, at + k * rows : at + (k + 1) * rows] for k in range(4)], axis=0)


def two_parts(value, width):
    high = value.astype(BF)
    low = (value - high.astype(F32)).astype(BF)
    parts = jnp.concatenate([high, low], axis=0).astype(F32)
    down = jnp.zeros((16 - parts.shape[0], parts.shape[1]), F32)
    parts = jnp.concatenate([parts, down], axis=0)
    right = jnp.zeros((16, width - parts.shape[1]), F32)
    return jnp.concatenate([parts, right], axis=1).astype(BF)


def image_kernel(n, half, *refs):
    params, coefs, units = refs[0], refs[1 : 1 + n], refs[1 + n : 1 + 2 * n]
    *losses, out_ref = refs[1 + 2 * n :]
    total, width = coefs[0].shape[1], units[0].shape[1]
    tile = total // 4
    for j in range(2):
        cols = slice((2 * half + j) * tile, (2 * half + j + 1) * tile)
        grad = t_mm(coefs[0][:, cols], units[0][...])
        for k in range(1, n):
            grad = grad + t_mm(coefs[k][:, cols], units[k][...])
        out_ref[j * tile : (j + 1) * tile, :] = (params[0] * grad).astype(out_ref.dtype)
    if losses:
        rows = total // 8
        tail = loss_rows(losses[0][...], total // 2, rows)
        out_ref[2 * tile :, :] = two_parts(tail, width)


def image_grad(params, coefs, units, half, dtype, losses=()):
    n, total, width = len(coefs), coefs[0].shape[1], units[0].shape[1]
    out = [((total // 2 + (16 if losses else 0), width), dtype)]
    args = [params, *coefs, *units, *losses]
    flops = 1024 if losses else LONG
    return call(functools.partial(image_kernel, n, half), out, args, smem=1, flops=flops)[0]


def quarter_kernel(own, moved, keep, *go):
    cut = keep.shape[0]
    keep[...] = own[:cut] + moved[:cut].astype(F32)
    for k, ref in enumerate(go):
        at = slice((k + 1) * cut, (k + 2) * cut)
        ref[...] = (own[at] + moved[at].astype(F32)).astype(BF)


def quarters(own, moved, flops=1024):
    cut, width = own.shape[0] // 4, own.shape[1]
    out = [((cut, width), F32)] + [((cut, width), BF)] * 3
    return call(quarter_kernel, out, [own, moved], flops=flops)


def image_quarter_kernel(own, moved, losses, keep, loss_out, *go):
    rows = keep.shape[0]
    keep[...] = own[:rows] + moved[:rows].astype(F32)
    tail = moved[own.shape[0] :, :rows].astype(F32)
    loss_out[...] = loss_rows(losses[...], 0, rows) + tail[0:4] + tail[4:8]
    for k, ref in enumerate(go):
        at = slice((k + 1) * rows, (k + 2) * rows)
        ref[...] = (own[at] + moved[at].astype(F32)).astype(BF)


def back(unit, length, grad):
    inner = jnp.sum(unit * grad, axis=1, keepdims=True)
    return ((grad - unit * inner) / length).astype(BF)


def image_delta_kernel(own, a, b, c, unit, length, out):
    grad = own[...] + a[...].astype(F32) + b[...].astype(F32) + c[...].astype(F32)
    out[...] = back(unit[...], length[...], grad)


def text_kernel(own, a, b, keep, go):
    grad = own[...] + a[...].astype(F32) + b[...].astype(F32)
    rows = keep.shape[0]
    keep[...] = grad[:rows]
    go[...] = grad[rows:].astype(BF)


def text_weight_kernel(params, images, *refs):
    coefs, feats, units, lengths = refs[:3], refs[3:7], refs[7:11], refs[11:15]
    far_up, far_down, pick, *grads, part_keep, part_go = refs[15:]
    half = part_keep.shape[0]
    deltas = []
    for k in range(3):
        grad = params[0] * mm(coefs[k][...], images[...])
        grads[k][...] = grad
        deltas.append(back(units[k][...], lengths[k][...], grad))
    grad = jnp.concatenate([far_up[...], far_down[...]], axis=0).astype(F32)
    deltas.append(back(units[3][...], lengths[3][...], grad))
    delta = jnp.concatenate(deltas, axis=0)
    rows = jnp.concatenate([f[...] for f in feats], axis=0)
    rows = mm(rows, pick[...]).astype(BF)
    part_go[...] = t_mm(rows[:, half:], delta).astype(BF)
    part_keep[...] = t_mm(rows[:, :half], delta)


def weight_kernel(feats, a, b, c, d, part_keep, part_go):
    half = part_keep.shape[0]
    delta = jnp.concatenate([a[...], b[...], c[...], d[...]], axis=0)
    part_go[...] = t_mm(feats[:, half:], delta).astype(BF)
    part_keep[...] = t_mm(feats[:, :half], delta)


def select_kernel(n, *refs):
    feats = jnp.concatenate([r[...] for r in refs[:n]], axis=0)
    refs[n + 1][...] = mm(feats, refs[n][...]).astype(BF)


def select(blocks, pick):
    n, rows = len(blocks), blocks[0].shape[0]
    out = [((n * rows, pick.shape[1]), BF)]
    return call(functools.partial(select_kernel, n), out, [*blocks, pick])[0]


def feature_grad_kernel(delta, weight, out):
    out[...] = mm_t(delta[...], weight[...]).astype(BF)


def text_quarter_kernel(own, a, b, c, loss, keep, *go):
    total = own[...] + a[...].astype(F32) + b[...].astype(F32) + c[...].astype(F32)
    cut, width = keep.shape
    keep[...] = total[:cut]
    for k, ref in enumerate(go):
        part = total[(k + 1) * cut : (k + 2) * cut]
        fill = jnp.zeros((ref.shape[0] - 16 - cut, width), F32)
        tail = two_parts(loss[3 - k : 4 - k], width).astype(F32)
        ref[...] = jnp.concatenate([part, fill, tail], axis=0).astype(BF)


def tail_kernel(img, i1, i2, i3, txt, t1, t2, t3, loss, keep, loss_out, *go):
    total_i, total_t, losses = img[...], txt[...], loss[0:1]
    rows, cut = losses.shape[1], total_t.shape[0]
    for ref in (i1, i2, i3):
        total_i = total_i + ref[...].astype(F32)
    for ref in (t1, t2, t3):
        moved = ref[...].astype(F32)
        total_t = total_t + moved[:cut]
        tail = moved[moved.shape[0] - 16 :, :rows]
        losses = losses + tail[0:1] + tail[1:2]
    loss_out[...] = losses / rows
    cut_i, cut_t, width = total_i.shape[0] // 4, cut // 4, total_i.shape[1]
    for k, ref in enumerate((keep, *go)):
        parts = [
            total_i[k * cut_i : (k + 1) * cut_i],
            jnp.zeros((16 - cut_i, width), F32),
            total_t[k * cut_t : (k + 1) * cut_t],
            jnp.zeros((16 - cut_t, width), F32),
        ]
        ref[...] = jnp.concatenate(parts, axis=0).astype(ref.dtype)


def last_kernel(keep, a, b, c, out_i, out_t):
    total = keep[...] + a[...].astype(F32) + b[...].astype(F32) + c[...].astype(F32)
    out_i[...] = total[: out_i.shape[0]]
    out_t[...] = total[16 : 16 + out_t.shape[0]]


def across(value, distance):
    pairs = [(i, i ^ distance) for i in range(4)]
    return lax.ppermute(value, ("xh", "xl"), pairs)


def selection(depth, cut, steps):
    names = ("c", "xh", "xl", "y", "z")
    dims = [SIZES[a] if a in steps else 1 for a in names] + [cut]
    away = dict(zip(names + ("row",), (i.reshape(1, -1).astype(np.int32) for i in np.indices(dims))))
    place = 0
    for a in ("xh", "y", "z", "c", "xl"):
        place = place * SIZES[a] + ((lax.axis_index(a) + away[a]) & (SIZES[a] - 1))
    return (jnp.arange(depth)[:, None] == place * cut + away["row"]).astype(BF)


def per_device(image_feats, text_feats, match, w_image, w_text, log_temp, bias):
    img_x, txt_x = image_feats[0], text_feats[0]
    rows, width = img_x.shape[0], w_image.shape[1]
    scale = jnp.exp(log_temp[0])
    params = jnp.stack([scale, bias[0]])

    paired = jnp.concatenate([match[0], jnp.full((1, 7 * rows), -1, jnp.int32)], axis=1)
    cut, cut_img = txt_x.shape[1] // 128, img_x.shape[1] // 128
    txt_pick = selection(txt_x.shape[1], cut, ("c", "z", "y", "xh", "xl"))
    img_pick = selection(img_x.shape[1], cut_img, ("c", "z", "xh", "xl"))

    pair_rows = 2 * rows
    partner = rot(txt_x, "xh", 1)
    img_last, partner = lax.optimization_barrier((img_x, partner))
    img_first, txt_pick = lax.optimization_barrier((img_x, txt_pick))
    img_near = [rot(img_first, "y", 1), rot(img_last, "y", 2), rot(img_first, "y", 3)]
    (pair,) = call(stack_kernel, [((pair_rows, txt_x.shape[1]), BF)], [txt_x, partner])
    before, after = rot(pair, "z", 1), rot(pair, "z", -1)
    far = [rot(before[:rows], "z", 1), rot(after[rows:], "z", -1)]
    unit_0, unit_txt, len_txt = project([pair], w_text, pair_rows, kept=pair_rows)
    *img_near, before, after, paired, unit_0, unit_txt, txt_pick, img_pick = lax.optimization_barrier(
        (*img_near, before, after, paired, unit_0, unit_txt, txt_pick, img_pick)
    )
    (img_mine,) = call(stack_kernel, [((4 * rows, img_x.shape[1]), BF)], [img_x, *img_near])
    img_moved = rot(img_mine, "c", 1)

    sets = [project([before], w_text, pair_rows, kept=pair_rows), None]
    sets.append(project([after], w_text, pair_rows, kept=pair_rows))
    img_moved, sets[0][0], sets[2][0] = lax.optimization_barrier((img_moved, sets[0][0], sets[2][0]))
    images, unit_img, len_img = project([img_mine, img_moved], w_image, pair_rows, kept=rows)
    *far, images = lax.optimization_barrier((*far, images))
    (txt_far,) = call(stack_kernel, [((pair_rows, txt_x.shape[1]), BF)], far)
    sets[1] = project([txt_far], w_text, pair_rows, kept=pair_rows)
    units = [part[0] for part in sets]

    rows_of = [units[0], units[2], unit_0, units[1]]
    coefs, losses = pair_terms(params, images, [units[0], units[2], units[1], unit_0], paired)
    coefs = [coefs[0], coefs[1], coefs[3], coefs[2]]
    other = image_grad(params, coefs, rows_of, 1, BF, [losses])
    own = image_grad(params, coefs, rows_of, 0, F32)

    coef_far, own = lax.optimization_barrier((coefs[3], own))
    far_grad = call(far_kernel, [((rows, width), BF)] * 2, [params, images, coef_far], smem=1)
    up, down = rot(far_grad[0], "z", 1), rot(far_grad[1], "z", -1)
    other, far_first = lax.optimization_barrier((rot(other, "c", 1), far_grad[0]))
    keep, loss, *go = call(
        image_quarter_kernel,
        [((rows, width), F32), ((4, rows), F32)] + [((rows, width), BF)] * 3,
        [own, other, losses],
    )
    img_parts = [rot(go[k - 1], "y", -k) for k in (1, 3, 2)]

    half_t = txt_x.shape[1] // 2
    feats = [before, after, pair, txt_far]
    row_units = [sets[0][1], sets[2][1], unit_txt, sets[1][1]]
    lengths = [sets[0][2], sets[2][2], len_txt, sets[1][2]]
    *near_coefs, keep = lax.optimization_barrier((*coefs[:3], keep))
    *grads, own_txt, part_keep, part_go = call(
        text_weight_kernel,
        [((pair_rows, width), F32)] * 3 + [((half_t, width), F32), ((half_t, width), BF)],
        [params, images, *near_coefs, *feats, *row_units, *lengths, far_first, far_grad[1], txt_pick],
        smem=1,
        flops=LONG,
        mib=40,
    )
    before_go, after_go = call(join_kernel, [((pair_rows, width), BF)] * 2, [*grads, up, down])
    txt_parts = [rot(before_go, "z", -1), rot(after_go, "z", 1)]
    img_parts[0], img_parts[1], img_parts[2], _ = lax.optimization_barrier((*img_parts, before_go))
    (delta_img,) = call(
        image_delta_kernel,
        [((rows, width), BF)],
        [keep, *img_parts, unit_img, len_img],
        flops=LONG,
    )
    gathered = [rot(delta_img, "y", k) for k in (1, 2, 3)]
    keep, *txt_go = quarters(part_keep, rot(part_go, "c", 1), flops=LONG)
    txt_go = [across(txt_go[k - 1], k) for k in (1, 3, 2)]
    own_grad, go_x = call(
        text_kernel, [((rows, width), F32), ((rows, width), BF)], [own_txt, *txt_parts]
    )
    img_feats = select([img_mine], img_pick)
    (grad_image,) = call(
        feature_grad_kernel, [((rows, img_x.shape[1]), BF)], [delta_img, w_image]
    )
    *gathered, txt_go[0], txt_go[1], img_feats, grad_image = lax.optimization_barrier(
        (*gathered, txt_go[0], txt_go[1], img_feats, grad_image)
    )
    half_i = img_feats.shape[1] // 2
    part_keep, part_go = call(
        weight_kernel,
        [((half_i, width), F32), ((half_i, width), BF)],
        [img_feats, delta_img, *gathered],
    )
    keep_i, *go = quarters(part_keep, rot(part_go, "c", 1))
    img_go = [across(go[k - 1], k) for k in (1, 3, 2)]
    cut_y = keep.shape[0] // 4
    txt_go[2], keep_i = lax.optimization_barrier((txt_go[2], keep_i))
    sum_txt, *go = call(
        text_quarter_kernel,
        [((cut_y, width), F32)] + [(((cut_y + 15) // 16 * 16 + 16, width), BF)] * 3,
        [keep, *txt_go, loss],
    )
    txt_go = [rot(go[k - 1], "y", k) for k in (1, 3, 2)]
    moved, *img_go = lax.optimization_barrier((rot(go_x, "xh", 1), *img_go))
    grad_unit_txt = own_grad + moved.astype(F32)
    keep, row_loss, *go = call(
        tail_kernel,
        [((32, width), F32), ((1, rows), F32)] + [((32, width), BF)] * 3,
        [keep_i, *img_go, sum_txt, *txt_go, loss],
    )
    moved = [rot(go[k - 1], "z", k) for k in (1, 3, 2)]
    grad_w_image, grad_w_text = call(
        last_kernel, [((cut_img, width), F32), ((cut, width), F32)], [keep, *moved]
    )

    delta_txt = back(unit_txt[:rows], len_txt[:rows], grad_unit_txt)
    grad_text = mm_t(delta_txt, w_text).astype(BF)[None]
    return (row_loss, grad_image[None], grad_text, grad_w_image, grad_w_text)


def solution(mesh):
    fine = Mesh(mesh.devices.reshape([SIZES[a] for a in AXES]), AXES)
    blk = ("xh", "y", "z", "c")
    in_specs = (
        P("xl", blk, None),
        P("xl", blk, None),
        P("xl", blk, None),
        P(),
        P(),
        P(),
        P(),
    )
    out_specs = (
        P("xl", blk),
        P("xl", blk, None),
        P("xl", blk, None),
        P(AXES, None),
        P(AXES, None),
    )
    return jax.shard_map(
        per_device, mesh=fine, in_specs=in_specs, out_specs=out_specs, check_vma=False
    )
```

```python
import functools

import jax
import jax.numpy as jnp
import numpy as np
from jax import lax
from jax.experimental import pallas as pl
from jax.experimental.pallas import tpu as pltpu
from jax.sharding import Mesh
from jax.sharding import PartitionSpec as P

AXES = ("xh", "y", "z", "c", "xl")
SIZES = {"xh": 2, "y": 4, "z": 4, "c": 2, "xl": 2}
BF = jnp.bfloat16
F32 = jnp.float32
VMEM = pl.BlockSpec(memory_space=pltpu.VMEM)
SMEM = pl.BlockSpec(memory_space=pltpu.SMEM)
MIB = 1 << 20
LONG = 400 * 10**9


def rot(value, axis, steps):
    n = SIZES[axis]
    return lax.ppermute(value, axis, [(i, (i + steps) % n) for i in range(n)])


def mm(a, b):
    return jnp.dot(a, b, preferred_element_type=F32)


def mm_t(a, b):
    return lax.dot_general(a, b, (((1,), (1,)), ((), ())), preferred_element_type=F32)


def t_mm(a, b):
    return lax.dot_general(a, b, (((0,), (0,)), ((), ())), preferred_element_type=F32)


def call(kernel, out, args, smem=0, flops=1024):
    return pl.pallas_call(
        kernel,
        out_shape=[jax.ShapeDtypeStruct(shape, dtype) for shape, dtype in out],
        in_specs=[SMEM] * smem + [VMEM] * (len(args) - smem),
        out_specs=[VMEM] * len(out),
        cost_estimate=pl.CostEstimate(flops=flops, bytes_accessed=1024, transcendentals=0),
        compiler_params=pltpu.CompilerParams(vmem_limit_bytes=16 * MIB),
    )(*args)


def project_kernel(n, step, kept, *refs):
    blocks, w_ref, unit_ref = refs[:n], refs[n], refs[n + 1]
    start = 0
    for block in blocks:

        def part(i, _, block=block, start=start):
            at = pl.multiple_of(i * step, step)
            proj = mm(block[pl.ds(at, step), :], w_ref[...])
            length = jnp.sqrt(jnp.sum(proj * proj, axis=1, keepdims=True) + 1e-06)
            unit = proj / length
            unit_ref[pl.ds(start + at, step), :] = unit.astype(BF)
            if kept and start == 0:

                @pl.when(i == 0)
                def _():
                    refs[n + 2][...] = unit[:kept]
                    refs[n + 3][...] = length[:kept]

            return 0

        lax.fori_loop(0, block.shape[0] // step, part, 0)
        start += block.shape[0]


def project(blocks, weight, step, kept=0):
    n, rows, width = len(blocks), sum(b.shape[0] for b in blocks), weight.shape[1]
    out = [((rows, width), BF)]
    if kept:
        out += [((kept, width), F32), ((kept, 1), F32)]
    return list(call(functools.partial(project_kernel, n, step, kept), out, [*blocks, weight]))


def stack_kernel(*refs):
    rows = refs[0].shape[0]
    for k, ref in enumerate(refs[:-1]):
        refs[-1][k * rows : (k + 1) * rows, :] = ref[...]


def pair_kernel(n, first, split, *refs):
    params, images = refs[0], refs[1]
    units, at = refs[2 : 2 + n], 2 + n
    if first:
        paired = refs[at]
        at += 1
    coefs, loss_ref, grads = refs[at : at + n], refs[at + n], refs[at + n + 1 :]
    scale, offset = params[0], params[1]
    step = images.shape[0] // 4
    for k in range(n):
        own = first and k == n - 1

        def tile(j, _, k=k, own=own):
            at = pl.multiple_of(j * step, step)
            cols = pl.ds(at, step)
            margin = scale * mm_t(units[k][...], images[cols, :]) + offset
            if own:
                place = lax.broadcasted_iota(jnp.int32, margin.shape, 0)
                positive = place == paired[:, cols]
                margin = jnp.where(positive, -margin, margin)
            power = jnp.exp(margin)
            whole = 1.0 + power
            near = power * (1.0 - power * (0.5 - power * (1.0 / 3.0)))
            terms = jnp.where(power < 0.01, near, jnp.log(whole))
            turn = pl.reciprocal(whole, approx=True)
            coeff = power * (turn * (2.0 - whole * turn))
            if own:
                coeff = jnp.where(positive, -coeff, coeff)
            part = jnp.sum(terms, axis=0, keepdims=True)
            loss_ref[:, cols] = part if k == 0 else loss_ref[:, cols] + part
            coefs[k][:, cols] = coeff.astype(BF)
            return 0

        lax.fori_loop(0, 4, tile, 0)
    if split:
        grad = scale * mm(coefs[0][...], images[...])
        cut = grad.shape[0] // 2
        grads[0][...] = grad[:cut].astype(BF)
        grads[1][...] = grad[cut:].astype(BF)


def pair_terms(params, images, units, paired=None, split=False):
    n, (rows, width), total = len(units), units[0].shape, images.shape[0]
    first = paired is not None
    grads = [((rows // 2, width), BF)] * 2 if split else []
    out = [((rows, total), BF)] * n + [((1, total), F32)] + grads
    args = [params, images, *units] + ([paired] if first else [])
    res = call(functools.partial(pair_kernel, n, first, split), out, args, smem=1)
    return res[:n], res[n], list(res[n + 1 :])


def text_grad_kernel(n, *refs):
    params, images, coefs, grads = refs[0], refs[1], refs[2 : 2 + n], refs[2 + n :]
    for coef, grad in zip(coefs, grads):
        grad[...] = params[0] * mm(coef[...], images[...])


def text_grads(params, images, coefs):
    n, out = len(coefs), ((coefs[0].shape[0], images.shape[1]), F32)
    args = [params, images, *coefs]
    return call(functools.partial(text_grad_kernel, n), [out] * n, args, smem=1, flops=LONG)


def join_kernel(before, after, up, down, before_out, after_out):
    cut = up.shape[0]
    before_out[:cut] = before[:cut].astype(BF)
    before_out[cut:] = (before[cut:] + down[...].astype(F32)).astype(BF)
    after_out[:cut] = (after[:cut] + up[...].astype(F32)).astype(BF)
    after_out[cut:] = after[cut:].astype(BF)


def loss_rows(losses, at, rows):
    return jnp.concatenate([losses[:, at + k * rows : at + (k + 1) * rows] for k in range(4)], axis=0)


def two_parts(value, width):
    high = value.astype(BF)
    low = (value - high.astype(F32)).astype(BF)
    parts = jnp.concatenate([high, low], axis=0).astype(F32)
    down = jnp.zeros((16 - parts.shape[0], parts.shape[1]), F32)
    parts = jnp.concatenate([parts, down], axis=0)
    right = jnp.zeros((16, width - parts.shape[1]), F32)
    return jnp.concatenate([parts, right], axis=1).astype(BF)


def image_kernel(n, half, *refs):
    params, coefs, units = refs[0], refs[1 : 1 + n], refs[1 + n : 1 + 2 * n]
    *losses, out_ref = refs[1 + 2 * n :]
    total, width = coefs[0].shape[1], units[0].shape[1]
    tile = total // 4
    for j in range(2):
        cols = slice((2 * half + j) * tile, (2 * half + j + 1) * tile)
        grad = t_mm(coefs[0][:, cols], units[0][...])
        for k in range(1, n):
            grad = grad + t_mm(coefs[k][:, cols], units[k][...])
        out_ref[j * tile : (j + 1) * tile, :] = (params[0] * grad).astype(out_ref.dtype)
    if losses:
        rows = total // 8
        tail = loss_rows(losses[0][...] + losses[1][...], total // 2, rows)
        out_ref[2 * tile :, :] = two_parts(tail, width)


def image_grad(params, coefs, units, half, dtype, losses=()):
    n, total, width = len(coefs), coefs[0].shape[1], units[0].shape[1]
    out = [((total // 2 + (16 if losses else 0), width), dtype)]
    args = [params, *coefs, *units, *losses]
    flops = 1024 if losses else LONG
    return call(functools.partial(image_kernel, n, half), out, args, smem=1, flops=flops)[0]


def quarter_kernel(own, moved, keep, *go):
    cut = keep.shape[0]
    keep[...] = own[:cut] + moved[:cut].astype(F32)
    for k, ref in enumerate(go):
        at = slice((k + 1) * cut, (k + 2) * cut)
        ref[...] = (own[at] + moved[at].astype(F32)).astype(BF)


def quarters(own, moved):
    cut, width = own.shape[0] // 4, own.shape[1]
    return call(quarter_kernel, [((cut, width), F32)] + [((cut, width), BF)] * 3, [own, moved])


def image_quarter_kernel(own, moved, loss_a, loss_b, keep, loss_out, *go):
    rows = keep.shape[0]
    keep[...] = own[:rows] + moved[:rows].astype(F32)
    tail = moved[own.shape[0] :, :rows].astype(F32)
    loss_out[...] = loss_rows(loss_a[...] + loss_b[...], 0, rows) + tail[0:4] + tail[4:8]
    for k, ref in enumerate(go):
        at = slice((k + 1) * rows, (k + 2) * rows)
        ref[...] = (own[at] + moved[at].astype(F32)).astype(BF)


def back(unit, length, grad):
    inner = jnp.sum(unit * grad, axis=1, keepdims=True)
    return ((grad - unit * inner) / length).astype(BF)


def image_delta_kernel(own, a, b, c, unit, length, out):
    grad = own[...] + a[...].astype(F32) + b[...].astype(F32) + c[...].astype(F32)
    out[...] = back(unit[...], length[...], grad)


def text_kernel(own, a, b, keep, go):
    grad = own[...] + a[...].astype(F32) + b[...].astype(F32)
    rows = keep.shape[0]
    keep[...] = grad[:rows]
    go[...] = grad[rows:].astype(BF)


def text_weight_kernel(n, *refs):
    pick, part_keep, part_go = refs[-3:]
    half = part_keep.shape[0]
    feats, units, lengths, grads = refs[:n], refs[n : 2 * n], refs[2 * n : 3 * n], refs[3 * n : -3]
    deltas = []
    for k in range(n):
        grad = grads[k][...] if k < n - 1 else jnp.concatenate([g[...] for g in grads[k:]], axis=0)
        deltas.append(back(units[k][...], lengths[k][...], grad.astype(F32)))
    delta = jnp.concatenate(deltas, axis=0)
    feats = jnp.concatenate([f[...] for f in feats], axis=0)
    feats = mm(feats, pick[...]).astype(BF)
    part_go[...] = t_mm(feats[:, half:], delta).astype(BF)
    part_keep[...] = t_mm(feats[:, :half], delta)


def weight_kernel(feats, a, b, c, d, part_keep, part_go):
    half = part_keep.shape[0]
    delta = jnp.concatenate([a[...], b[...], c[...], d[...]], axis=0)
    part_go[...] = t_mm(feats[:, half:], delta).astype(BF)
    part_keep[...] = t_mm(feats[:, :half], delta)


def select_kernel(n, *refs):
    feats = jnp.concatenate([r[...] for r in refs[:n]], axis=0)
    refs[n + 1][...] = mm(feats, refs[n][...]).astype(BF)


def select(blocks, pick):
    n, rows = len(blocks), blocks[0].shape[0]
    out = [((n * rows, pick.shape[1]), BF)]
    return call(functools.partial(select_kernel, n), out, [*blocks, pick])[0]


def feature_grad_kernel(delta, weight, out):
    out[...] = mm_t(delta[...], weight[...]).astype(BF)


def text_quarter_kernel(own, a, b, c, loss, keep, *go):
    total = own[...] + a[...].astype(F32) + b[...].astype(F32) + c[...].astype(F32)
    cut, width = keep.shape
    keep[...] = total[:cut]
    for k, ref in enumerate(go):
        part = total[(k + 1) * cut : (k + 2) * cut]
        fill = jnp.zeros((ref.shape[0] - 16 - cut, width), F32)
        tail = two_parts(loss[3 - k : 4 - k], width).astype(F32)
        ref[...] = jnp.concatenate([part, fill, tail], axis=0).astype(BF)


def tail_kernel(img, i1, i2, i3, txt, t1, t2, t3, loss, keep, loss_out, *go):
    total_i, total_t, losses = img[...], txt[...], loss[0:1]
    rows, cut = losses.shape[1], total_t.shape[0]
    for ref in (i1, i2, i3):
        total_i = total_i + ref[...].astype(F32)
    for ref in (t1, t2, t3):
        moved = ref[...].astype(F32)
        total_t = total_t + moved[:cut]
        tail = moved[moved.shape[0] - 16 :, :rows]
        losses = losses + tail[0:1] + tail[1:2]
    loss_out[...] = losses / rows
    cut_i, cut_t, width = total_i.shape[0] // 4, cut // 4, total_i.shape[1]
    for k, ref in enumerate((keep, *go)):
        parts = [
            total_i[k * cut_i : (k + 1) * cut_i],
            jnp.zeros((16 - cut_i, width), F32),
            total_t[k * cut_t : (k + 1) * cut_t],
            jnp.zeros((16 - cut_t, width), F32),
        ]
        ref[...] = jnp.concatenate(parts, axis=0).astype(ref.dtype)


def last_kernel(keep, a, b, c, out_i, out_t):
    total = keep[...] + a[...].astype(F32) + b[...].astype(F32) + c[...].astype(F32)
    out_i[...] = total[: out_i.shape[0]]
    out_t[...] = total[16 : 16 + out_t.shape[0]]


def selection(depth, cut, steps):
    names = ("c", "z", "y", "xh", "xl")
    dims = [SIZES[a] if a in steps else 1 for a in names] + [cut]
    away = dict(zip(names + ("row",), (i.reshape(1, -1).astype(np.int32) for i in np.indices(dims))))
    place = 0
    for a in ("xh", "y", "z", "c", "xl"):
        place = place * SIZES[a] + ((lax.axis_index(a) + away[a]) & (SIZES[a] - 1))
    return (jnp.arange(depth)[:, None] == place * cut + away["row"]).astype(BF)


def per_device(image_feats, text_feats, match, w_image, w_text, log_temp, bias):
    img_x, txt_x = image_feats[0], text_feats[0]
    rows, width = img_x.shape[0], w_image.shape[1]
    scale = jnp.exp(log_temp[0])
    params = jnp.stack([scale, bias[0]])

    paired = jnp.concatenate([match[0], jnp.full((1, 7 * rows), -1, jnp.int32)], axis=1)
    cut, cut_img = txt_x.shape[1] // 128, img_x.shape[1] // 128
    txt_pick = selection(txt_x.shape[1], cut, ("c", "z", "y", "xh", "xl"))
    img_pick = selection(img_x.shape[1], cut_img, ("c", "z", "xh", "xl"))

    pair_rows = 2 * rows
    partner = rot(txt_x, "xh", 1)
    img_last, partner = lax.optimization_barrier((img_x, partner))
    img_first, txt_pick = lax.optimization_barrier((img_x, txt_pick))
    img_near = [rot(img_first, "y", 1), rot(img_last, "y", 2), rot(img_first, "y", 3)]
    (pair,) = call(stack_kernel, [((pair_rows, txt_x.shape[1]), BF)], [txt_x, partner])
    before, after = rot(pair, "z", 1), rot(pair, "z", -1)
    far = [rot(before[:rows], "z", 1), rot(after[rows:], "z", -1)]
    unit_0, unit_txt, len_txt = project([pair], w_text, pair_rows, kept=pair_rows)
    *img_near, before, after, paired, unit_0, unit_txt, txt_pick, img_pick = lax.optimization_barrier(
        (*img_near, before, after, paired, unit_0, unit_txt, txt_pick, img_pick)
    )
    (img_mine,) = call(stack_kernel, [((4 * rows, img_x.shape[1]), BF)], [img_x, *img_near])
    img_moved = rot(img_mine, "c", 1)

    sets = [project([before], w_text, pair_rows, kept=pair_rows), None]
    sets.append(project([after], w_text, pair_rows, kept=pair_rows))
    img_moved, sets[0][0], sets[2][0] = lax.optimization_barrier((img_moved, sets[0][0], sets[2][0]))
    images, unit_img, len_img = project([img_mine, img_moved], w_image, pair_rows, kept=rows)
    *far, images = lax.optimization_barrier((*far, images))
    (txt_far,) = call(stack_kernel, [((pair_rows, txt_x.shape[1]), BF)], far)
    sets[1] = project([txt_far], w_text, pair_rows, kept=pair_rows)
    units = [part[0] for part in sets]

    coefs_b, loss_b, far_grad = pair_terms(params, images, [units[1]], split=True)
    far = [rot(far_grad[0], "z", 1), rot(far_grad[1], "z", -1)]
    coefs_a, loss_a, _ = pair_terms(params, images, [units[0], units[2], unit_0], paired)
    losses = [loss_a, loss_b]
    coefs, rows_of = [*coefs_a, *coefs_b], [units[0], units[2], unit_0, units[1]]
    other = image_grad(params, coefs, rows_of, 1, BF, losses)
    own = image_grad(params, coefs, rows_of, 0, F32)

    keep, loss, *go = call(
        image_quarter_kernel,
        [((rows, width), F32), ((4, rows), F32)] + [((rows, width), BF)] * 3,
        [own, rot(other, "c", 1), *losses],
    )
    img_parts = [rot(go[k - 1], "y", -k) for k in (1, 3, 2)]
    *coefs_a, keep = lax.optimization_barrier((*coefs_a, keep))
    *grads, own_txt = text_grads(params, images, coefs_a)
    up, down, keep = lax.optimization_barrier((*far, keep))
    before_go, after_go = call(join_kernel, [((pair_rows, width), BF)] * 2, [*grads, up, down])
    txt_parts = [rot(before_go, "z", -1), rot(after_go, "z", 1)]

    half_t = txt_x.shape[1] // 2
    feats = [pair, before, after, txt_far]
    row_units = [unit_txt, sets[0][1], sets[2][1], sets[1][1]]
    lengths = [len_txt, sets[0][2], sets[2][2], sets[1][2]]
    far_grad[0], _ = lax.optimization_barrier((far_grad[0], before_go))
    part_keep, part_go = call(
        functools.partial(text_weight_kernel, 4),
        [((half_t, width), F32), ((half_t, width), BF)],
        [*feats, *row_units, *lengths, own_txt, *grads, *far_grad, txt_pick],
    )
    img_parts[0], img_parts[1], img_parts[2], part_keep = lax.optimization_barrier((*img_parts, part_keep))
    (delta_img,) = call(
        image_delta_kernel,
        [((rows, width), BF)],
        [keep, *img_parts, unit_img, len_img],
        flops=LONG,
    )
    gathered = [rot(delta_img, "y", k) for k in (1, 2, 3)]
    keep, *txt_go = quarters(part_keep, rot(part_go, "c", 1))
    txt_go = [rot(txt_go[k - 1], "z", k) for k in (1, 3, 2)]
    own_grad, go_x = call(
        text_kernel, [((rows, width), F32), ((rows, width), BF)], [own_txt, *txt_parts]
    )
    img_feats = select([img_mine], img_pick)
    (grad_image,) = call(
        feature_grad_kernel, [((rows, img_x.shape[1]), BF)], [delta_img, w_image]
    )
    *gathered, txt_go[0], txt_go[1], moved, img_feats, grad_image = lax.optimization_barrier(
        (*gathered, txt_go[0], txt_go[1], rot(go_x, "xh", 1), img_feats, grad_image)
    )
    grad_unit_txt = own_grad + moved.astype(F32)
    half_i = img_feats.shape[1] // 2
    part_keep, part_go = call(
        weight_kernel,
        [((half_i, width), F32), ((half_i, width), BF)],
        [img_feats, delta_img, *gathered],
    )
    keep_i, *go = quarters(part_keep, rot(part_go, "c", 1))
    img_go = [rot(go[k - 1], "z", k) for k in (1, 3, 2)]
    cut_y = keep.shape[0] // 4
    sum_txt, *go = call(
        text_quarter_kernel,
        [((cut_y, width), F32)] + [(((cut_y + 15) // 16 * 16 + 16, width), BF)] * 3,
        [keep, *txt_go, loss],
    )
    txt_go = [rot(go[k - 1], "y", k) for k in (1, 3, 2)]
    keep, row_loss, *go = call(
        tail_kernel,
        [((32, width), F32), ((1, rows), F32)] + [((32, width), BF)] * 3,
        [keep_i, *img_go, sum_txt, *txt_go, loss],
    )
    moved = []
    for dh, dl in ((0, 1), (1, 0), (1, 1)):
        pairs = [(h * 2 + l, ((h + dh) % 2) * 2 + (l + dl) % 2) for h in (0, 1) for l in (0, 1)]
        moved.append(lax.ppermute(go[2 * dh + dl - 1], ("xh", "xl"), pairs))
    grad_w_image, grad_w_text = call(
        last_kernel, [((cut_img, width), F32), ((cut, width), F32)], [keep, *moved]
    )

    delta_txt = back(unit_txt[:rows], len_txt[:rows], grad_unit_txt)
    grad_text = mm_t(delta_txt, w_text).astype(BF)[None]
    return (row_loss, grad_image[None], grad_text, grad_w_image, grad_w_text)


def solution(mesh):
    fine = Mesh(mesh.devices.reshape([SIZES[a] for a in AXES]), AXES)
    blk = ("xh", "y", "z", "c")
    in_specs = (
        P("xl", blk, None),
        P("xl", blk, None),
        P("xl", blk, None),
        P(),
        P(),
        P(),
        P(),
    )
    out_specs = (
        P("xl", blk),
        P("xl", blk, None),
        P("xl", blk, None),
        P(AXES, None),
        P(AXES, None),
    )
    return jax.shard_map(
        per_device, mesh=fine, in_specs=in_specs, out_specs=out_specs, check_vma=False
    )
```

```python
import functools

import jax
import jax.numpy as jnp
import numpy as np
from jax import lax
from jax.experimental import pallas as pl
from jax.experimental.pallas import tpu as pltpu
from jax.sharding import Mesh
from jax.sharding import PartitionSpec as P

AXES = ("xh", "y", "z", "c", "xl")
SIZES = {"xh": 2, "y": 4, "z": 4, "c": 2, "xl": 2}
BF = jnp.bfloat16
F32 = jnp.float32
VMEM = pl.BlockSpec(memory_space=pltpu.VMEM)
SMEM = pl.BlockSpec(memory_space=pltpu.SMEM)
MIB = 1 << 20
LONG = 400 * 10**9


def rot(value, axis, steps):
    n = SIZES[axis]
    return lax.ppermute(value, axis, [(i, (i + steps) % n) for i in range(n)])


def mm(a, b):
    return jnp.dot(a, b, preferred_element_type=F32)


def mm_t(a, b):
    return lax.dot_general(a, b, (((1,), (1,)), ((), ())), preferred_element_type=F32)


def t_mm(a, b):
    return lax.dot_general(a, b, (((0,), (0,)), ((), ())), preferred_element_type=F32)


def call(kernel, out, args, smem=0, flops=1024):
    return pl.pallas_call(
        kernel,
        out_shape=[jax.ShapeDtypeStruct(shape, dtype) for shape, dtype in out],
        in_specs=[SMEM] * smem + [VMEM] * (len(args) - smem),
        out_specs=[VMEM] * len(out),
        cost_estimate=pl.CostEstimate(flops=flops, bytes_accessed=1024, transcendentals=0),
        compiler_params=pltpu.CompilerParams(vmem_limit_bytes=16 * MIB),
    )(*args)


def project_kernel(n, step, kept, *refs):
    blocks, w_ref, unit_ref = refs[:n], refs[n], refs[n + 1]
    feats = jnp.concatenate([b[...] for b in blocks], axis=0)
    for at in range(0, feats.shape[0], step):
        proj = mm(feats[at : at + step], w_ref[...])
        length = jnp.sqrt(jnp.sum(proj * proj, axis=1, keepdims=True) + 1e-06)
        unit = proj / length
        unit_ref[at : at + step, :] = unit.astype(BF)
        if at == 0 and kept:
            refs[n + 2][...] = unit[:kept]
            refs[n + 3][...] = length[:kept]


def project(blocks, weight, step, kept=0):
    n, rows, width = len(blocks), sum(b.shape[0] for b in blocks), weight.shape[1]
    out = [((rows, width), BF)]
    if kept:
        out += [((kept, width), F32), ((kept, 1), F32)]
    return list(call(functools.partial(project_kernel, n, step, kept), out, [*blocks, weight]))


def stack_kernel(*refs):
    rows = refs[0].shape[0]
    for k, ref in enumerate(refs[:-1]):
        refs[-1][k * rows : (k + 1) * rows, :] = ref[...]


def pair_kernel(n, first, split, *refs):
    params, images = refs[0], refs[1]
    units, at = refs[2 : 2 + n], 2 + n
    if first:
        paired = refs[at]
        at += 1
    coefs, loss_ref, grads = refs[at : at + n], refs[at + n], refs[at + n + 1 :]
    scale, offset = params[0], params[1]
    step = images.shape[0] // 4
    for k in range(n):
        own = first and k == n - 1
        for j in range(4):
            cols = slice(j * step, (j + 1) * step)
            margin = scale * mm_t(units[k][...], images[cols, :]) + offset
            if own:
                place = lax.broadcasted_iota(jnp.int32, margin.shape, 0)
                positive = place == paired[:, cols]
                margin = jnp.where(positive, -margin, margin)
            power = jnp.exp(margin)
            whole = 1.0 + power
            near = power * (1.0 - power * (0.5 - power * (1.0 / 3.0)))
            terms = jnp.where(power < 0.01, near, jnp.log(whole))
            turn = pl.reciprocal(whole, approx=True)
            coeff = power * (turn * (2.0 - whole * turn))
            if own:
                coeff = jnp.where(positive, -coeff, coeff)
            part = jnp.sum(terms, axis=0, keepdims=True)
            loss_ref[:, cols] = part if k == 0 else loss_ref[:, cols] + part
            coefs[k][:, cols] = coeff.astype(BF)
    if split:
        grad = scale * mm(coefs[0][...], images[...])
        cut = grad.shape[0] // 2
        grads[0][...] = grad[:cut].astype(BF)
        grads[1][...] = grad[cut:].astype(BF)


def pair_terms(params, images, units, paired=None, split=False):
    n, (rows, width), total = len(units), units[0].shape, images.shape[0]
    first = paired is not None
    grads = [((rows // 2, width), BF)] * 2 if split else []
    out = [((rows, total), BF)] * n + [((1, total), F32)] + grads
    args = [params, images, *units] + ([paired] if first else [])
    res = call(functools.partial(pair_kernel, n, first, split), out, args, smem=1)
    return res[:n], res[n], list(res[n + 1 :])


def text_grad_kernel(n, *refs):
    params, images, coefs, grads = refs[0], refs[1], refs[2 : 2 + n], refs[2 + n :]
    for coef, grad in zip(coefs, grads):
        grad[...] = params[0] * mm(coef[...], images[...])


def text_grads(params, images, coefs):
    n, out = len(coefs), ((coefs[0].shape[0], images.shape[1]), F32)
    args = [params, images, *coefs]
    return call(functools.partial(text_grad_kernel, n), [out] * n, args, smem=1, flops=LONG)


def join_kernel(before, after, up, down, before_out, after_out):
    cut = up.shape[0]
    before_out[:cut] = before[:cut].astype(BF)
    before_out[cut:] = (before[cut:] + down[...].astype(F32)).astype(BF)
    after_out[:cut] = (after[:cut] + up[...].astype(F32)).astype(BF)
    after_out[cut:] = after[cut:].astype(BF)


def loss_rows(losses, at, rows):
    return jnp.concatenate([losses[:, at + k * rows : at + (k + 1) * rows] for k in range(4)], axis=0)


def two_parts(value, width):
    high = value.astype(BF)
    low = (value - high.astype(F32)).astype(BF)
    parts = jnp.concatenate([high, low], axis=0).astype(F32)
    down = jnp.zeros((16 - parts.shape[0], parts.shape[1]), F32)
    parts = jnp.concatenate([parts, down], axis=0)
    right = jnp.zeros((16, width - parts.shape[1]), F32)
    return jnp.concatenate([parts, right], axis=1).astype(BF)


def image_kernel(n, half, *refs):
    params, coefs, units = refs[0], refs[1 : 1 + n], refs[1 + n : 1 + 2 * n]
    *losses, out_ref = refs[1 + 2 * n :]
    total, width = coefs[0].shape[1], units[0].shape[1]
    tile = total // 4
    for j in range(2):
        cols = slice((2 * half + j) * tile, (2 * half + j + 1) * tile)
        grad = t_mm(coefs[0][:, cols], units[0][...])
        for k in range(1, n):
            grad = grad + t_mm(coefs[k][:, cols], units[k][...])
        out_ref[j * tile : (j + 1) * tile, :] = (params[0] * grad).astype(out_ref.dtype)
    if losses:
        rows = total // 8
        tail = loss_rows(losses[0][...] + losses[1][...], total // 2, rows)
        out_ref[2 * tile :, :] = two_parts(tail, width)


def image_grad(params, coefs, units, half, dtype, losses=()):
    n, total, width = len(coefs), coefs[0].shape[1], units[0].shape[1]
    out = [((total // 2 + (16 if losses else 0), width), dtype)]
    args = [params, *coefs, *units, *losses]
    flops = 1024 if losses else LONG
    return call(functools.partial(image_kernel, n, half), out, args, smem=1, flops=flops)[0]


def quarter_kernel(own, moved, keep, *go):
    cut = keep.shape[0]
    keep[...] = own[:cut] + moved[:cut].astype(F32)
    for k, ref in enumerate(go):
        at = slice((k + 1) * cut, (k + 2) * cut)
        ref[...] = (own[at] + moved[at].astype(F32)).astype(BF)


def quarters(own, moved):
    cut, width = own.shape[0] // 4, own.shape[1]
    return call(quarter_kernel, [((cut, width), F32)] + [((cut, width), BF)] * 3, [own, moved])


def image_quarter_kernel(own, moved, loss_a, loss_b, keep, loss_out, *go):
    rows = keep.shape[0]
    keep[...] = own[:rows] + moved[:rows].astype(F32)
    tail = moved[own.shape[0] :, :rows].astype(F32)
    loss_out[...] = loss_rows(loss_a[...] + loss_b[...], 0, rows) + tail[0:4] + tail[4:8]
    for k, ref in enumerate(go):
        at = slice((k + 1) * rows, (k + 2) * rows)
        ref[...] = (own[at] + moved[at].astype(F32)).astype(BF)


def back(unit, length, grad):
    inner = jnp.sum(unit * grad, axis=1, keepdims=True)
    return ((grad - unit * inner) / length).astype(BF)


def image_delta_kernel(own, a, b, c, unit, length, out):
    grad = own[...] + a[...].astype(F32) + b[...].astype(F32) + c[...].astype(F32)
    out[...] = back(unit[...], length[...], grad)


def text_kernel(own, a, b, keep, go):
    grad = own[...] + a[...].astype(F32) + b[...].astype(F32)
    rows = keep.shape[0]
    keep[...] = grad[:rows]
    go[...] = grad[rows:].astype(BF)


def text_weight_kernel(n, *refs):
    pick, part_keep, part_go = refs[-3:]
    half = part_keep.shape[0]
    feats, units, lengths, grads = refs[:n], refs[n : 2 * n], refs[2 * n : 3 * n], refs[3 * n : -3]
    deltas = []
    for k in range(n):
        grad = grads[k][...] if k < n - 1 else jnp.concatenate([g[...] for g in grads[k:]], axis=0)
        deltas.append(back(units[k][...], lengths[k][...], grad.astype(F32)))
    delta = jnp.concatenate(deltas, axis=0)
    feats = jnp.concatenate([f[...] for f in feats], axis=0)
    feats = mm(feats, pick[...]).astype(BF)
    part_go[...] = t_mm(feats[:, half:], delta).astype(BF)
    part_keep[...] = t_mm(feats[:, :half], delta)


def weight_kernel(feats, a, b, c, d, e, part_keep, part_go):
    half = part_keep.shape[0]
    delta = jnp.concatenate([a[...], b[...], c[...], d[...], e[...]], axis=0)
    part_go[...] = t_mm(feats[:, half:], delta).astype(BF)
    part_keep[...] = t_mm(feats[:, :half], delta)


def select_kernel(n, *refs):
    feats = jnp.concatenate([r[...] for r in refs[:n]], axis=0)
    refs[n + 1][...] = mm(feats, refs[n][...]).astype(BF)


def select(blocks, pick):
    n, rows = len(blocks), blocks[0].shape[0]
    out = [((n * rows, pick.shape[1]), BF)]
    return call(functools.partial(select_kernel, n), out, [*blocks, pick])[0]


def feature_grad_kernel(delta, weight, out):
    out[...] = mm_t(delta[...], weight[...]).astype(BF)


def text_quarter_kernel(own, a, b, c, loss, keep, *go):
    total = own[...] + a[...].astype(F32) + b[...].astype(F32) + c[...].astype(F32)
    cut, width = keep.shape
    keep[...] = total[:cut]
    for k, ref in enumerate(go):
        part = total[(k + 1) * cut : (k + 2) * cut]
        fill = jnp.zeros((ref.shape[0] - 16 - cut, width), F32)
        tail = two_parts(loss[3 - k : 4 - k], width).astype(F32)
        ref[...] = jnp.concatenate([part, fill, tail], axis=0).astype(BF)


def tail_kernel(img, i1, i2, i3, txt, t1, t2, t3, loss, keep, loss_out, *go):
    total_i, total_t, losses = img[...], txt[...], loss[0:1]
    rows, cut = losses.shape[1], total_t.shape[0]
    for ref in (i1, i2, i3):
        total_i = total_i + ref[...].astype(F32)
    for ref in (t1, t2, t3):
        moved = ref[...].astype(F32)
        total_t = total_t + moved[:cut]
        tail = moved[moved.shape[0] - 16 :, :rows]
        losses = losses + tail[0:1] + tail[1:2]
    loss_out[...] = losses / rows
    cut_i, cut_t, width = total_i.shape[0] // 4, cut // 4, total_i.shape[1]
    for k, ref in enumerate((keep, *go)):
        parts = [
            total_i[k * cut_i : (k + 1) * cut_i],
            jnp.zeros((16 - cut_i, width), F32),
            total_t[k * cut_t : (k + 1) * cut_t],
            jnp.zeros((16 - cut_t, width), F32),
        ]
        ref[...] = jnp.concatenate(parts, axis=0).astype(ref.dtype)


def last_kernel(keep, a, b, c, out_i, out_t):
    total = keep[...] + a[...].astype(F32) + b[...].astype(F32) + c[...].astype(F32)
    out_i[...] = total[: out_i.shape[0]]
    out_t[...] = total[16 : 16 + out_t.shape[0]]


def selection(depth, cut, steps):
    names = ("c", "z", "y", "xh", "xl")
    dims = [SIZES[a] if a in steps else 1 for a in names] + [cut]
    away = dict(zip(names + ("row",), (i.reshape(1, -1).astype(np.int32) for i in np.indices(dims))))
    place = 0
    for a in ("xh", "y", "z", "c", "xl"):
        place = place * SIZES[a] + ((lax.axis_index(a) + away[a]) & (SIZES[a] - 1))
    return (jnp.arange(depth)[:, None] == place * cut + away["row"]).astype(BF)


def per_device(image_feats, text_feats, match, w_image, w_text, log_temp, bias):
    img_x, txt_x = image_feats[0], text_feats[0]
    rows, width = img_x.shape[0], w_image.shape[1]
    scale = jnp.exp(log_temp[0])
    params = jnp.stack([scale, bias[0]])

    paired = jnp.concatenate([match[0], jnp.full((1, 7 * rows), -1, jnp.int32)], axis=1)
    cut, cut_img = txt_x.shape[1] // 128, img_x.shape[1] // 128
    txt_pick = selection(txt_x.shape[1], cut, ("c", "z", "y", "xh", "xl"))
    img_pick = selection(img_x.shape[1], cut_img, ("c", "z", "xh", "xl"))

    pair_rows = 2 * rows
    partner = rot(txt_x, "xh", 1)
    img_last, partner = lax.optimization_barrier((img_x, partner))
    img_first, txt_pick = lax.optimization_barrier((img_x, txt_pick))
    img_near = [rot(img_first, "y", 1), rot(img_last, "y", 2), rot(img_first, "y", 3)]
    (pair,) = call(stack_kernel, [((pair_rows, txt_x.shape[1]), BF)], [txt_x, partner])
    before, after = rot(pair, "z", 1), rot(pair, "z", -1)
    far = [rot(before[:rows], "z", 1), rot(after[rows:], "z", -1)]
    unit_0, unit_txt, len_txt = project([pair], w_text, pair_rows, kept=pair_rows)
    *img_near, before, after, paired, unit_0, unit_txt, txt_pick, img_pick = lax.optimization_barrier(
        (*img_near, before, after, paired, unit_0, unit_txt, txt_pick, img_pick)
    )
    (img_mine,) = call(stack_kernel, [((4 * rows, img_x.shape[1]), BF)], [img_x, *img_near])
    img_moved = rot(img_mine, "c", 1)

    sets = [project([before], w_text, pair_rows, kept=pair_rows), None]
    sets.append(project([after], w_text, pair_rows, kept=pair_rows))
    img_moved, sets[0][0], sets[2][0] = lax.optimization_barrier((img_moved, sets[0][0], sets[2][0]))
    images, unit_img, len_img = project([img_mine, img_moved], w_image, pair_rows, kept=rows)
    *far, images = lax.optimization_barrier((*far, images))
    (txt_far,) = call(stack_kernel, [((pair_rows, txt_x.shape[1]), BF)], far)
    sets[1] = project([txt_far], w_text, pair_rows, kept=pair_rows)
    units = [part[0] for part in sets]

    coefs_b, loss_b, far_grad = pair_terms(params, images, [units[1]], split=True)
    far = [rot(far_grad[0], "z", 1), rot(far_grad[1], "z", -1)]
    coefs_a, loss_a, _ = pair_terms(params, images, [units[0], units[2], unit_0], paired)
    losses = [loss_a, loss_b]
    coefs, rows_of = [*coefs_a, *coefs_b], [units[0], units[2], unit_0, units[1]]
    other = image_grad(params, coefs, rows_of, 1, BF, losses)
    own = image_grad(params, coefs, rows_of, 0, F32)

    keep, loss, *go = call(
        image_quarter_kernel,
        [((rows, width), F32), ((4, rows), F32)] + [((rows, width), BF)] * 3,
        [own, rot(other, "c", 1), *losses],
    )
    img_parts = [rot(go[k - 1], "y", -k) for k in (1, 3, 2)]
    *coefs_a, keep = lax.optimization_barrier((*coefs_a, keep))
    *grads, own_txt = text_grads(params, images, coefs_a)
    up, down, keep = lax.optimization_barrier((*far, keep))
    before_go, after_go = call(join_kernel, [((pair_rows, width), BF)] * 2, [*grads, up, down])
    txt_parts = [rot(before_go, "z", -1), rot(after_go, "z", 1)]

    half_t = txt_x.shape[1] // 2
    feats = [pair, before, after, txt_far]
    row_units = [unit_txt, sets[0][1], sets[2][1], sets[1][1]]
    lengths = [len_txt, sets[0][2], sets[2][2], sets[1][2]]
    far_grad[0], _ = lax.optimization_barrier((far_grad[0], before_go))
    part_keep, part_go = call(
        functools.partial(text_weight_kernel, 4),
        [((half_t, width), F32), ((half_t, width), BF)],
        [*feats, *row_units, *lengths, own_txt, *grads, *far_grad, txt_pick],
    )
    img_parts[0], img_parts[1], img_parts[2], part_keep = lax.optimization_barrier((*img_parts, part_keep))
    (delta_img,) = call(
        image_delta_kernel,
        [((rows, width), BF)],
        [keep, *img_parts, unit_img, len_img],
        flops=LONG,
    )
    half = rows // 2
    gathered = [rot(delta_img, "y", 1), rot(delta_img, "y", -1)]
    far = [rot(gathered[0][:half], "y", 1), rot(gathered[1][half:], "y", -1)]
    part_go, *txt_parts = lax.optimization_barrier((rot(part_go, "c", 1), *txt_parts))
    keep, *txt_go = quarters(part_keep, part_go)
    txt_go = [rot(txt_go[k - 1], "z", k) for k in (1, 3, 2)]
    own_grad, go_x = call(
        text_kernel, [((rows, width), F32), ((rows, width), BF)], [own_txt, *txt_parts]
    )
    img_feats = select([img_mine], img_pick)
    (grad_image,) = call(
        feature_grad_kernel, [((rows, img_x.shape[1]), BF)], [delta_img, w_image]
    )
    *far, txt_go[0], txt_go[1], moved, img_feats, grad_image = lax.optimization_barrier(
        (*far, txt_go[0], txt_go[1], rot(go_x, "xh", 1), img_feats, grad_image)
    )
    grad_unit_txt = own_grad + moved.astype(F32)
    half_i = img_feats.shape[1] // 2
    part_keep, part_go = call(
        weight_kernel,
        [((half_i, width), F32), ((half_i, width), BF)],
        [img_feats, delta_img, gathered[0], *far, gathered[1]],
    )
    keep_i, *go = quarters(part_keep, rot(part_go, "c", 1))
    img_go = [rot(go[k - 1], "z", k) for k in (1, 3, 2)]
    cut_y = keep.shape[0] // 4
    txt_go[2], keep_i = lax.optimization_barrier((txt_go[2], keep_i))
    sum_txt, *go = call(
        text_quarter_kernel,
        [((cut_y, width), F32)] + [(((cut_y + 15) // 16 * 16 + 16, width), BF)] * 3,
        [keep, *txt_go, loss],
    )
    txt_go = [rot(go[k - 1], "y", k) for k in (1, 3, 2)]
    keep, row_loss, *go = call(
        tail_kernel,
        [((32, width), F32), ((1, rows), F32)] + [((32, width), BF)] * 3,
        [keep_i, *img_go, sum_txt, *txt_go, loss],
    )
    moved = []
    for dh, dl in ((0, 1), (1, 0), (1, 1)):
        pairs = [(h * 2 + l, ((h + dh) % 2) * 2 + (l + dl) % 2) for h in (0, 1) for l in (0, 1)]
        moved.append(lax.ppermute(go[2 * dh + dl - 1], ("xh", "xl"), pairs))
    grad_w_image, grad_w_text = call(
        last_kernel, [((cut_img, width), F32), ((cut, width), F32)], [keep, *moved]
    )

    delta_txt = back(unit_txt[:rows], len_txt[:rows], grad_unit_txt)
    grad_text = mm_t(delta_txt, w_text).astype(BF)[None]
    return (row_loss, grad_image[None], grad_text, grad_w_image, grad_w_text)


def solution(mesh):
    fine = Mesh(mesh.devices.reshape([SIZES[a] for a in AXES]), AXES)
    blk = ("xh", "y", "z", "c")
    in_specs = (
        P("xl", blk, None),
        P("xl", blk, None),
        P("xl", blk, None),
        P(),
        P(),
        P(),
        P(),
    )
    out_specs = (
        P("xl", blk),
        P("xl", blk, None),
        P("xl", blk, None),
        P(AXES, None),
        P(AXES, None),
    )
    return jax.shard_map(
        per_device, mesh=fine, in_specs=in_specs, out_specs=out_specs, check_vma=False
    )
```

```python
import functools

import jax
import jax.numpy as jnp
import numpy as np
from jax import lax
from jax.experimental import pallas as pl
from jax.experimental.pallas import tpu as pltpu
from jax.sharding import Mesh
from jax.sharding import PartitionSpec as P

AXES = ("xh", "y", "z", "c", "xl")
SIZES = {"xh": 2, "y": 4, "z": 4, "c": 2, "xl": 2}
BF = jnp.bfloat16
F32 = jnp.float32
VMEM = pl.BlockSpec(memory_space=pltpu.VMEM)
SMEM = pl.BlockSpec(memory_space=pltpu.SMEM)
MIB = 1 << 20
LONG = 400 * 10**9


def rot(value, axis, steps):
    n = SIZES[axis]
    return lax.ppermute(value, axis, [(i, (i + steps) % n) for i in range(n)])


def mm(a, b):
    return jnp.dot(a, b, preferred_element_type=F32)


def mm_t(a, b):
    return lax.dot_general(a, b, (((1,), (1,)), ((), ())), preferred_element_type=F32)


def t_mm(a, b):
    return lax.dot_general(a, b, (((0,), (0,)), ((), ())), preferred_element_type=F32)


def call(kernel, out, args, smem=0, flops=1024):
    return pl.pallas_call(
        kernel,
        out_shape=[jax.ShapeDtypeStruct(shape, dtype) for shape, dtype in out],
        in_specs=[SMEM] * smem + [VMEM] * (len(args) - smem),
        out_specs=[VMEM] * len(out),
        cost_estimate=pl.CostEstimate(flops=flops, bytes_accessed=1024, transcendentals=0),
        compiler_params=pltpu.CompilerParams(vmem_limit_bytes=16 * MIB),
    )(*args)


def project_kernel(n, step, kept, *refs):
    blocks, w_ref, unit_ref = refs[:n], refs[n], refs[n + 1]
    feats = jnp.concatenate([b[...] for b in blocks], axis=0)
    for at in range(0, feats.shape[0], step):
        proj = mm(feats[at : at + step], w_ref[...])
        length = jnp.sqrt(jnp.sum(proj * proj, axis=1, keepdims=True) + 1e-06)
        unit = proj / length
        unit_ref[at : at + step, :] = unit.astype(BF)
        if at == 0 and kept:
            refs[n + 2][...] = unit[:kept]
            refs[n + 3][...] = length[:kept]


def project(blocks, weight, step, kept=0):
    n, rows, width = len(blocks), sum(b.shape[0] for b in blocks), weight.shape[1]
    out = [((rows, width), BF)]
    if kept:
        out += [((kept, width), F32), ((kept, 1), F32)]
    return list(call(functools.partial(project_kernel, n, step, kept), out, [*blocks, weight]))


def stack_kernel(*refs):
    rows = refs[0].shape[0]
    for k, ref in enumerate(refs[:-1]):
        refs[-1][k * rows : (k + 1) * rows, :] = ref[...]


def pair_kernel(n, first, split, *refs):
    params, images = refs[0], refs[1]
    units, at = refs[2 : 2 + n], 2 + n
    if first:
        paired = refs[at]
        at += 1
    coefs, loss_ref, grads = refs[at : at + n], refs[at + n], refs[at + n + 1 :]
    scale, offset = params[0], params[1]
    step = images.shape[0] // 4
    for k in range(n):
        own = first and k == n - 1
        for j in range(4):
            cols = slice(j * step, (j + 1) * step)
            margin = scale * mm_t(units[k][...], images[cols, :]) + offset
            if own:
                place = lax.broadcasted_iota(jnp.int32, margin.shape, 0)
                positive = place == paired[:, cols]
                margin = jnp.where(positive, -margin, margin)
            power = jnp.exp(margin)
            whole = 1.0 + power
            near = power * (1.0 - power * (0.5 - power * (1.0 / 3.0)))
            terms = jnp.where(power < 0.01, near, jnp.log(whole))
            turn = pl.reciprocal(whole, approx=True)
            coeff = power * (turn * (2.0 - whole * turn))
            if own:
                coeff = jnp.where(positive, -coeff, coeff)
            part = jnp.sum(terms, axis=0, keepdims=True)
            loss_ref[:, cols] = part if k == 0 else loss_ref[:, cols] + part
            coefs[k][:, cols] = coeff.astype(BF)
    if split:
        grad = scale * mm(coefs[0][...], images[...])
        cut = grad.shape[0] // 2
        grads[0][...] = grad[:cut].astype(BF)
        grads[1][...] = grad[cut:].astype(BF)


def pair_terms(params, images, units, paired=None, split=False):
    n, (rows, width), total = len(units), units[0].shape, images.shape[0]
    first = paired is not None
    grads = [((rows // 2, width), BF)] * 2 if split else []
    out = [((rows, total), BF)] * n + [((1, total), F32)] + grads
    args = [params, images, *units] + ([paired] if first else [])
    res = call(functools.partial(pair_kernel, n, first, split), out, args, smem=1)
    return res[:n], res[n], list(res[n + 1 :])


def text_grad_kernel(n, *refs):
    params, images, coefs, grads = refs[0], refs[1], refs[2 : 2 + n], refs[2 + n :]
    for coef, grad in zip(coefs, grads):
        grad[...] = params[0] * mm(coef[...], images[...])


def text_grads(params, images, coefs):
    n, out = len(coefs), ((coefs[0].shape[0], images.shape[1]), F32)
    args = [params, images, *coefs]
    return call(functools.partial(text_grad_kernel, n), [out] * n, args, smem=1, flops=LONG)


def join_kernel(before, after, up, down, before_out, after_out):
    cut = up.shape[0]
    before_out[:cut] = before[:cut].astype(BF)
    before_out[cut:] = (before[cut:] + down[...].astype(F32)).astype(BF)
    after_out[:cut] = (after[:cut] + up[...].astype(F32)).astype(BF)
    after_out[cut:] = after[cut:].astype(BF)


def loss_rows(losses, at, rows):
    return jnp.concatenate([losses[:, at + k * rows : at + (k + 1) * rows] for k in range(4)], axis=0)


def two_parts(value, width):
    high = value.astype(BF)
    low = (value - high.astype(F32)).astype(BF)
    parts = jnp.concatenate([high, low], axis=0).astype(F32)
    down = jnp.zeros((16 - parts.shape[0], parts.shape[1]), F32)
    parts = jnp.concatenate([parts, down], axis=0)
    right = jnp.zeros((16, width - parts.shape[1]), F32)
    return jnp.concatenate([parts, right], axis=1).astype(BF)


def image_kernel(n, half, *refs):
    params, coefs, units = refs[0], refs[1 : 1 + n], refs[1 + n : 1 + 2 * n]
    *losses, out_ref = refs[1 + 2 * n :]
    total, width = coefs[0].shape[1], units[0].shape[1]
    tile = total // 4
    for j in range(2):
        cols = slice((2 * half + j) * tile, (2 * half + j + 1) * tile)
        grad = t_mm(coefs[0][:, cols], units[0][...])
        for k in range(1, n):
            grad = grad + t_mm(coefs[k][:, cols], units[k][...])
        out_ref[j * tile : (j + 1) * tile, :] = (params[0] * grad).astype(out_ref.dtype)
    if losses:
        rows = total // 8
        tail = loss_rows(losses[0][...] + losses[1][...], total // 2, rows)
        out_ref[2 * tile :, :] = two_parts(tail, width)


def image_grad(params, coefs, units, half, dtype, losses=()):
    n, total, width = len(coefs), coefs[0].shape[1], units[0].shape[1]
    out = [((total // 2 + (16 if losses else 0), width), dtype)]
    args = [params, *coefs, *units, *losses]
    flops = 1024 if losses else LONG
    return call(functools.partial(image_kernel, n, half), out, args, smem=1, flops=flops)[0]


def quarter_kernel(own, moved, keep, *go):
    cut = keep.shape[0]
    keep[...] = own[:cut] + moved[:cut].astype(F32)
    for k, ref in enumerate(go):
        at = slice((k + 1) * cut, (k + 2) * cut)
        ref[...] = (own[at] + moved[at].astype(F32)).astype(BF)


def quarters(own, moved):
    cut, width = own.shape[0] // 4, own.shape[1]
    return call(quarter_kernel, [((cut, width), F32)] + [((cut, width), BF)] * 3, [own, moved])


def image_quarter_kernel(own, moved, loss_a, loss_b, keep, loss_out, *go):
    rows = keep.shape[0]
    keep[...] = own[:rows] + moved[:rows].astype(F32)
    tail = moved[own.shape[0] :, :rows].astype(F32)
    loss_out[...] = loss_rows(loss_a[...] + loss_b[...], 0, rows) + tail[0:4] + tail[4:8]
    for k, ref in enumerate(go):
        at = slice((k + 1) * rows, (k + 2) * rows)
        ref[...] = (own[at] + moved[at].astype(F32)).astype(BF)


def back(unit, length, grad):
    inner = jnp.sum(unit * grad, axis=1, keepdims=True)
    return ((grad - unit * inner) / length).astype(BF)


def image_delta_kernel(own, a, b, c, unit, length, out):
    grad = own[...] + a[...].astype(F32) + b[...].astype(F32) + c[...].astype(F32)
    out[...] = back(unit[...], length[...], grad)


def text_kernel(own, a, b, keep, go):
    grad = own[...] + a[...].astype(F32) + b[...].astype(F32)
    rows = keep.shape[0]
    keep[...] = grad[:rows]
    go[...] = grad[rows:].astype(BF)


def text_weight_kernel(n, *refs):
    pick, part_keep, part_go = refs[-3:]
    half = part_keep.shape[0]
    feats, units, lengths, grads = refs[:n], refs[n : 2 * n], refs[2 * n : 3 * n], refs[3 * n : -3]
    deltas = []
    for k in range(n):
        grad = grads[k][...] if k < n - 1 else jnp.concatenate([g[...] for g in grads[k:]], axis=0)
        deltas.append(back(units[k][...], lengths[k][...], grad.astype(F32)))
    delta = jnp.concatenate(deltas, axis=0)
    feats = jnp.concatenate([f[...] for f in feats], axis=0)
    feats = mm(feats, pick[...]).astype(BF)
    part_go[...] = t_mm(feats[:, half:], delta).astype(BF)
    part_keep[...] = t_mm(feats[:, :half], delta)


def weight_kernel(feats, a, b, c, d, e, part_keep, part_go):
    half = part_keep.shape[0]
    delta = jnp.concatenate([a[...], b[...], c[...], d[...], e[...]], axis=0)
    part_go[...] = t_mm(feats[:, half:], delta).astype(BF)
    part_keep[...] = t_mm(feats[:, :half], delta)


def select_kernel(n, *refs):
    feats = jnp.concatenate([r[...] for r in refs[:n]], axis=0)
    refs[n + 1][...] = mm(feats, refs[n][...]).astype(BF)


def select(blocks, pick):
    n, rows = len(blocks), blocks[0].shape[0]
    out = [((n * rows, pick.shape[1]), BF)]
    return call(functools.partial(select_kernel, n), out, [*blocks, pick])[0]


def feature_grad_kernel(delta, weight, out):
    out[...] = mm_t(delta[...], weight[...]).astype(BF)


def text_quarter_kernel(own, a, b, c, loss, keep, *go):
    total = own[...] + a[...].astype(F32) + b[...].astype(F32) + c[...].astype(F32)
    cut, width = keep.shape
    keep[...] = total[:cut]
    for k, ref in enumerate(go):
        part = total[(k + 1) * cut : (k + 2) * cut]
        fill = jnp.zeros((ref.shape[0] - 16 - cut, width), F32)
        tail = two_parts(loss[3 - k : 4 - k], width).astype(F32)
        ref[...] = jnp.concatenate([part, fill, tail], axis=0).astype(BF)


def tail_kernel(img, i1, i2, i3, txt, t1, t2, t3, loss, keep, loss_out, *go):
    total_i, total_t, losses = img[...], txt[...], loss[0:1]
    rows, cut = losses.shape[1], total_t.shape[0]
    for ref in (i1, i2, i3):
        total_i = total_i + ref[...].astype(F32)
    for ref in (t1, t2, t3):
        moved = ref[...].astype(F32)
        total_t = total_t + moved[:cut]
        tail = moved[moved.shape[0] - 16 :, :rows]
        losses = losses + tail[0:1] + tail[1:2]
    loss_out[...] = losses / rows
    cut_i, cut_t, width = total_i.shape[0] // 4, cut // 4, total_i.shape[1]
    for k, ref in enumerate((keep, *go)):
        parts = [
            total_i[k * cut_i : (k + 1) * cut_i],
            jnp.zeros((16 - cut_i, width), F32),
            total_t[k * cut_t : (k + 1) * cut_t],
            jnp.zeros((16 - cut_t, width), F32),
        ]
        ref[...] = jnp.concatenate(parts, axis=0).astype(ref.dtype)


def last_kernel(keep, a, b, c, out_i, out_t):
    total = keep[...] + a[...].astype(F32) + b[...].astype(F32) + c[...].astype(F32)
    out_i[...] = total[: out_i.shape[0]]
    out_t[...] = total[16 : 16 + out_t.shape[0]]


def selection(depth, cut, steps):
    names = ("c", "z", "y", "xh", "xl")
    dims = [SIZES[a] if a in steps else 1 for a in names] + [cut]
    away = dict(zip(names + ("row",), (i.reshape(1, -1).astype(np.int32) for i in np.indices(dims))))
    place = 0
    for a in ("xh", "y", "z", "c", "xl"):
        place = place * SIZES[a] + ((lax.axis_index(a) + away[a]) & (SIZES[a] - 1))
    return (jnp.arange(depth)[:, None] == place * cut + away["row"]).astype(BF)


def per_device(image_feats, text_feats, match, w_image, w_text, log_temp, bias):
    img_x, txt_x = image_feats[0], text_feats[0]
    rows, width = img_x.shape[0], w_image.shape[1]
    scale = jnp.exp(log_temp[0])
    params = jnp.stack([scale, bias[0]])

    paired = jnp.concatenate([match[0], jnp.full((1, 7 * rows), -1, jnp.int32)], axis=1)
    cut, cut_img = txt_x.shape[1] // 128, img_x.shape[1] // 128
    txt_pick = selection(txt_x.shape[1], cut, ("c", "z", "y", "xh", "xl"))
    img_pick = selection(img_x.shape[1], cut_img, ("c", "z", "xh", "xl"))

    pair_rows = 2 * rows
    partner = rot(txt_x, "xh", 1)
    img_last, partner = lax.optimization_barrier((img_x, partner))
    img_first, txt_pick = lax.optimization_barrier((img_x, txt_pick))
    img_near = [rot(img_first, "y", 1), rot(img_last, "y", 2), rot(img_first, "y", 3)]
    (pair,) = call(stack_kernel, [((pair_rows, txt_x.shape[1]), BF)], [txt_x, partner])
    before, after = rot(pair, "z", 1), rot(pair, "z", -1)
    far = [rot(before[:rows], "z", 1), rot(after[rows:], "z", -1)]
    unit_0, unit_txt, len_txt = project([pair], w_text, pair_rows, kept=pair_rows)
    *img_near, before, after, paired, unit_0, unit_txt, txt_pick, img_pick = lax.optimization_barrier(
        (*img_near, before, after, paired, unit_0, unit_txt, txt_pick, img_pick)
    )
    (img_mine,) = call(stack_kernel, [((4 * rows, img_x.shape[1]), BF)], [img_x, *img_near])
    img_moved = rot(img_mine, "c", 1)

    sets = [project([before], w_text, pair_rows, kept=pair_rows), None]
    sets.append(project([after], w_text, pair_rows, kept=pair_rows))
    img_moved, sets[0][0], sets[2][0] = lax.optimization_barrier((img_moved, sets[0][0], sets[2][0]))
    images, unit_img, len_img = project([img_mine, img_moved], w_image, pair_rows, kept=rows)
    *far, images = lax.optimization_barrier((*far, images))
    (txt_far,) = call(stack_kernel, [((pair_rows, txt_x.shape[1]), BF)], far)
    sets[1] = project([txt_far], w_text, pair_rows, kept=pair_rows)
    units = [part[0] for part in sets]

    coefs_b, loss_b, far_grad = pair_terms(params, images, [units[1]], split=True)
    far = [rot(far_grad[0], "z", 1), rot(far_grad[1], "z", -1)]
    coefs_a, loss_a, _ = pair_terms(params, images, [units[0], units[2], unit_0], paired)
    losses = [loss_a, loss_b]
    coefs, rows_of = [*coefs_a, *coefs_b], [units[0], units[2], unit_0, units[1]]
    other = image_grad(params, coefs, rows_of, 1, BF, losses)
    own = image_grad(params, coefs, rows_of, 0, F32)

    keep, loss, *go = call(
        image_quarter_kernel,
        [((rows, width), F32), ((4, rows), F32)] + [((rows, width), BF)] * 3,
        [own, rot(other, "c", 1), *losses],
    )
    img_parts = [rot(go[k - 1], "y", -k) for k in (1, 3, 2)]
    *coefs_a, keep = lax.optimization_barrier((*coefs_a, keep))
    *grads, own_txt = text_grads(params, images, coefs_a)
    up, down, keep = lax.optimization_barrier((*far, keep))
    before_go, after_go = call(join_kernel, [((pair_rows, width), BF)] * 2, [*grads, up, down])
    txt_parts = [rot(before_go, "z", -1), rot(after_go, "z", 1)]

    half_t = txt_x.shape[1] // 2
    feats = [pair, before, after, txt_far]
    row_units = [unit_txt, sets[0][1], sets[2][1], sets[1][1]]
    lengths = [len_txt, sets[0][2], sets[2][2], sets[1][2]]
    far_grad[0], _ = lax.optimization_barrier((far_grad[0], before_go))
    part_keep, part_go = call(
        functools.partial(text_weight_kernel, 4),
        [((half_t, width), F32), ((half_t, width), BF)],
        [*feats, *row_units, *lengths, own_txt, *grads, *far_grad, txt_pick],
    )
    img_parts[0], img_parts[1], img_parts[2], part_keep = lax.optimization_barrier((*img_parts, part_keep))
    (delta_img,) = call(
        image_delta_kernel,
        [((rows, width), BF)],
        [keep, *img_parts, unit_img, len_img],
        flops=LONG,
    )
    half = rows // 2
    gathered = [rot(delta_img, "y", 1), rot(delta_img, "y", -1)]
    far = [rot(gathered[0][:half], "y", 1), rot(gathered[1][half:], "y", -1)]
    part_go, *txt_parts = lax.optimization_barrier((rot(part_go, "c", 1), *txt_parts))
    keep, *txt_go = quarters(part_keep, part_go)
    txt_go = [rot(txt_go[k - 1], "z", k) for k in (1, 3, 2)]
    own_grad, go_x = call(
        text_kernel, [((rows, width), F32), ((rows, width), BF)], [own_txt, *txt_parts]
    )
    img_feats = select([img_mine], img_pick)
    (grad_image,) = call(
        feature_grad_kernel, [((rows, img_x.shape[1]), BF)], [delta_img, w_image]
    )
    *far, txt_go[0], txt_go[1], txt_go[2], moved, img_feats, grad_image = lax.optimization_barrier(
        (*far, *txt_go, rot(go_x, "xh", 1), img_feats, grad_image)
    )
    grad_unit_txt = own_grad + moved.astype(F32)
    half_i = img_feats.shape[1] // 2
    part_keep, part_go = call(
        weight_kernel,
        [((half_i, width), F32), ((half_i, width), BF)],
        [img_feats, delta_img, gathered[0], *far, gathered[1]],
    )
    keep_i, *go = quarters(part_keep, rot(part_go, "c", 1))
    img_go = [rot(go[k - 1], "z", k) for k in (1, 3, 2)]
    cut_y = keep.shape[0] // 4
    sum_txt, *go = call(
        text_quarter_kernel,
        [((cut_y, width), F32)] + [(((cut_y + 15) // 16 * 16 + 16, width), BF)] * 3,
        [keep, *txt_go, loss],
    )
    txt_go = [rot(go[k - 1], "y", k) for k in (1, 3, 2)]
    delta_txt = back(unit_txt[:rows], len_txt[:rows], grad_unit_txt)
    grad_text = mm_t(delta_txt, w_text).astype(BF)[None]
    grad_text, *txt_go = lax.optimization_barrier((grad_text, *txt_go))
    keep, row_loss, *go = call(
        tail_kernel,
        [((32, width), F32), ((1, rows), F32)] + [((32, width), BF)] * 3,
        [keep_i, *img_go, sum_txt, *txt_go, loss],
    )
    moved = []
    for dh, dl in ((0, 1), (1, 0), (1, 1)):
        pairs = [(h * 2 + l, ((h + dh) % 2) * 2 + (l + dl) % 2) for h in (0, 1) for l in (0, 1)]
        moved.append(lax.ppermute(go[2 * dh + dl - 1], ("xh", "xl"), pairs))
    grad_w_image, grad_w_text = call(
        last_kernel, [((cut_img, width), F32), ((cut, width), F32)], [keep, *moved]
    )

    return (row_loss, grad_image[None], grad_text, grad_w_image, grad_w_text)


def solution(mesh):
    fine = Mesh(mesh.devices.reshape([SIZES[a] for a in AXES]), AXES)
    blk = ("xh", "y", "z", "c")
    in_specs = (
        P("xl", blk, None),
        P("xl", blk, None),
        P("xl", blk, None),
        P(),
        P(),
        P(),
        P(),
    )
    out_specs = (
        P("xl", blk),
        P("xl", blk, None),
        P("xl", blk, None),
        P(AXES, None),
        P(AXES, None),
    )
    return jax.shard_map(
        per_device, mesh=fine, in_specs=in_specs, out_specs=out_specs, check_vma=False
    )
```

```python
import functools

import jax
import jax.numpy as jnp
import numpy as np
from jax import lax
from jax.experimental import pallas as pl
from jax.experimental.pallas import tpu as pltpu
from jax.sharding import Mesh
from jax.sharding import PartitionSpec as P

AXES = ("xh", "y", "z", "c", "xl")
SIZES = {"xh": 2, "y": 4, "z": 4, "c": 2, "xl": 2}
BF = jnp.bfloat16
F32 = jnp.float32
VMEM = pl.BlockSpec(memory_space=pltpu.VMEM)
SMEM = pl.BlockSpec(memory_space=pltpu.SMEM)
MIB = 1 << 20
LONG = 400 * 10**9


def rot(value, axis, steps):
    n = SIZES[axis]
    return lax.ppermute(value, axis, [(i, (i + steps) % n) for i in range(n)])


def mm(a, b):
    return jnp.dot(a, b, preferred_element_type=F32)


def mm_t(a, b):
    return lax.dot_general(a, b, (((1,), (1,)), ((), ())), preferred_element_type=F32)


def t_mm(a, b):
    return lax.dot_general(a, b, (((0,), (0,)), ((), ())), preferred_element_type=F32)


def call(kernel, out, args, smem=0, flops=1024):
    return pl.pallas_call(
        kernel,
        out_shape=[jax.ShapeDtypeStruct(shape, dtype) for shape, dtype in out],
        in_specs=[SMEM] * smem + [VMEM] * (len(args) - smem),
        out_specs=[VMEM] * len(out),
        cost_estimate=pl.CostEstimate(flops=flops, bytes_accessed=1024, transcendentals=0),
        compiler_params=pltpu.CompilerParams(vmem_limit_bytes=16 * MIB),
    )(*args)


def project_kernel(n, step, kept, *refs):
    blocks, w_ref, unit_ref = refs[:n], refs[n], refs[n + 1]
    feats = jnp.concatenate([b[...] for b in blocks], axis=0)
    for at in range(0, feats.shape[0], step):
        proj = mm(feats[at : at + step], w_ref[...])
        length = jnp.sqrt(jnp.sum(proj * proj, axis=1, keepdims=True) + 1e-06)
        unit = proj / length
        unit_ref[at : at + step, :] = unit.astype(BF)
        if at == 0 and kept:
            refs[n + 2][...] = unit[:kept]
            refs[n + 3][...] = length[:kept]


def project(blocks, weight, step, kept=0):
    n, rows, width = len(blocks), sum(b.shape[0] for b in blocks), weight.shape[1]
    out = [((rows, width), BF)]
    if kept:
        out += [((kept, width), F32), ((kept, 1), F32)]
    return list(call(functools.partial(project_kernel, n, step, kept), out, [*blocks, weight]))


def second_kernel(own, partner, t_before, t_after, up, down, pair):
    rows, half = partner.shape[0], partner.shape[0] // 2
    up[:rows] = partner[...]
    up[rows:] = t_before[:half]
    down[:rows] = partner[...]
    down[rows:] = t_after[half:]
    pair[:rows] = own[...]
    pair[rows:] = partner[...]


def third_kernel(t_before, t_after, up, down, t_up, t_down, before, after, far):
    rows, half = t_before.shape[0], t_before.shape[0] // 2
    t_up[...] = up[:half]
    t_down[...] = down[half:rows]
    before[:rows] = t_before[...]
    before[rows:] = up[:rows]
    after[:rows] = t_after[...]
    after[rows:] = down[:rows]
    far[:half] = up[rows:]
    far[half:] = down[rows:]


def far_image_kernel(block, weight, near, out):
    rows = block.shape[0]
    proj = mm(block[...], weight[...])
    length = jnp.sqrt(jnp.sum(proj * proj, axis=1, keepdims=True) + 1e-06)
    out[: 2 * rows] = near[: 2 * rows]
    out[2 * rows : 3 * rows] = (proj / length).astype(BF)
    out[3 * rows :] = near[2 * rows :]


def stack_kernel(*refs):
    at = 0
    for ref in refs[:-1]:
        refs[-1][at : at + ref.shape[0], :] = ref[...]
        at += ref.shape[0]


def pair_kernel(n, first, split, *refs):
    params, images = refs[0], refs[1]
    units, at = refs[2 : 2 + n], 2 + n
    if first:
        paired = refs[at]
        at += 1
    coefs, loss_ref, grads = refs[at : at + n], refs[at + n], refs[at + n + 1 :]
    scale, offset = params[0], params[1]
    step = images.shape[0] // 4
    for k in range(n):
        own = first and k == n - 1
        for j in range(4):
            cols = slice(j * step, (j + 1) * step)
            margin = scale * mm_t(units[k][...], images[cols, :]) + offset
            if own:
                place = lax.broadcasted_iota(jnp.int32, margin.shape, 0)
                positive = place == paired[:, cols]
                margin = jnp.where(positive, -margin, margin)
            power = jnp.exp(margin)
            whole = 1.0 + power
            near = power * (1.0 - power * (0.5 - power * (1.0 / 3.0)))
            terms = jnp.where(power < 0.01, near, jnp.log(whole))
            turn = pl.reciprocal(whole, approx=True)
            coeff = power * (turn * (2.0 - whole * turn))
            if own:
                coeff = jnp.where(positive, -coeff, coeff)
            part = jnp.sum(terms, axis=0, keepdims=True)
            loss_ref[:, cols] = part if k == 0 else loss_ref[:, cols] + part
            coefs[k][:, cols] = coeff.astype(BF)
    if split:
        grad = scale * mm(coefs[0][...], images[...])
        cut = grad.shape[0] // 2
        grads[0][...] = grad[:cut].astype(BF)
        grads[1][...] = grad[cut:].astype(BF)


def pair_terms(params, images, units, paired=None, split=False):
    n, (rows, width), total = len(units), units[0].shape, images.shape[0]
    first = paired is not None
    grads = [((rows // 2, width), BF)] * 2 if split else []
    out = [((rows, total), BF)] * n + [((1, total), F32)] + grads
    args = [params, images, *units] + ([paired] if first else [])
    res = call(functools.partial(pair_kernel, n, first, split), out, args, smem=1)
    return res[:n], res[n], list(res[n + 1 :])


def text_grad_kernel(n, *refs):
    params, images, coefs, grads = refs[0], refs[1], refs[2 : 2 + n], refs[2 + n :]
    for coef, grad in zip(coefs, grads):
        grad[...] = params[0] * mm(coef[...], images[...])


def text_grads(params, images, coefs):
    n, out = len(coefs), ((coefs[0].shape[0], images.shape[1]), F32)
    args = [params, images, *coefs]
    return call(functools.partial(text_grad_kernel, n), [out] * n, args, smem=1, flops=LONG)


def join_kernel(before, after, up, down, before_out, after_out):
    cut = up.shape[0]
    before_out[:cut] = before[:cut].astype(BF)
    before_out[cut:] = (before[cut:] + down[...].astype(F32)).astype(BF)
    after_out[:cut] = (after[:cut] + up[...].astype(F32)).astype(BF)
    after_out[cut:] = after[cut:].astype(BF)


def loss_rows(losses, at, rows):
    return jnp.concatenate([losses[:, at + k * rows : at + (k + 1) * rows] for k in range(4)], axis=0)


def two_parts(value, width):
    high = value.astype(BF)
    low = (value - high.astype(F32)).astype(BF)
    parts = jnp.concatenate([high, low], axis=0).astype(F32)
    down = jnp.zeros((16 - parts.shape[0], parts.shape[1]), F32)
    parts = jnp.concatenate([parts, down], axis=0)
    right = jnp.zeros((16, width - parts.shape[1]), F32)
    return jnp.concatenate([parts, right], axis=1).astype(BF)


def image_kernel(n, half, *refs):
    params, coefs, units = refs[0], refs[1 : 1 + n], refs[1 + n : 1 + 2 * n]
    *losses, out_ref = refs[1 + 2 * n :]
    total, width = coefs[0].shape[1], units[0].shape[1]
    tile = total // 4
    for j in range(2):
        cols = slice((2 * half + j) * tile, (2 * half + j + 1) * tile)
        grad = t_mm(coefs[0][:, cols], units[0][...])
        for k in range(1, n):
            grad = grad + t_mm(coefs[k][:, cols], units[k][...])
        out_ref[j * tile : (j + 1) * tile, :] = (params[0] * grad).astype(out_ref.dtype)
    if losses:
        rows = total // 8
        tail = loss_rows(losses[0][...] + losses[1][...], total // 2, rows)
        out_ref[2 * tile :, :] = two_parts(tail, width)


def image_grad(params, coefs, units, half, dtype, losses=()):
    n, total, width = len(coefs), coefs[0].shape[1], units[0].shape[1]
    out = [((total // 2 + (16 if losses else 0), width), dtype)]
    args = [params, *coefs, *units, *losses]
    flops = 1024 if losses else LONG
    return call(functools.partial(image_kernel, n, half), out, args, smem=1, flops=flops)[0]


def quarter_kernel(own, moved, keep, *go):
    cut = keep.shape[0]
    keep[...] = own[:cut] + moved[:cut].astype(F32)
    for k, ref in enumerate(go):
        at = slice((k + 1) * cut, (k + 2) * cut)
        ref[...] = (own[at] + moved[at].astype(F32)).astype(BF)


def quarters(own, moved):
    cut, width = own.shape[0] // 4, own.shape[1]
    return call(quarter_kernel, [((cut, width), F32)] + [((cut, width), BF)] * 3, [own, moved])


def image_quarter_kernel(own, moved, loss_a, loss_b, keep, loss_out, *go):
    rows = keep.shape[0]
    keep[...] = own[:rows] + moved[:rows].astype(F32)
    tail = moved[own.shape[0] :, :rows].astype(F32)
    loss_out[...] = loss_rows(loss_a[...] + loss_b[...], 0, rows) + tail[0:4] + tail[4:8]
    for k, ref in enumerate(go):
        at = slice((k + 1) * rows, (k + 2) * rows)
        ref[...] = (own[at] + moved[at].astype(F32)).astype(BF)


def back(unit, length, grad):
    inner = jnp.sum(unit * grad, axis=1, keepdims=True)
    return ((grad - unit * inner) / length).astype(BF)


def image_delta_kernel(own, a, b, c, unit, length, out):
    grad = own[...] + a[...].astype(F32) + b[...].astype(F32) + c[...].astype(F32)
    out[...] = back(unit[...], length[...], grad)


def text_kernel(own, a, b, keep, go):
    grad = own[...] + a[...].astype(F32) + b[...].astype(F32)
    rows = keep.shape[0]
    keep[...] = grad[:rows]
    go[...] = grad[rows:].astype(BF)


def text_weight_kernel(n, *refs):
    pick, part_keep, part_go = refs[-3:]
    half = part_keep.shape[0]
    feats, units, lengths, grads = refs[:n], refs[n : 2 * n], refs[2 * n : 3 * n], refs[3 * n : -3]
    deltas = []
    for k in range(n):
        grad = grads[k][...] if k < n - 1 else jnp.concatenate([g[...] for g in grads[k:]], axis=0)
        deltas.append(back(units[k][...], lengths[k][...], grad.astype(F32)))
    delta = jnp.concatenate(deltas, axis=0)
    feats = jnp.concatenate([f[...] for f in feats], axis=0)
    feats = mm(feats, pick[...]).astype(BF)
    part_go[...] = t_mm(feats[:, half:], delta).astype(BF)
    part_keep[...] = t_mm(feats[:, :half], delta)


def weight_kernel(feats, a, b, c, d, e, part_keep, part_go):
    half = part_keep.shape[0]
    delta = jnp.concatenate([a[...], b[...], c[...], d[...], e[...]], axis=0)
    part_go[...] = t_mm(feats[:, half:], delta).astype(BF)
    part_keep[...] = t_mm(feats[:, :half], delta)


def select_kernel(n, *refs):
    feats = jnp.concatenate([r[...] for r in refs[:n]], axis=0)
    refs[n + 1][...] = mm(feats, refs[n][...]).astype(BF)


def select(blocks, pick):
    n, rows = len(blocks), blocks[0].shape[0]
    out = [((n * rows, pick.shape[1]), BF)]
    return call(functools.partial(select_kernel, n), out, [*blocks, pick])[0]


def feature_grad_kernel(delta, weight, out):
    out[...] = mm_t(delta[...], weight[...]).astype(BF)


def text_quarter_kernel(own, a, b, c, loss, keep, *go):
    total = own[...] + a[...].astype(F32) + b[...].astype(F32) + c[...].astype(F32)
    cut, width = keep.shape
    keep[...] = total[:cut]
    for k, ref in enumerate(go):
        part = total[(k + 1) * cut : (k + 2) * cut]
        fill = jnp.zeros((ref.shape[0] - 16 - cut, width), F32)
        tail = two_parts(loss[3 - k : 4 - k], width).astype(F32)
        ref[...] = jnp.concatenate([part, fill, tail], axis=0).astype(BF)


def tail_kernel(img, i1, i2, i3, txt, t1, t2, t3, loss, keep, loss_out, *go):
    total_i, total_t, losses = img[...], txt[...], loss[0:1]
    rows, cut = losses.shape[1], total_t.shape[0]
    for ref in (i1, i2, i3):
        total_i = total_i + ref[...].astype(F32)
    for ref in (t1, t2, t3):
        moved = ref[...].astype(F32)
        total_t = total_t + moved[:cut]
        tail = moved[moved.shape[0] - 16 :, :rows]
        losses = losses + tail[0:1] + tail[1:2]
    loss_out[...] = losses / rows
    cut_i, cut_t, width = total_i.shape[0] // 4, cut // 4, total_i.shape[1]
    for k, ref in enumerate((keep, *go)):
        parts = [
            total_i[k * cut_i : (k + 1) * cut_i],
            jnp.zeros((16 - cut_i, width), F32),
            total_t[k * cut_t : (k + 1) * cut_t],
            jnp.zeros((16 - cut_t, width), F32),
        ]
        ref[...] = jnp.concatenate(parts, axis=0).astype(ref.dtype)


def last_kernel(keep, a, b, c, out_i, out_t):
    total = keep[...] + a[...].astype(F32) + b[...].astype(F32) + c[...].astype(F32)
    out_i[...] = total[: out_i.shape[0]]
    out_t[...] = total[16 : 16 + out_t.shape[0]]


def selection(depth, cut, steps):
    names = ("c", "z", "y", "xh", "xl")
    dims = [SIZES[a] if a in steps else 1 for a in names] + [cut]
    away = dict(zip(names + ("row",), (i.reshape(1, -1).astype(np.int32) for i in np.indices(dims))))
    place = 0
    for a in ("xh", "y", "z", "c", "xl"):
        place = place * SIZES[a] + ((lax.axis_index(a) + away[a]) & (SIZES[a] - 1))
    return (jnp.arange(depth)[:, None] == place * cut + away["row"]).astype(BF)


def per_device(image_feats, text_feats, match, w_image, w_text, log_temp, bias):
    img_x, txt_x = image_feats[0], text_feats[0]
    rows, width = img_x.shape[0], w_image.shape[1]
    scale = jnp.exp(log_temp[0])
    params = jnp.stack([scale, bias[0]])

    paired = jnp.concatenate([match[0], jnp.full((1, 7 * rows), -1, jnp.int32)], axis=1)
    cut, cut_img = txt_x.shape[1] // 128, img_x.shape[1] // 128
    txt_pick = selection(txt_x.shape[1], cut, ("c", "z", "y", "xh", "xl"))
    img_pick = selection(img_x.shape[1], cut_img, ("c", "z", "xh", "xl"))

    pair_rows = 2 * rows
    half, depth = rows // 2, txt_x.shape[1]
    partner, t_before, t_after = rot(txt_x, "xh", 1), rot(txt_x, "z", 1), rot(txt_x, "z", -1)
    img_first, txt_pick = lax.optimization_barrier((img_x, txt_pick))
    i_before, i_after = rot(img_first, "y", 1), rot(img_first, "y", -1)
    partner, t_before, t_after, img_last = lax.optimization_barrier(
        (partner, t_before, t_after, img_x)
    )
    i_far = rot(img_last, "y", 2)
    up, down, pair = call(
        second_kernel,
        [((rows + half, depth), BF)] * 2 + [((pair_rows, depth), BF)],
        [txt_x, partner, t_before, t_after],
    )
    up, down = rot(up, "z", 1), rot(down, "z", -1)
    unit_0, unit_txt, len_txt = project([pair], w_text, pair_rows, kept=pair_rows)
    near, unit_img, len_img = project([img_x, i_before, i_after], w_image, rows, kept=rows)
    up, down, near, paired, unit_0, unit_txt, img_pick = lax.optimization_barrier(
        (up, down, near, paired, unit_0, unit_txt, img_pick)
    )
    t_up, t_down, before, after, far_own = call(
        third_kernel,
        [((half, depth), BF)] * 2 + [((pair_rows, depth), BF)] * 2 + [((rows, depth), BF)],
        [t_before, t_after, up, down],
    )
    far = [far_own, rot(t_up, "z", 1), rot(t_down, "z", -1)]
    (mine,) = call(far_image_kernel, [((4 * rows, width), BF)], [i_far, w_image, near])
    moved = rot(mine, "c", 1)
    img_raw = [img_x, i_before, i_far, i_after]

    sets = [project([before], w_text, pair_rows, kept=pair_rows), None]
    sets.append(project([after], w_text, pair_rows, kept=pair_rows))
    moved, sets[0][0], sets[2][0] = lax.optimization_barrier((moved, sets[0][0], sets[2][0]))
    (images,) = call(stack_kernel, [((8 * rows, width), BF)], [mine, moved])
    far[1], far[2], images = lax.optimization_barrier((far[1], far[2], images))
    (txt_far,) = call(stack_kernel, [((pair_rows, depth), BF)], far)
    sets[1] = project([txt_far], w_text, pair_rows, kept=pair_rows)
    units = [part[0] for part in sets]

    coefs_b, loss_b, far_grad = pair_terms(params, images, [units[1]], split=True)
    far = [rot(far_grad[0], "z", 1), rot(far_grad[1], "z", -1)]
    coefs_a, loss_a, _ = pair_terms(params, images, [units[0], units[2], unit_0], paired)
    losses = [loss_a, loss_b]
    coefs, rows_of = [*coefs_a, *coefs_b], [units[0], units[2], unit_0, units[1]]
    other = image_grad(params, coefs, rows_of, 1, BF, losses)
    own = image_grad(params, coefs, rows_of, 0, F32)

    keep, loss, *go = call(
        image_quarter_kernel,
        [((rows, width), F32), ((4, rows), F32)] + [((rows, width), BF)] * 3,
        [own, rot(other, "c", 1), *losses],
    )
    img_parts = [rot(go[k - 1], "y", -k) for k in (1, 3, 2)]
    *coefs_a, keep = lax.optimization_barrier((*coefs_a, keep))
    *grads, own_txt = text_grads(params, images, coefs_a)
    up, down, keep = lax.optimization_barrier((*far, keep))
    before_go, after_go = call(join_kernel, [((pair_rows, width), BF)] * 2, [*grads, up, down])
    txt_parts = [rot(before_go, "z", -1), rot(after_go, "z", 1)]

    half_t = txt_x.shape[1] // 2
    feats = [pair, before, after, txt_far]
    row_units = [unit_txt, sets[0][1], sets[2][1], sets[1][1]]
    lengths = [len_txt, sets[0][2], sets[2][2], sets[1][2]]
    far_grad[0], _ = lax.optimization_barrier((far_grad[0], before_go))
    part_keep, part_go = call(
        functools.partial(text_weight_kernel, 4),
        [((half_t, width), F32), ((half_t, width), BF)],
        [*feats, *row_units, *lengths, own_txt, *grads, *far_grad, txt_pick],
    )
    img_parts[0], img_parts[1], img_parts[2], part_keep = lax.optimization_barrier((*img_parts, part_keep))
    (delta_img,) = call(
        image_delta_kernel,
        [((rows, width), BF)],
        [keep, *img_parts, unit_img, len_img],
        flops=LONG,
    )
    gathered = [rot(delta_img, "y", 1), rot(delta_img, "y", -1)]
    far = [rot(gathered[0][:half], "y", 1), rot(gathered[1][half:], "y", -1)]
    part_go, *txt_parts = lax.optimization_barrier((rot(part_go, "c", 1), *txt_parts))
    keep, *txt_go = quarters(part_keep, part_go)
    txt_go = [rot(txt_go[k - 1], "z", k) for k in (1, 3, 2)]
    own_grad, go_x = call(
        text_kernel, [((rows, width), F32), ((rows, width), BF)], [own_txt, *txt_parts]
    )
    img_feats = select(img_raw, img_pick)
    (grad_image,) = call(
        feature_grad_kernel, [((rows, img_x.shape[1]), BF)], [delta_img, w_image]
    )
    *far, txt_go[0], txt_go[1], txt_go[2], moved, img_feats, grad_image = lax.optimization_barrier(
        (*far, *txt_go, rot(go_x, "xh", 1), img_feats, grad_image)
    )
    grad_unit_txt = own_grad + moved.astype(F32)
    half_i = img_feats.shape[1] // 2
    part_keep, part_go = call(
        weight_kernel,
        [((half_i, width), F32), ((half_i, width), BF)],
        [img_feats, delta_img, gathered[0], *far, gathered[1]],
    )
    keep_i, *go = quarters(part_keep, rot(part_go, "c", 1))
    img_go = [rot(go[k - 1], "z", k) for k in (1, 3, 2)]
    cut_y = keep.shape[0] // 4
    sum_txt, *go = call(
        text_quarter_kernel,
        [((cut_y, width), F32)] + [(((cut_y + 15) // 16 * 16 + 16, width), BF)] * 3,
        [keep, *txt_go, loss],
    )
    txt_go = [rot(go[k - 1], "y", k) for k in (1, 3, 2)]
    delta_txt = back(unit_txt[:rows], len_txt[:rows], grad_unit_txt)
    grad_text = mm_t(delta_txt, w_text).astype(BF)[None]
    grad_text, *txt_go = lax.optimization_barrier((grad_text, *txt_go))
    keep, row_loss, *go = call(
        tail_kernel,
        [((32, width), F32), ((1, rows), F32)] + [((32, width), BF)] * 3,
        [keep_i, *img_go, sum_txt, *txt_go, loss],
    )
    moved = []
    for dh, dl in ((0, 1), (1, 0), (1, 1)):
        pairs = [(h * 2 + l, ((h + dh) % 2) * 2 + (l + dl) % 2) for h in (0, 1) for l in (0, 1)]
        moved.append(lax.ppermute(go[2 * dh + dl - 1], ("xh", "xl"), pairs))
    grad_w_image, grad_w_text = call(
        last_kernel, [((cut_img, width), F32), ((cut, width), F32)], [keep, *moved]
    )

    return (row_loss, grad_image[None], grad_text, grad_w_image, grad_w_text)


def solution(mesh):
    fine = Mesh(mesh.devices.reshape([SIZES[a] for a in AXES]), AXES)
    blk = ("xh", "y", "z", "c")
    in_specs = (
        P("xl", blk, None),
        P("xl", blk, None),
        P("xl", blk, None),
        P(),
        P(),
        P(),
        P(),
    )
    out_specs = (
        P("xl", blk),
        P("xl", blk, None),
        P("xl", blk, None),
        P(AXES, None),
        P(AXES, None),
    )
    return jax.shard_map(
        per_device, mesh=fine, in_specs=in_specs, out_specs=out_specs, check_vma=False
    )
```

```python
import functools

import jax
import jax.numpy as jnp
import numpy as np
from jax import lax
from jax.experimental import pallas as pl
from jax.experimental.pallas import tpu as pltpu
from jax.sharding import Mesh
from jax.sharding import PartitionSpec as P

AXES = ("xh", "y", "z", "c", "xl")
SIZES = {"xh": 2, "y": 4, "z": 4, "c": 2, "xl": 2}
BF = jnp.bfloat16
F32 = jnp.float32
VMEM = pl.BlockSpec(memory_space=pltpu.VMEM)
SMEM = pl.BlockSpec(memory_space=pltpu.SMEM)
MIB = 1 << 20
LONG = 400 * 10**9


def rot(value, axis, steps):
    n = SIZES[axis]
    return lax.ppermute(value, axis, [(i, (i + steps) % n) for i in range(n)])


def mm(a, b):
    return jnp.dot(a, b, preferred_element_type=F32)


def mm_t(a, b):
    return lax.dot_general(a, b, (((1,), (1,)), ((), ())), preferred_element_type=F32)


def t_mm(a, b):
    return lax.dot_general(a, b, (((0,), (0,)), ((), ())), preferred_element_type=F32)


def call(kernel, out, args, smem=0, flops=1024):
    return pl.pallas_call(
        kernel,
        out_shape=[jax.ShapeDtypeStruct(shape, dtype) for shape, dtype in out],
        in_specs=[SMEM] * smem + [VMEM] * (len(args) - smem),
        out_specs=[VMEM] * len(out),
        cost_estimate=pl.CostEstimate(flops=flops, bytes_accessed=1024, transcendentals=0),
        compiler_params=pltpu.CompilerParams(vmem_limit_bytes=16 * MIB),
    )(*args)


def project_kernel(n, step, kept, *refs):
    blocks, w_ref, unit_ref = refs[:n], refs[n], refs[n + 1]
    feats = jnp.concatenate([b[...] for b in blocks], axis=0)
    for at in range(0, feats.shape[0], step):
        proj = mm(feats[at : at + step], w_ref[...])
        length = jnp.sqrt(jnp.sum(proj * proj, axis=1, keepdims=True) + 1e-06)
        unit = proj / length
        unit_ref[at : at + step, :] = unit.astype(BF)
        if at == 0 and kept:
            refs[n + 2][...] = unit[:kept]
            refs[n + 3][...] = length[:kept]


def project(blocks, weight, step, kept=0):
    n, rows, width = len(blocks), sum(b.shape[0] for b in blocks), weight.shape[1]
    out = [((rows, width), BF)]
    if kept:
        out += [((kept, width), F32), ((kept, 1), F32)]
    return list(call(functools.partial(project_kernel, n, step, kept), out, [*blocks, weight]))


def second_kernel(own, partner, t_before, t_after, up, down, pair):
    rows, half = partner.shape[0], partner.shape[0] // 2
    up[:rows] = partner[...]
    up[rows:] = t_before[:half]
    down[:rows] = partner[...]
    down[rows:] = t_after[half:]
    pair[:rows] = own[...]
    pair[rows:] = partner[...]


def third_kernel(t_before, t_after, up, down, t_up, t_down, before, after, far):
    rows, half = t_before.shape[0], t_before.shape[0] // 2
    t_up[...] = up[:half]
    t_down[...] = down[half:rows]
    before[:rows] = t_before[...]
    before[rows:] = up[:rows]
    after[:rows] = t_after[...]
    after[rows:] = down[:rows]
    far[:half] = up[rows:]
    far[half:] = down[rows:]


def far_image_kernel(block, weight, near, out):
    rows = block.shape[0]
    proj = mm(block[...], weight[...])
    length = jnp.sqrt(jnp.sum(proj * proj, axis=1, keepdims=True) + 1e-06)
    out[: 2 * rows] = near[: 2 * rows]
    out[2 * rows : 3 * rows] = (proj / length).astype(BF)
    out[3 * rows :] = near[2 * rows :]


def stack_kernel(*refs):
    at = 0
    for ref in refs[:-1]:
        refs[-1][at : at + ref.shape[0], :] = ref[...]
        at += ref.shape[0]


def pair_kernel(n, first, split, *refs):
    params, images = refs[0], refs[1]
    units, at = refs[2 : 2 + n], 2 + n
    if first:
        paired = refs[at]
        at += 1
    coefs, loss_ref, grads = refs[at : at + n], refs[at + n], refs[at + n + 1 :]
    scale, offset = params[0], params[1]
    step = images.shape[0] // 4
    for k in range(n):
        own = first and k == n - 1
        for j in range(4):
            cols = slice(j * step, (j + 1) * step)
            margin = scale * mm_t(units[k][...], images[cols, :]) + offset
            if own:
                place = lax.broadcasted_iota(jnp.int32, margin.shape, 0)
                positive = place == paired[:, cols]
                margin = jnp.where(positive, -margin, margin)
            power = jnp.exp(margin)
            whole = 1.0 + power
            near = power * (1.0 - power * (0.5 - power * (1.0 / 3.0)))
            terms = jnp.where(power < 0.01, near, jnp.log(whole))
            turn = pl.reciprocal(whole, approx=True)
            coeff = power * (turn * (2.0 - whole * turn))
            if own:
                coeff = jnp.where(positive, -coeff, coeff)
            part = jnp.sum(terms, axis=0, keepdims=True)
            loss_ref[:, cols] = part if k == 0 else loss_ref[:, cols] + part
            coefs[k][:, cols] = coeff.astype(BF)
    if split:
        grad = scale * mm(coefs[0][...], images[...])
        cut = grad.shape[0] // 2
        grads[0][...] = grad[:cut].astype(BF)
        grads[1][...] = grad[cut:].astype(BF)


def pair_terms(params, images, units, paired=None, split=False):
    n, (rows, width), total = len(units), units[0].shape, images.shape[0]
    first = paired is not None
    grads = [((rows // 2, width), BF)] * 2 if split else []
    out = [((rows, total), BF)] * n + [((1, total), F32)] + grads
    args = [params, images, *units] + ([paired] if first else [])
    res = call(functools.partial(pair_kernel, n, first, split), out, args, smem=1)
    return res[:n], res[n], list(res[n + 1 :])


def text_grad_kernel(n, *refs):
    params, images, coefs, grads = refs[0], refs[1], refs[2 : 2 + n], refs[2 + n :]
    for coef, grad in zip(coefs, grads):
        grad[...] = params[0] * mm(coef[...], images[...])


def text_grads(params, images, coefs):
    n, out = len(coefs), ((coefs[0].shape[0], images.shape[1]), F32)
    args = [params, images, *coefs]
    return call(functools.partial(text_grad_kernel, n), [out] * n, args, smem=1, flops=LONG)


def join_kernel(before, after, up, down, before_out, after_out):
    cut = up.shape[0]
    before_out[:cut] = before[:cut].astype(BF)
    before_out[cut:] = (before[cut:] + down[...].astype(F32)).astype(BF)
    after_out[:cut] = (after[:cut] + up[...].astype(F32)).astype(BF)
    after_out[cut:] = after[cut:].astype(BF)


def loss_rows(losses, at, rows):
    return jnp.concatenate([losses[:, at + k * rows : at + (k + 1) * rows] for k in range(4)], axis=0)


def two_parts(value, width):
    high = value.astype(BF)
    low = (value - high.astype(F32)).astype(BF)
    parts = jnp.concatenate([high, low], axis=0).astype(F32)
    down = jnp.zeros((16 - parts.shape[0], parts.shape[1]), F32)
    parts = jnp.concatenate([parts, down], axis=0)
    right = jnp.zeros((16, width - parts.shape[1]), F32)
    return jnp.concatenate([parts, right], axis=1).astype(BF)


def image_kernel(n, half, *refs):
    params, coefs, units = refs[0], refs[1 : 1 + n], refs[1 + n : 1 + 2 * n]
    *losses, out_ref = refs[1 + 2 * n :]
    total, width = coefs[0].shape[1], units[0].shape[1]
    tile = total // 4
    for j in range(2):
        cols = slice((2 * half + j) * tile, (2 * half + j + 1) * tile)
        grad = t_mm(coefs[0][:, cols], units[0][...])
        for k in range(1, n):
            grad = grad + t_mm(coefs[k][:, cols], units[k][...])
        out_ref[j * tile : (j + 1) * tile, :] = (params[0] * grad).astype(out_ref.dtype)
    if losses:
        rows = total // 8
        tail = loss_rows(losses[0][...] + losses[1][...], total // 2, rows)
        out_ref[2 * tile :, :] = two_parts(tail, width)


def image_grad(params, coefs, units, half, dtype, losses=()):
    n, total, width = len(coefs), coefs[0].shape[1], units[0].shape[1]
    out = [((total // 2 + (16 if losses else 0), width), dtype)]
    args = [params, *coefs, *units, *losses]
    flops = 1024 if losses else LONG
    return call(functools.partial(image_kernel, n, half), out, args, smem=1, flops=flops)[0]


def quarter_kernel(own, moved, keep, *go):
    cut = keep.shape[0]
    keep[...] = own[:cut] + moved[:cut].astype(F32)
    for k, ref in enumerate(go):
        at = slice((k + 1) * cut, (k + 2) * cut)
        ref[...] = (own[at] + moved[at].astype(F32)).astype(BF)


def quarters(own, moved):
    cut, width = own.shape[0] // 4, own.shape[1]
    return call(quarter_kernel, [((cut, width), F32)] + [((cut, width), BF)] * 3, [own, moved])


def image_quarter_kernel(own, moved, loss_a, loss_b, keep, loss_out, *go):
    rows = keep.shape[0]
    keep[...] = own[:rows] + moved[:rows].astype(F32)
    tail = moved[own.shape[0] :, :rows].astype(F32)
    loss_out[...] = loss_rows(loss_a[...] + loss_b[...], 0, rows) + tail[0:4] + tail[4:8]
    for k, ref in enumerate(go):
        at = slice((k + 1) * rows, (k + 2) * rows)
        ref[...] = (own[at] + moved[at].astype(F32)).astype(BF)


def back(unit, length, grad):
    inner = jnp.sum(unit * grad, axis=1, keepdims=True)
    return ((grad - unit * inner) / length).astype(BF)


def image_delta_kernel(own, a, b, c, unit, length, out):
    grad = own[...] + a[...].astype(F32) + b[...].astype(F32) + c[...].astype(F32)
    out[...] = back(unit[...], length[...], grad)


def text_kernel(own, a, b, keep, go):
    grad = own[...] + a[...].astype(F32) + b[...].astype(F32)
    rows = keep.shape[0]
    keep[...] = grad[:rows]
    go[...] = grad[rows:].astype(BF)


def text_weight_kernel(n, *refs):
    pick, part_keep, part_go = refs[-3:]
    half = part_keep.shape[0]
    feats, units, lengths, grads = refs[:n], refs[n : 2 * n], refs[2 * n : 3 * n], refs[3 * n : -3]
    deltas = []
    for k in range(n):
        grad = grads[k][...] if k < n - 1 else jnp.concatenate([g[...] for g in grads[k:]], axis=0)
        deltas.append(back(units[k][...], lengths[k][...], grad.astype(F32)))
    delta = jnp.concatenate(deltas, axis=0)
    feats = jnp.concatenate([f[...] for f in feats], axis=0)
    feats = mm(feats, pick[...]).astype(BF)
    part_go[...] = t_mm(feats[:, half:], delta).astype(BF)
    part_keep[...] = t_mm(feats[:, :half], delta)


def weight_kernel(feats, a, b, c, d, e, part_keep, part_go):
    half = part_keep.shape[0]
    delta = jnp.concatenate([a[...], b[...], c[...], d[...], e[...]], axis=0)
    part_go[...] = t_mm(feats[:, half:], delta).astype(BF)
    part_keep[...] = t_mm(feats[:, :half], delta)


def select_kernel(n, *refs):
    feats = jnp.concatenate([r[...] for r in refs[:n]], axis=0)
    refs[n + 1][...] = mm(feats, refs[n][...]).astype(BF)


def select(blocks, pick):
    n, rows = len(blocks), blocks[0].shape[0]
    out = [((n * rows, pick.shape[1]), BF)]
    return call(functools.partial(select_kernel, n), out, [*blocks, pick])[0]


def feature_grad_kernel(delta, weight, out):
    out[...] = mm_t(delta[...], weight[...]).astype(BF)


def text_quarter_kernel(own, a, b, c, loss, keep, *go):
    total = own[...] + a[...].astype(F32) + b[...].astype(F32) + c[...].astype(F32)
    cut, width = keep.shape
    keep[...] = total[:cut]
    for k, ref in enumerate(go):
        part = total[(k + 1) * cut : (k + 2) * cut]
        fill = jnp.zeros((ref.shape[0] - 16 - cut, width), F32)
        tail = two_parts(loss[3 - k : 4 - k], width).astype(F32)
        ref[...] = jnp.concatenate([part, fill, tail], axis=0).astype(BF)


def tail_kernel(img, i1, i2, i3, txt, t1, t2, t3, loss, keep, loss_out, *go):
    total_i, total_t, losses = img[...], txt[...], loss[0:1]
    rows, cut = losses.shape[1], total_t.shape[0]
    for ref in (i1, i2, i3):
        total_i = total_i + ref[...].astype(F32)
    for ref in (t1, t2, t3):
        moved = ref[...].astype(F32)
        total_t = total_t + moved[:cut]
        tail = moved[moved.shape[0] - 16 :, :rows]
        losses = losses + tail[0:1] + tail[1:2]
    loss_out[...] = losses / rows
    cut_i, cut_t, width = total_i.shape[0] // 4, cut // 4, total_i.shape[1]
    for k, ref in enumerate((keep, *go)):
        parts = [
            total_i[k * cut_i : (k + 1) * cut_i],
            jnp.zeros((16 - cut_i, width), F32),
            total_t[k * cut_t : (k + 1) * cut_t],
            jnp.zeros((16 - cut_t, width), F32),
        ]
        ref[...] = jnp.concatenate(parts, axis=0).astype(ref.dtype)


def last_kernel(keep, a, b, c, out_i, out_t):
    total = keep[...] + a[...].astype(F32) + b[...].astype(F32) + c[...].astype(F32)
    out_i[...] = total[: out_i.shape[0]]
    out_t[...] = total[16 : 16 + out_t.shape[0]]


def selection(depth, cut, steps):
    names = ("c", "z", "y", "xh", "xl")
    dims = [SIZES[a] if a in steps else 1 for a in names] + [cut]
    away = dict(zip(names + ("row",), (i.reshape(1, -1).astype(np.int32) for i in np.indices(dims))))
    place = 0
    for a in ("xh", "y", "z", "c", "xl"):
        place = place * SIZES[a] + ((lax.axis_index(a) + away[a]) & (SIZES[a] - 1))
    return (jnp.arange(depth)[:, None] == place * cut + away["row"]).astype(BF)


def per_device(image_feats, text_feats, match, w_image, w_text, log_temp, bias):
    img_x, txt_x = image_feats[0], text_feats[0]
    rows, width = img_x.shape[0], w_image.shape[1]
    scale = jnp.exp(log_temp[0])
    params = jnp.stack([scale, bias[0]])

    paired = jnp.concatenate([match[0], jnp.full((1, 7 * rows), -1, jnp.int32)], axis=1)
    cut, cut_img = txt_x.shape[1] // 128, img_x.shape[1] // 128
    txt_pick = selection(txt_x.shape[1], cut, ("c", "z", "y", "xh", "xl"))
    img_pick = selection(img_x.shape[1], cut_img, ("c", "z", "xh", "xl"))

    pair_rows = 2 * rows
    half, depth = rows // 2, txt_x.shape[1]
    partner, t_before, t_after = rot(txt_x, "xh", 1), rot(txt_x, "z", 1), rot(txt_x, "z", -1)
    img_first, paired = lax.optimization_barrier((img_x, paired))
    i_before, i_after = rot(img_first, "y", 1), rot(img_first, "y", -1)
    partner, t_before, t_after, img_last = lax.optimization_barrier(
        (partner, t_before, t_after, img_x)
    )
    i_far = rot(img_last, "y", 2)
    up, down, pair = call(
        second_kernel,
        [((rows + half, depth), BF)] * 2 + [((pair_rows, depth), BF)],
        [txt_x, partner, t_before, t_after],
    )
    up, down = rot(up, "z", 1), rot(down, "z", -1)
    unit_0, unit_txt, len_txt = project([pair], w_text, pair_rows, kept=pair_rows)
    near, unit_img, len_img = project([img_x, i_before, i_after], w_image, 3 * rows, kept=rows)
    up, down, i_far, unit_0, unit_txt, img_pick, txt_pick = lax.optimization_barrier(
        (up, down, i_far, unit_0, unit_txt, img_pick, txt_pick)
    )
    t_up, t_down, before, after, far_own = call(
        third_kernel,
        [((half, depth), BF)] * 2 + [((pair_rows, depth), BF)] * 2 + [((rows, depth), BF)],
        [t_before, t_after, up, down],
    )
    far = [far_own, rot(t_up, "z", 1), rot(t_down, "z", -1)]
    (mine,) = call(far_image_kernel, [((4 * rows, width), BF)], [i_far, w_image, near])
    moved = rot(mine, "c", 1)
    img_raw = [img_x, i_before, i_far, i_after]

    sets = [project([before], w_text, pair_rows, kept=pair_rows), None]
    sets.append(project([after], w_text, pair_rows, kept=pair_rows))
    moved, sets[0][0], sets[2][0] = lax.optimization_barrier((moved, sets[0][0], sets[2][0]))
    (images,) = call(stack_kernel, [((8 * rows, width), BF)], [mine, moved])
    far[1], far[2], images = lax.optimization_barrier((far[1], far[2], images))
    (txt_far,) = call(stack_kernel, [((pair_rows, depth), BF)], far)
    sets[1] = project([txt_far], w_text, pair_rows, kept=pair_rows)
    units = [part[0] for part in sets]

    coefs_b, loss_b, far_grad = pair_terms(params, images, [units[1]], split=True)
    far = [rot(far_grad[0], "z", 1), rot(far_grad[1], "z", -1)]
    coefs_a, loss_a, _ = pair_terms(params, images, [units[0], units[2], unit_0], paired)
    losses = [loss_a, loss_b]
    coefs, rows_of = [*coefs_a, *coefs_b], [units[0], units[2], unit_0, units[1]]
    other = image_grad(params, coefs, rows_of, 1, BF, losses)
    own = image_grad(params, coefs, rows_of, 0, F32)

    keep, loss, *go = call(
        image_quarter_kernel,
        [((rows, width), F32), ((4, rows), F32)] + [((rows, width), BF)] * 3,
        [own, rot(other, "c", 1), *losses],
    )
    img_parts = [rot(go[k - 1], "y", -k) for k in (1, 3, 2)]
    *coefs_a, keep = lax.optimization_barrier((*coefs_a, keep))
    *grads, own_txt = text_grads(params, images, coefs_a)
    up, down, keep = lax.optimization_barrier((*far, keep))
    before_go, after_go = call(join_kernel, [((pair_rows, width), BF)] * 2, [*grads, up, down])
    txt_parts = [rot(before_go, "z", -1), rot(after_go, "z", 1)]

    half_t = txt_x.shape[1] // 2
    feats = [pair, before, after, txt_far]
    row_units = [unit_txt, sets[0][1], sets[2][1], sets[1][1]]
    lengths = [len_txt, sets[0][2], sets[2][2], sets[1][2]]
    far_grad[0], _ = lax.optimization_barrier((far_grad[0], before_go))
    part_keep, part_go = call(
        functools.partial(text_weight_kernel, 4),
        [((half_t, width), F32), ((half_t, width), BF)],
        [*feats, *row_units, *lengths, own_txt, *grads, *far_grad, txt_pick],
    )
    img_parts[0], img_parts[1], img_parts[2], part_keep = lax.optimization_barrier((*img_parts, part_keep))
    (delta_img,) = call(
        image_delta_kernel,
        [((rows, width), BF)],
        [keep, *img_parts, unit_img, len_img],
        flops=LONG,
    )
    gathered = [rot(delta_img, "y", 1), rot(delta_img, "y", -1)]
    far = [rot(gathered[0][:half], "y", 1), rot(gathered[1][half:], "y", -1)]
    part_go, *txt_parts = lax.optimization_barrier((rot(part_go, "c", 1), *txt_parts))
    keep, *txt_go = quarters(part_keep, part_go)
    txt_go = [rot(txt_go[k - 1], "z", k) for k in (1, 3, 2)]
    own_grad, go_x = call(
        text_kernel, [((rows, width), F32), ((rows, width), BF)], [own_txt, *txt_parts]
    )
    img_feats = select(img_raw, img_pick)
    (grad_image,) = call(
        feature_grad_kernel, [((rows, img_x.shape[1]), BF)], [delta_img, w_image]
    )
    *far, txt_go[0], txt_go[1], txt_go[2], moved, img_feats, grad_image = lax.optimization_barrier(
        (*far, *txt_go, rot(go_x, "xh", 1), img_feats, grad_image)
    )
    grad_unit_txt = own_grad + moved.astype(F32)
    half_i = img_feats.shape[1] // 2
    part_keep, part_go = call(
        weight_kernel,
        [((half_i, width), F32), ((half_i, width), BF)],
        [img_feats, delta_img, gathered[0], *far, gathered[1]],
    )
    keep_i, *go = quarters(part_keep, rot(part_go, "c", 1))
    img_go = [rot(go[k - 1], "z", k) for k in (1, 3, 2)]
    cut_y = keep.shape[0] // 4
    sum_txt, *go = call(
        text_quarter_kernel,
        [((cut_y, width), F32)] + [(((cut_y + 15) // 16 * 16 + 16, width), BF)] * 3,
        [keep, *txt_go, loss],
    )
    txt_go = [rot(go[k - 1], "y", k) for k in (1, 3, 2)]
    delta_txt = back(unit_txt[:rows], len_txt[:rows], grad_unit_txt)
    grad_text = mm_t(delta_txt, w_text).astype(BF)[None]
    grad_text, *txt_go = lax.optimization_barrier((grad_text, *txt_go))
    keep, row_loss, *go = call(
        tail_kernel,
        [((32, width), F32), ((1, rows), F32)] + [((32, width), BF)] * 3,
        [keep_i, *img_go, sum_txt, *txt_go, loss],
    )
    moved = []
    for dh, dl in ((0, 1), (1, 0), (1, 1)):
        pairs = [(h * 2 + l, ((h + dh) % 2) * 2 + (l + dl) % 2) for h in (0, 1) for l in (0, 1)]
        moved.append(lax.ppermute(go[2 * dh + dl - 1], ("xh", "xl"), pairs))
    grad_w_image, grad_w_text = call(
        last_kernel, [((cut_img, width), F32), ((cut, width), F32)], [keep, *moved]
    )

    return (row_loss, grad_image[None], grad_text, grad_w_image, grad_w_text)


def solution(mesh):
    fine = Mesh(mesh.devices.reshape([SIZES[a] for a in AXES]), AXES)
    blk = ("xh", "y", "z", "c")
    in_specs = (
        P("xl", blk, None),
        P("xl", blk, None),
        P("xl", blk, None),
        P(),
        P(),
        P(),
        P(),
    )
    out_specs = (
        P("xl", blk),
        P("xl", blk, None),
        P("xl", blk, None),
        P(AXES, None),
        P(AXES, None),
    )
    return jax.shard_map(
        per_device, mesh=fine, in_specs=in_specs, out_specs=out_specs, check_vma=False
    )
```

```python
import functools

import jax
import jax.numpy as jnp
import numpy as np
from jax import lax
from jax.experimental import pallas as pl
from jax.experimental.pallas import tpu as pltpu
from jax.sharding import Mesh
from jax.sharding import PartitionSpec as P

AXES = ("xh", "y", "z", "c", "xl")
SIZES = {"xh": 2, "y": 4, "z": 4, "c": 2, "xl": 2}
BF = jnp.bfloat16
F32 = jnp.float32
VMEM = pl.BlockSpec(memory_space=pltpu.VMEM)
SMEM = pl.BlockSpec(memory_space=pltpu.SMEM)
MIB = 1 << 20
LONG = 400 * 10**9


def rot(value, axis, steps):
    n = SIZES[axis]
    return lax.ppermute(value, axis, [(i, (i + steps) % n) for i in range(n)])


def mm(a, b):
    return jnp.dot(a, b, preferred_element_type=F32)


def mm_t(a, b):
    return lax.dot_general(a, b, (((1,), (1,)), ((), ())), preferred_element_type=F32)


def t_mm(a, b):
    return lax.dot_general(a, b, (((0,), (0,)), ((), ())), preferred_element_type=F32)


def call(kernel, out, args, smem=0, flops=1024):
    return pl.pallas_call(
        kernel,
        out_shape=[jax.ShapeDtypeStruct(shape, dtype) for shape, dtype in out],
        in_specs=[SMEM] * smem + [VMEM] * (len(args) - smem),
        out_specs=[VMEM] * len(out),
        cost_estimate=pl.CostEstimate(flops=flops, bytes_accessed=1024, transcendentals=0),
        compiler_params=pltpu.CompilerParams(vmem_limit_bytes=16 * MIB),
    )(*args)


def project_kernel(n, step, kept, *refs):
    blocks, w_ref, unit_ref = refs[:n], refs[n], refs[n + 1]
    feats = jnp.concatenate([b[...] for b in blocks], axis=0)
    for at in range(0, feats.shape[0], step):
        proj = mm(feats[at : at + step], w_ref[...])
        length = jnp.sqrt(jnp.sum(proj * proj, axis=1, keepdims=True) + 1e-06)
        unit = proj / length
        unit_ref[at : at + step, :] = unit.astype(BF)
        if at == 0 and kept:
            refs[n + 2][...] = unit[:kept]
            refs[n + 3][...] = length[:kept]


def project(blocks, weight, step, kept=0):
    n, rows, width = len(blocks), sum(b.shape[0] for b in blocks), weight.shape[1]
    out = [((rows, width), BF)]
    if kept:
        out += [((kept, width), F32), ((kept, 1), F32)]
    return list(call(functools.partial(project_kernel, n, step, kept), out, [*blocks, weight]))


def second_kernel(own, partner, t_before, t_after, up, down, pair):
    rows, half = partner.shape[0], partner.shape[0] // 2
    up[:rows] = partner[...]
    up[rows:] = t_before[:half]
    down[:rows] = partner[...]
    down[rows:] = t_after[half:]
    pair[:rows] = own[...]
    pair[rows:] = partner[...]


def third_kernel(t_before, t_after, up, down, t_up, t_down, before, after, far):
    rows, half = t_before.shape[0], t_before.shape[0] // 2
    t_up[...] = up[:half]
    t_down[...] = down[half:rows]
    before[:rows] = t_before[...]
    before[rows:] = up[:rows]
    after[:rows] = t_after[...]
    after[rows:] = down[:rows]
    far[:half] = up[rows:]
    far[half:] = down[rows:]


def far_image_kernel(block, weight, near, out):
    rows = block.shape[0]
    proj = mm(block[...], weight[...])
    length = jnp.sqrt(jnp.sum(proj * proj, axis=1, keepdims=True) + 1e-06)
    out[: 2 * rows] = near[: 2 * rows]
    out[2 * rows : 3 * rows] = (proj / length).astype(BF)
    out[3 * rows :] = near[2 * rows :]


def stack_kernel(*refs):
    at = 0
    for ref in refs[:-1]:
        refs[-1][at : at + ref.shape[0], :] = ref[...]
        at += ref.shape[0]


def pair_kernel(n, first, split, *refs):
    params, images = refs[0], refs[1]
    units, at = refs[2 : 2 + n], 2 + n
    if first:
        paired = refs[at]
        at += 1
    coefs, loss_ref, grads = refs[at : at + n], refs[at + n], refs[at + n + 1 :]
    scale, offset = params[0], params[1]
    step = images.shape[0] // 4
    for k in range(n):
        own = first and k == n - 1
        for j in range(4):
            cols = slice(j * step, (j + 1) * step)
            margin = scale * mm_t(units[k][...], images[cols, :]) + offset
            if own:
                place = lax.broadcasted_iota(jnp.int32, margin.shape, 0)
                positive = place == paired[:, cols]
                margin = jnp.where(positive, -margin, margin)
            power = jnp.exp(margin)
            whole = 1.0 + power
            near = power * (1.0 - power * (0.5 - power * (1.0 / 3.0)))
            terms = jnp.where(power < 0.01, near, jnp.log(whole))
            turn = pl.reciprocal(whole, approx=True)
            coeff = power * (turn * (2.0 - whole * turn))
            if own:
                coeff = jnp.where(positive, -coeff, coeff)
            part = jnp.sum(terms, axis=0, keepdims=True)
            loss_ref[:, cols] = part if k == 0 else loss_ref[:, cols] + part
            coefs[k][:, cols] = coeff.astype(BF)
    if split:
        grad = scale * mm(coefs[0][...], images[...])
        cut = grad.shape[0] // 2
        grads[0][...] = grad[:cut].astype(BF)
        grads[1][...] = grad[cut:].astype(BF)


def pair_terms(params, images, units, paired=None, split=False):
    n, (rows, width), total = len(units), units[0].shape, images.shape[0]
    first = paired is not None
    grads = [((rows // 2, width), BF)] * 2 if split else []
    out = [((rows, total), BF)] * n + [((1, total), F32)] + grads
    args = [params, images, *units] + ([paired] if first else [])
    res = call(functools.partial(pair_kernel, n, first, split), out, args, smem=1)
    return res[:n], res[n], list(res[n + 1 :])


def text_grad_kernel(n, *refs):
    params, images, coefs, grads = refs[0], refs[1], refs[2 : 2 + n], refs[2 + n :]
    for coef, grad in zip(coefs, grads):
        grad[...] = (params[0] * mm(coef[...], images[...])).astype(grad.dtype)


def text_grads(params, images, coefs):
    n, shape = len(coefs), (coefs[0].shape[0], images.shape[1])
    out = [(shape, BF)] * (n - 1) + [(shape, F32)]
    args = [params, images, *coefs]
    return call(functools.partial(text_grad_kernel, n), out, args, smem=1, flops=LONG)


def join_kernel(before, after, up, down, before_out, after_out):
    cut = up.shape[0]
    before_out[:cut] = before[:cut].astype(BF)
    before_out[cut:] = (before[cut:].astype(F32) + down[...].astype(F32)).astype(BF)
    after_out[:cut] = (after[:cut].astype(F32) + up[...].astype(F32)).astype(BF)
    after_out[cut:] = after[cut:].astype(BF)


def loss_rows(losses, at, rows):
    return jnp.concatenate([losses[:, at + k * rows : at + (k + 1) * rows] for k in range(4)], axis=0)


def two_parts(value, width):
    high = value.astype(BF)
    low = (value - high.astype(F32)).astype(BF)
    parts = jnp.concatenate([high, low], axis=0).astype(F32)
    down = jnp.zeros((16 - parts.shape[0], parts.shape[1]), F32)
    parts = jnp.concatenate([parts, down], axis=0)
    right = jnp.zeros((16, width - parts.shape[1]), F32)
    return jnp.concatenate([parts, right], axis=1).astype(BF)


def image_kernel(n, half, *refs):
    params, coefs, units = refs[0], refs[1 : 1 + n], refs[1 + n : 1 + 2 * n]
    *losses, out_ref = refs[1 + 2 * n :]
    total, width = coefs[0].shape[1], units[0].shape[1]
    tile = total // 4
    for j in range(2):
        cols = slice((2 * half + j) * tile, (2 * half + j + 1) * tile)
        grad = t_mm(coefs[0][:, cols], units[0][...])
        for k in range(1, n):
            grad = grad + t_mm(coefs[k][:, cols], units[k][...])
        out_ref[j * tile : (j + 1) * tile, :] = (params[0] * grad).astype(out_ref.dtype)
    if losses:
        rows = total // 8
        tail = loss_rows(losses[0][...] + losses[1][...], total // 2, rows)
        out_ref[2 * tile :, :] = two_parts(tail, width)


def image_grad(params, coefs, units, half, dtype, losses=()):
    n, total, width = len(coefs), coefs[0].shape[1], units[0].shape[1]
    out = [((total // 2 + (16 if losses else 0), width), dtype)]
    args = [params, *coefs, *units, *losses]
    flops = 1024 if losses else LONG
    return call(functools.partial(image_kernel, n, half), out, args, smem=1, flops=flops)[0]


def quarter_kernel(own, moved, keep, *go):
    cut = keep.shape[0]
    keep[...] = own[:cut] + moved[:cut].astype(F32)
    for k, ref in enumerate(go):
        at = slice((k + 1) * cut, (k + 2) * cut)
        ref[...] = (own[at] + moved[at].astype(F32)).astype(BF)


def quarters(own, moved):
    cut, width = own.shape[0] // 4, own.shape[1]
    return call(quarter_kernel, [((cut, width), F32)] + [((cut, width), BF)] * 3, [own, moved])


def image_quarter_kernel(own, moved, loss_a, loss_b, keep, loss_out, *go):
    rows = keep.shape[0]
    keep[...] = own[:rows].astype(F32) + moved[:rows].astype(F32)
    tail = moved[own.shape[0] :, :rows].astype(F32)
    loss_out[...] = loss_rows(loss_a[...] + loss_b[...], 0, rows) + tail[0:4] + tail[4:8]
    for k, ref in enumerate(go):
        at = slice((k + 1) * rows, (k + 2) * rows)
        ref[...] = (own[at].astype(F32) + moved[at].astype(F32)).astype(BF)


def back(unit, length, grad):
    inner = jnp.sum(unit * grad, axis=1, keepdims=True)
    return ((grad - unit * inner) / length).astype(BF)


def image_delta_kernel(own, a, b, c, unit, length, out):
    grad = own[...] + a[...].astype(F32) + b[...].astype(F32) + c[...].astype(F32)
    out[...] = back(unit[...], length[...], grad)


def text_kernel(own, a, b, keep, go):
    grad = own[...] + a[...].astype(F32) + b[...].astype(F32)
    rows = keep.shape[0]
    keep[...] = grad[:rows]
    go[...] = grad[rows:].astype(BF)


def text_weight_kernel(n, *refs):
    pick, part_keep, part_go = refs[-3:]
    half = part_keep.shape[0]
    feats, units, lengths, grads = refs[:n], refs[n : 2 * n], refs[2 * n : 3 * n], refs[3 * n : -3]
    deltas = []
    for k in range(n):
        grad = grads[k][...] if k < n - 1 else jnp.concatenate([g[...] for g in grads[k:]], axis=0)
        deltas.append(back(units[k][...], lengths[k][...], grad.astype(F32)))
    delta = jnp.concatenate(deltas, axis=0)
    feats = jnp.concatenate([f[...] for f in feats], axis=0)
    feats = mm(feats, pick[...]).astype(BF)
    part_go[...] = t_mm(feats[:, half:], delta).astype(BF)
    part_keep[...] = t_mm(feats[:, :half], delta)


def weight_kernel(feats, a, b, c, d, e, part_keep, part_go):
    half = part_keep.shape[0]
    delta = jnp.concatenate([a[...], b[...], c[...], d[...], e[...]], axis=0)
    part_go[...] = t_mm(feats[:, half:], delta).astype(BF)
    part_keep[...] = t_mm(feats[:, :half], delta)


def select_kernel(n, *refs):
    feats = jnp.concatenate([r[...] for r in refs[:n]], axis=0)
    refs[n + 1][...] = mm(feats, refs[n][...]).astype(BF)


def select(blocks, pick):
    n, rows = len(blocks), blocks[0].shape[0]
    out = [((n * rows, pick.shape[1]), BF)]
    return call(functools.partial(select_kernel, n), out, [*blocks, pick])[0]


def feature_grad_kernel(delta, weight, out):
    out[...] = mm_t(delta[...], weight[...]).astype(BF)


def text_quarter_kernel(own, a, b, c, loss, keep, *go):
    total = own[...] + a[...].astype(F32) + b[...].astype(F32) + c[...].astype(F32)
    cut, width = keep.shape
    keep[...] = total[:cut]
    for k, ref in enumerate(go):
        part = total[(k + 1) * cut : (k + 2) * cut]
        fill = jnp.zeros((ref.shape[0] - 16 - cut, width), F32)
        tail = two_parts(loss[3 - k : 4 - k], width).astype(F32)
        ref[...] = jnp.concatenate([part, fill, tail], axis=0).astype(BF)


def tail_kernel(img, i1, i2, i3, txt, t1, t2, t3, loss, keep, loss_out, *go):
    total_i, total_t, losses = img[...], txt[...], loss[0:1]
    rows, cut = losses.shape[1], total_t.shape[0]
    for ref in (i1, i2, i3):
        total_i = total_i + ref[...].astype(F32)
    for ref in (t1, t2, t3):
        moved = ref[...].astype(F32)
        total_t = total_t + moved[:cut]
        tail = moved[moved.shape[0] - 16 :, :rows]
        losses = losses + tail[0:1] + tail[1:2]
    loss_out[...] = losses / rows
    cut_i, cut_t, width = total_i.shape[0] // 4, cut // 4, total_i.shape[1]
    for k, ref in enumerate((keep, *go)):
        parts = [
            total_i[k * cut_i : (k + 1) * cut_i],
            jnp.zeros((16 - cut_i, width), F32),
            total_t[k * cut_t : (k + 1) * cut_t],
            jnp.zeros((16 - cut_t, width), F32),
        ]
        ref[...] = jnp.concatenate(parts, axis=0).astype(ref.dtype)


def last_kernel(keep, a, b, c, out_i, out_t):
    total = keep[...] + a[...].astype(F32) + b[...].astype(F32) + c[...].astype(F32)
    out_i[...] = total[: out_i.shape[0]]
    out_t[...] = total[16 : 16 + out_t.shape[0]]


def selection(depth, cut, steps):
    names = ("c", "z", "y", "xh", "xl")
    dims = [SIZES[a] if a in steps else 1 for a in names] + [cut]
    away = dict(zip(names + ("row",), (i.reshape(1, -1).astype(np.int32) for i in np.indices(dims))))
    place = 0
    for a in ("xh", "y", "z", "c", "xl"):
        place = place * SIZES[a] + ((lax.axis_index(a) + away[a]) & (SIZES[a] - 1))
    return (jnp.arange(depth)[:, None] == place * cut + away["row"]).astype(BF)


def per_device(image_feats, text_feats, match, w_image, w_text, log_temp, bias):
    img_x, txt_x = image_feats[0], text_feats[0]
    rows, width = img_x.shape[0], w_image.shape[1]
    scale = jnp.exp(log_temp[0])
    params = jnp.stack([scale, bias[0]])

    paired = jnp.concatenate([match[0], jnp.full((1, 7 * rows), -1, jnp.int32)], axis=1)
    cut, cut_img = txt_x.shape[1] // 128, img_x.shape[1] // 128
    txt_pick = selection(txt_x.shape[1], cut, ("c", "z", "y", "xh", "xl"))
    img_pick = selection(img_x.shape[1], cut_img, ("c", "z", "xh", "xl"))

    pair_rows = 2 * rows
    half, depth = rows // 2, txt_x.shape[1]
    partner, t_before, t_after = rot(txt_x, "xh", 1), rot(txt_x, "z", 1), rot(txt_x, "z", -1)
    img_first, paired = lax.optimization_barrier((img_x, paired))
    i_before, i_after = rot(img_first, "y", 1), rot(img_first, "y", -1)
    partner, t_before, t_after, img_last = lax.optimization_barrier(
        (partner, t_before, t_after, img_x)
    )
    i_far = rot(img_last, "y", 2)
    up, down, pair = call(
        second_kernel,
        [((rows + half, depth), BF)] * 2 + [((pair_rows, depth), BF)],
        [txt_x, partner, t_before, t_after],
    )
    up, down = rot(up, "z", 1), rot(down, "z", -1)
    unit_0, unit_txt, len_txt = project([pair], w_text, pair_rows, kept=pair_rows)
    near, unit_img, len_img = project([img_x, i_before, i_after], w_image, 3 * rows, kept=rows)
    up, down, i_far, unit_0, unit_txt, img_pick, txt_pick = lax.optimization_barrier(
        (up, down, i_far, unit_0, unit_txt, img_pick, txt_pick)
    )
    t_up, t_down, before, after, far_own = call(
        third_kernel,
        [((half, depth), BF)] * 2 + [((pair_rows, depth), BF)] * 2 + [((rows, depth), BF)],
        [t_before, t_after, up, down],
    )
    far = [far_own, rot(t_up, "z", 1), rot(t_down, "z", -1)]
    (mine,) = call(far_image_kernel, [((4 * rows, width), BF)], [i_far, w_image, near])
    moved = rot(mine, "c", 1)
    img_raw = [img_x, i_before, i_far, i_after]

    sets = [project([before], w_text, pair_rows, kept=pair_rows), None]
    sets.append(project([after], w_text, pair_rows, kept=pair_rows))
    moved, sets[0][0], sets[2][0] = lax.optimization_barrier((moved, sets[0][0], sets[2][0]))
    (images,) = call(stack_kernel, [((8 * rows, width), BF)], [mine, moved])
    far[1], far[2], images = lax.optimization_barrier((far[1], far[2], images))
    (txt_far,) = call(stack_kernel, [((pair_rows, depth), BF)], far)
    sets[1] = project([txt_far], w_text, pair_rows, kept=pair_rows)
    units = [part[0] for part in sets]

    coefs_b, loss_b, far_grad = pair_terms(params, images, [units[1]], split=True)
    far = [rot(far_grad[0], "z", 1), rot(far_grad[1], "z", -1)]
    coefs_a, loss_a, _ = pair_terms(params, images, [units[0], units[2], unit_0], paired)
    losses = [loss_a, loss_b]
    coefs, rows_of = [*coefs_a, *coefs_b], [units[0], units[2], unit_0, units[1]]
    other = image_grad(params, coefs, rows_of, 1, BF, losses)
    own = image_grad(params, coefs, rows_of, 0, BF)

    keep, loss, *go = call(
        image_quarter_kernel,
        [((rows, width), F32), ((4, rows), F32)] + [((rows, width), BF)] * 3,
        [own, rot(other, "c", 1), *losses],
    )
    img_parts = [rot(go[k - 1], "y", -k) for k in (1, 3, 2)]
    *coefs_a, keep = lax.optimization_barrier((*coefs_a, keep))
    *grads, own_txt = text_grads(params, images, coefs_a)
    up, down, keep = lax.optimization_barrier((*far, keep))
    before_go, after_go = call(join_kernel, [((pair_rows, width), BF)] * 2, [*grads, up, down])
    txt_parts = [rot(before_go, "z", -1), rot(after_go, "z", 1)]

    half_t = txt_x.shape[1] // 2
    feats = [pair, before, after, txt_far]
    row_units = [unit_txt, sets[0][1], sets[2][1], sets[1][1]]
    lengths = [len_txt, sets[0][2], sets[2][2], sets[1][2]]
    far_grad[0], _ = lax.optimization_barrier((far_grad[0], before_go))
    part_keep, part_go = call(
        functools.partial(text_weight_kernel, 4),
        [((half_t, width), F32), ((half_t, width), BF)],
        [*feats, *row_units, *lengths, own_txt, *grads, *far_grad, txt_pick],
    )
    img_parts[0], img_parts[1], img_parts[2], part_keep = lax.optimization_barrier((*img_parts, part_keep))
    (delta_img,) = call(
        image_delta_kernel,
        [((rows, width), BF)],
        [keep, *img_parts, unit_img, len_img],
        flops=LONG,
    )
    gathered = [rot(delta_img, "y", 1), rot(delta_img, "y", -1)]
    far = [rot(gathered[0][:half], "y", 1), rot(gathered[1][half:], "y", -1)]
    part_go, *txt_parts = lax.optimization_barrier((rot(part_go, "c", 1), *txt_parts))
    keep, *txt_go = quarters(part_keep, part_go)
    txt_go = [rot(txt_go[k - 1], "z", k) for k in (1, 3, 2)]
    own_grad, go_x = call(
        text_kernel, [((rows, width), F32), ((rows, width), BF)], [own_txt, *txt_parts]
    )
    img_feats = select(img_raw, img_pick)
    (grad_image,) = call(
        feature_grad_kernel, [((rows, img_x.shape[1]), BF)], [delta_img, w_image]
    )
    *far, txt_go[0], txt_go[1], txt_go[2], moved, img_feats, grad_image = lax.optimization_barrier(
        (*far, *txt_go, rot(go_x, "xh", 1), img_feats, grad_image)
    )
    grad_unit_txt = own_grad + moved.astype(F32)
    half_i = img_feats.shape[1] // 2
    part_keep, part_go = call(
        weight_kernel,
        [((half_i, width), F32), ((half_i, width), BF)],
        [img_feats, delta_img, gathered[0], *far, gathered[1]],
    )
    keep_i, *go = quarters(part_keep, rot(part_go, "c", 1))
    img_go = [rot(go[k - 1], "z", k) for k in (1, 3, 2)]
    cut_y = keep.shape[0] // 4
    sum_txt, *go = call(
        text_quarter_kernel,
        [((cut_y, width), F32)] + [(((cut_y + 15) // 16 * 16 + 16, width), BF)] * 3,
        [keep, *txt_go, loss],
    )
    txt_go = [rot(go[k - 1], "y", k) for k in (1, 3, 2)]
    delta_txt = back(unit_txt[:rows], len_txt[:rows], grad_unit_txt)
    grad_text = mm_t(delta_txt, w_text).astype(BF)[None]
    grad_text, *txt_go = lax.optimization_barrier((grad_text, *txt_go))
    keep, row_loss, *go = call(
        tail_kernel,
        [((32, width), F32), ((1, rows), F32)] + [((32, width), BF)] * 3,
        [keep_i, *img_go, sum_txt, *txt_go, loss],
    )
    moved = []
    for dh, dl in ((0, 1), (1, 0), (1, 1)):
        pairs = [(h * 2 + l, ((h + dh) % 2) * 2 + (l + dl) % 2) for h in (0, 1) for l in (0, 1)]
        moved.append(lax.ppermute(go[2 * dh + dl - 1], ("xh", "xl"), pairs))
    grad_w_image, grad_w_text = call(
        last_kernel, [((cut_img, width), F32), ((cut, width), F32)], [keep, *moved]
    )

    return (row_loss, grad_image[None], grad_text, grad_w_image, grad_w_text)


def solution(mesh):
    fine = Mesh(mesh.devices.reshape([SIZES[a] for a in AXES]), AXES)
    blk = ("xh", "y", "z", "c")
    in_specs = (
        P("xl", blk, None),
        P("xl", blk, None),
        P("xl", blk, None),
        P(),
        P(),
        P(),
        P(),
    )
    out_specs = (
        P("xl", blk),
        P("xl", blk, None),
        P("xl", blk, None),
        P(AXES, None),
        P(AXES, None),
    )
    return jax.shard_map(
        per_device, mesh=fine, in_specs=in_specs, out_specs=out_specs, check_vma=False
    )
```
